512 devices in a mesh: row: 32 (over x, z_hi, core), col: 16 (over z_lo, y).
Axes of the slice: x: 4, y: 4, z: 16 (z_hi: 4, z_lo: 4; z = z_hi * 4 + z_lo), core: 2. Of those that a mesh axis runs over, the one named last changes fastest.
Arguments:
- tokens: bfloat16 [4096, 6144], P('row', 'col'), may hold values from -40 to 40
- ln_gain: bfloat16 [6144], P('col'), may hold values from 0.5 to 1.5
- w_qkv: bfloat16 [6144, 3, 4096], P('row', None, 'col'), may hold values from -1 to 1
- q_gain: float32 [4096], P('col'), may hold values from 0.8 to 6
- k_gain: float32 [4096], P('col'), may hold values from 0.8 to 6
Outputs:
- attended: bfloat16 [4096, 4096], P('row', 'col')
The draws below stay inside these ranges and needn't reach their ends.
All inputs are finite; a program needn't handle non-finite values.
Results may differ from the reference program's by a relative error of at most 0.03.
Values may be sent and summed in bfloat16 or wider, within the bound.
No kernel may reach another device: no remote copies, remote signals or barrier semaphores. Data moves between devices by JAX's collectives and lax.ppermute only.
A program may use at most 64 MiB of HBM per device.

```python
import jax
import jax.numpy as jnp
from jax import lax

D = 6144
DH = 128
HEADS = 32
SEQ = 4096


def head_levels(key, lowest, highest):
    key_level, key_entry = jax.random.split(key)
    head_level = jnp.exp(jax.random.uniform(key_level, (HEADS, 1), jnp.float32, jnp.log(lowest), jnp.log(highest)))
    entries = jax.random.uniform(key_entry, (HEADS, DH), jnp.float32, 0.8, 1.2)
    return (head_level * entries).reshape(HEADS * DH)


def draw_tokens(key, part):
    key = jax.random.fold_in(key, 11)
    key_base = jax.random.fold_in(key, 0)
    drawn = jax.random.normal(key_base, (SEQ, D), jnp.float32)
    return jnp.clip(drawn, -6.0, 6.0).astype(jnp.bfloat16)


def draw_w_qkv(key, part):
    key = jax.random.fold_in(key, 13)
    key_base = jax.random.fold_in(key, 0)
    drawn = jax.random.normal(key_base, (D, 3, HEADS * DH), jnp.float32)
    return (jnp.clip(drawn, -6.0, 6.0) * D ** (-0.5)).astype(jnp.bfloat16)


def draw_q_gain(key, part):
    key = jax.random.fold_in(key, 21)
    return head_levels(key, 1.0, 2.2)


def draw_k_gain(key, part):
    key = jax.random.fold_in(key, 22)
    return head_levels(key, 1.0, 2.2)


def setup_inputs(seed: int = 0) -> dict:
    streams_of = jax.random.split(jax.random.key(seed), 6)
    return {
        "tokens": draw_tokens(jax.random.fold_in(streams_of[5], 71), 0),
        "ln_gain": jnp.clip(1.0 + 0.1 * jax.random.normal(streams_of[1], (D,), jnp.float32), 0.5, 1.5).astype(jnp.bfloat16),
        "w_qkv": draw_w_qkv(jax.random.fold_in(streams_of[5], 71), 0),
        "q_gain": draw_q_gain(jax.random.fold_in(streams_of[5], 71), 0),
        "k_gain": draw_k_gain(jax.random.fold_in(streams_of[5], 71), 0),
    }


EPSILON = 1e-06

def head_norm(values, gain_row, head_count, head_width):
    row_count = values.shape[0]
    grouped = values.reshape(row_count, head_count, head_width)
    center = lax.optimization_barrier(jnp.mean(grouped, axis=2, keepdims=True))
    spread = lax.optimization_barrier(jnp.mean(grouped * grouped, axis=2, keepdims=True)) - center * center
    scaled = (grouped - center) * lax.rsqrt(spread + EPSILON) * gain_row.reshape(1, head_count, head_width)
    return scaled.reshape(row_count, head_count * head_width).astype(jnp.bfloat16)

def one_head(operands):
    query_head, key_head, value_head = operands
    scores = jnp.dot(query_head, key_head.T, preferred_element_type=jnp.float32) * DH ** (-0.5)
    running_max = lax.optimization_barrier(jnp.max(scores, axis=1, keepdims=True))
    weights = jnp.exp(scores - running_max)
    running_sum = lax.optimization_barrier(jnp.sum(weights, axis=1, keepdims=True))
    weighted = jnp.dot(weights.astype(jnp.bfloat16), value_head, preferred_element_type=jnp.float32)
    return weighted / running_sum

def reference(tokens, ln_gain, w_qkv, q_gain, k_gain):
    values = tokens.astype(jnp.float32)
    center = lax.optimization_barrier(jnp.mean(values, axis=1, keepdims=True))
    spread = lax.optimization_barrier(jnp.mean(values * values, axis=1, keepdims=True)) - center * center
    normed = ((values - center) * lax.rsqrt(spread + EPSILON) * ln_gain.astype(jnp.float32)).astype(jnp.bfloat16)
    head_total = HEADS * DH
    projected = jnp.dot(normed, w_qkv.reshape(D, 3 * head_total), preferred_element_type=jnp.float32)
    projected = projected.reshape(SEQ, 3, head_total)
    query_normed = head_norm(projected[:, 0], q_gain, HEADS, DH)
    key_normed = head_norm(projected[:, 1], k_gain, HEADS, DH)
    value_rows = projected[:, 2].astype(jnp.bfloat16)

    def by_heads(matrix):
        return jnp.transpose(matrix.reshape(SEQ, HEADS, DH), (1, 0, 2))
    outcome = lax.map(one_head, (by_heads(query_normed), by_heads(key_normed), by_heads(value_rows)))
    return jnp.transpose(outcome, (1, 0, 2)).reshape(SEQ, head_total).astype(jnp.bfloat16)
```

```python
import numpy as np
import jax
import jax.numpy as jnp
from jax import lax
from jax.experimental import pallas as pl
from jax.experimental.pallas import tpu as pltpu
from jax.sharding import Mesh, PartitionSpec as P

DH = 128
EPSILON = 1e-06
NX = NZH = NZL = NY = 4
CORES = 2
AXES = ("x", "zh", "core", "zl", "y")
SIZES = (NX, NZH, CORES, NZL, NY)
VMEM_LIMIT = 56 * 1024 * 1024


def shift(values, axes, move):
    sizes = [SIZES[AXES.index(axis)] for axis in axes]
    pairs = [
        (int(np.ravel_multi_index(src, sizes)), int(np.ravel_multi_index(move(src), sizes)))
        for src in np.ndindex(*sizes)
    ]
    return lax.ppermute(values, axes, pairs)


def relabel(values):
    return shift(values, ("zh", "core", "zl", "y"), lambda i: (i[3], i[1], i[2], i[0]))


def relabel_cross(values):
    return shift(values, ("zh", "core", "zl", "y"), lambda i: (i[3], 1 - i[1], i[2], i[0]))


def along_z(values, step):
    return shift(values, ("zh", "zl"), lambda i: divmod((i[0] * NZL + i[1] + step) % 16, NZL))


def swap_cores(values):
    return shift(values, ("core",), lambda i: (1 - i[0],))


def spread(values, axes, count):
    return lax.all_to_all(jnp.broadcast_to(values[None], (count,) + values.shape), axes, 0, 0)


def project_kernel(
    where, t0, t1, t2a, t2b, t3, p0, p1, p2a, p2b, p3, gain, head_gain, w, kv_out, q_out, normed
):
    zl = where[0]
    pieces = (
        ((t0, 0, 128), (p0, 128, 128)),
        ((t1, 0, 128), (p1, 128, 128)),
        ((t2a, 0, 64), (t2b, 64, 64), (p2a, 128, 64), (p2b, 192, 64)),
        ((t3, 0, 128), (p3, 128, 128)),
    )
    rows = 256
    features = 6144

    def block(slot, y):
        return jnp.concatenate([ref[y] for ref, _, _ in pieces[slot]], axis=0).astype(jnp.float32)

    total = jnp.zeros((rows, 1), jnp.float32)
    squares = jnp.zeros((rows, 1), jnp.float32)
    for slot in range(4):
        for y in range(NY):
            x = block(slot, y)
            total += jnp.sum(x, axis=1, keepdims=True)
            squares += jnp.sum(x * x, axis=1, keepdims=True)
    center = total / features
    scale = lax.rsqrt(squares / features - center * center + EPSILON)
    acc = jnp.zeros((rows, 3 * DH), jnp.float32)
    for slot in range(4):
        for y in range(NY):
            c = lax.rem(zl + slot, NZL) * NY + y
            x = block(slot, y)
            n = ((x - center) * scale * gain[c]).astype(jnp.bfloat16)
            acc += jnp.dot(n, w[c], preferred_element_type=jnp.float32)

    def head_norm(values, row):
        mid = jnp.mean(values, axis=1, keepdims=True)
        var = jnp.mean(values * values, axis=1, keepdims=True) - mid * mid
        return ((values - mid) * lax.rsqrt(var + EPSILON) * row).astype(jnp.bfloat16)

    q_out[...] = head_norm(acc[:, :DH], head_gain[0])
    kv_out[:, :DH] = head_norm(acc[:, DH : 2 * DH], head_gain[1])
    kv_out[:, DH:] = acc[:, 2 * DH :].astype(jnp.bfloat16)


def attend_kernel(q, kv, out):
    keys = kv[:, :, :DH].reshape(-1, DH)
    values = kv[:, :, DH:].reshape(-1, DH)
    scores = lax.dot_general(
        q[...], keys, (((1,), (1,)), ((), ())), preferred_element_type=jnp.float32
    ) * (DH ** -0.5)
    top = jnp.max(scores, axis=1, keepdims=True)
    weights = jnp.exp(scores - top)
    total = jnp.sum(weights, axis=1, keepdims=True)
    mixed = jnp.dot(weights.astype(jnp.bfloat16), values, preferred_element_type=jnp.float32)
    out[...] = (mixed / total).astype(jnp.bfloat16)


def body(tokens, ln_gain, w_qkv, q_gain, k_gain):
    core = lax.axis_index("core")
    zl = lax.axis_index("zl")
    zh = lax.axis_index("zh")

    with jax.named_scope("weights"):
        w_mine = lax.dynamic_slice_in_dim(w_qkv, core * DH, DH, axis=2).reshape(192, 3 * DH)
        w_other = lax.dynamic_slice_in_dim(w_qkv, (1 - core) * DH, DH, axis=2).reshape(192, 3 * DH)
        w_same = relabel(w_mine)
        w_cross = relabel_cross(w_other)
        w_block = jnp.where(
            core == 0,
            jnp.concatenate([w_same, w_cross], axis=0),
            jnp.concatenate([w_cross, w_same], axis=0),
        )
        w_all = lax.all_gather(w_block, ("x", "y"), axis=0)

    with jax.named_scope("tokens"):
        line = spread(tokens, "y", NY)
        t0 = relabel(line)
        t1 = along_z(t0, -1)
        t3 = along_z(t0, 1)
        t2a = along_z(t0[:, :64], 2)
        t2b = along_z(t0[:, 64:], -2)
        mine = (t0, t1, t2a, t2b, t3)
        theirs = tuple(swap_cores(t) for t in mine)

    with jax.named_scope("gains"):
        gains = spread(
            jnp.concatenate([ln_gain.astype(jnp.float32), q_gain, k_gain]), ("zl", "y"), NZL * NY
        )
        gain = gains[:, None, :384]
        head = lax.dynamic_slice_in_dim(gains, zl * NY + zh, 1, axis=0)
        head = lax.dynamic_slice_in_dim(head[:, 384:].reshape(2, 2, DH), core, 1, axis=1)

    with jax.named_scope("project"):
        kv, q = pl.pallas_call(
            project_kernel,
            out_shape=(
                jax.ShapeDtypeStruct((256, 2 * DH), jnp.bfloat16),
                jax.ShapeDtypeStruct((256, DH), jnp.bfloat16),
            ),
            in_specs=[pl.BlockSpec(memory_space=pltpu.SMEM)]
            + [pl.BlockSpec(memory_space=pltpu.VMEM)] * 13,
            out_specs=(pl.BlockSpec(memory_space=pltpu.VMEM),) * 2,
            scratch_shapes=[pltpu.VMEM((8, 128), jnp.float32)],
            compiler_params=pltpu.CompilerParams(vmem_limit_bytes=VMEM_LIMIT),
        )(zl.reshape(1).astype(jnp.int32), *mine, *theirs, gain, head, w_all)

    with jax.named_scope("keys"):
        kv_all = spread(kv, ("x", "y"), NX * NY)

    with jax.named_scope("attend"):
        out = pl.pallas_call(
            attend_kernel,
            out_shape=jax.ShapeDtypeStruct((256, DH), jnp.bfloat16),
            in_specs=[pl.BlockSpec(memory_space=pltpu.VMEM)] * 2,
            out_specs=pl.BlockSpec(memory_space=pltpu.VMEM),
            compiler_params=pltpu.CompilerParams(vmem_limit_bytes=VMEM_LIMIT),
        )(q, kv_all)

    with jax.named_scope("home"):
        same = relabel(out[:128])
        cross = relabel_cross(out[128:])
        return jnp.where(
            core == 0,
            jnp.concatenate([same, cross], axis=1),
            jnp.concatenate([cross, same], axis=1),
        )


def solution(mesh):
    fine = Mesh(mesh.devices.reshape(SIZES), AXES)
    rows = ("x", "zh", "core")
    cols = ("zl", "y")
    in_specs = (P(rows, cols), P(cols), P(rows, None, cols), P(cols), P(cols))
    return jax.shard_map(body, mesh=fine, in_specs=in_specs, out_specs=P(rows, cols), check_vma=False)
```

```python
import numpy as np
import jax
import jax.numpy as jnp
from jax import lax
from jax.experimental import pallas as pl
from jax.experimental.pallas import tpu as pltpu
from jax.sharding import Mesh, PartitionSpec as P

DH = 128
EPSILON = 1e-06
NX = NZH = NZL = NY = 4
CORES = 2
AXES = ("x", "zh", "core", "zl", "y")
SIZES = (NX, NZH, CORES, NZL, NY)
VMEM_LIMIT = 56 * 1024 * 1024


def shift(values, axes, move):
    sizes = [SIZES[AXES.index(axis)] for axis in axes]
    pairs = [
        (int(np.ravel_multi_index(src, sizes)), int(np.ravel_multi_index(move(src), sizes)))
        for src in np.ndindex(*sizes)
    ]
    return lax.ppermute(values, axes, pairs)


def relabel(values):
    return shift(values, ("zh", "core", "zl", "y"), lambda i: (i[3], i[1], i[2], i[0]))


def relabel_cross(values):
    return shift(values, ("zh", "core", "zl", "y"), lambda i: (i[3], 1 - i[1], i[2], i[0]))


def rotate(values):
    return shift(values, ("x", "zh", "zl", "y"), lambda i: (i[2], i[3], i[0], i[1]))


def along_z(values, step):
    return shift(values, ("zh", "zl"), lambda i: divmod((i[0] * NZL + i[1] + step) % 16, NZL))


def swap_cores(values):
    return shift(values, ("core",), lambda i: (1 - i[0],))


def spread(values, axes, count):
    return lax.all_to_all(jnp.broadcast_to(values[None], (count,) + values.shape), axes, 0, 0)


def partial_kernel(
    where, t0, t1, t2a, t2b, t3, p0, p1, p2a, p2b, p3, w, out
):
    zl = where[0]
    pieces = (
        (t0, p0),
        (t1, p1),
        (t2a, t2b, p2a, p2b),
        (t3, p3),
    )
    for slot in range(4):
        acc = None
        for y in range(NY):
            x = jnp.concatenate([ref[y] for ref in pieces[slot]], axis=0)
            term = jnp.dot(x, w[y], preferred_element_type=jnp.float32)
            acc = term if acc is None else acc + term
        out[lax.rem(zl + slot, NZL)] = acc


def heads_kernel(part, head_gain, kv_out, q_out):
    acc = part[0] + part[1] + part[2] + part[3]

    def head_norm(values, row):
        mid = jnp.mean(values, axis=1, keepdims=True)
        var = jnp.mean(values * values, axis=1, keepdims=True) - mid * mid
        return ((values - mid) * lax.rsqrt(var + EPSILON) * row).astype(jnp.bfloat16)

    q_out[...] = head_norm(acc[:, :DH], head_gain[0])
    kv_out[:, :DH] = head_norm(acc[:, DH : 2 * DH], head_gain[1])
    kv_out[:, DH:] = acc[:, 2 * DH :].astype(jnp.bfloat16)


def attend_kernel(q, kv, out):
    keys = kv[:, :, :DH].reshape(-1, DH)
    values = kv[:, :, DH:].reshape(-1, DH)
    scores = lax.dot_general(
        q[...], keys, (((1,), (1,)), ((), ())), preferred_element_type=jnp.float32
    ) * (DH ** -0.5)
    top = jnp.max(scores, axis=1, keepdims=True)
    weights = jnp.exp(scores - top)
    total = jnp.sum(weights, axis=1, keepdims=True)
    mixed = jnp.dot(weights.astype(jnp.bfloat16), values, preferred_element_type=jnp.float32)
    out[...] = (mixed / total).astype(jnp.bfloat16)


def kernel_call(kernel, out_shape, args, scalars=0):
    vmem = pl.BlockSpec(memory_space=pltpu.VMEM)
    smem = pl.BlockSpec(memory_space=pltpu.SMEM)
    return pl.pallas_call(
        kernel,
        out_shape=out_shape,
        in_specs=[smem] * scalars + [vmem] * (len(args) - scalars),
        out_specs=jax.tree.map(lambda _: vmem, out_shape),
        compiler_params=pltpu.CompilerParams(vmem_limit_bytes=VMEM_LIMIT),
    )(*args)


def body(tokens, ln_gain, w_qkv, q_gain, k_gain):
    core = lax.axis_index("core")
    zl = lax.axis_index("zl")
    zh = lax.axis_index("zh")

    with jax.named_scope("weights"):
        w_mine = lax.dynamic_slice_in_dim(w_qkv, core * DH, DH, axis=2).reshape(192, 3 * DH)
        w_other = lax.dynamic_slice_in_dim(w_qkv, (1 - core) * DH, DH, axis=2).reshape(192, 3 * DH)
        w_same = relabel(w_mine)
        w_cross = relabel_cross(w_other)

    with jax.named_scope("norm"):
        x = tokens.astype(jnp.float32)
        sums = jnp.concatenate([jnp.sum(x, axis=1), jnp.sum(x * x, axis=1), q_gain, k_gain])
        shared = spread(sums[None], ("zl", "y"), NZL * NY)
        features = tokens.shape[1] * NZL * NY
        stats = jnp.sum(shared[:, 0, :256], axis=0) / features
        center = stats[:128, None]
        var = stats[128:, None] - center * center
        normed = ((x - center) * lax.rsqrt(var + EPSILON) * ln_gain.astype(jnp.float32)).astype(
            jnp.bfloat16
        )
        head = lax.dynamic_slice_in_dim(shared[:, 0, 256:], zl * NY + zh, 1, axis=0)
        head = lax.dynamic_slice_in_dim(head.reshape(2, 2, DH), core, 1, axis=1)

    with jax.named_scope("tokens"):
        line = spread(normed, "y", NY)
        t0 = rotate(line)
        t1 = along_z(t0, -1)
        t3 = along_z(t0, 1)
        t2a = along_z(t0[:, :64], 2)
        t2b = along_z(t0[:, 64:], -2)
        mine = (t0, t1, t2a, t2b, t3)
        theirs = tuple(swap_cores(t) for t in mine)

    with jax.named_scope("weights"):
        w_block = jnp.where(
            core == 0,
            jnp.concatenate([w_same, w_cross], axis=0),
            jnp.concatenate([w_cross, w_same], axis=0),
        )
        w_line = spread(w_block, "y", NY)

    with jax.named_scope("project"):
        part = kernel_call(
            partial_kernel,
            jax.ShapeDtypeStruct((NX, 256, 3 * DH), jnp.float32),
            (zl.reshape(1).astype(jnp.int32), *mine, *theirs, w_line),
            scalars=1,
        )
        part = lax.all_to_all(part, "x", 0, 0)
        kv, q = kernel_call(
            heads_kernel,
            (
                jax.ShapeDtypeStruct((256, 2 * DH), jnp.bfloat16),
                jax.ShapeDtypeStruct((256, DH), jnp.bfloat16),
            ),
            (part, head),
        )

    with jax.named_scope("keys"):
        kv_all = spread(kv, ("x", "y"), NX * NY)

    with jax.named_scope("attend"):
        out = kernel_call(
            attend_kernel, jax.ShapeDtypeStruct((256, DH), jnp.bfloat16), (q, kv_all)
        )

    with jax.named_scope("home"):
        same = relabel(out[:128])
        cross = relabel_cross(out[128:])
        return jnp.where(
            core == 0,
            jnp.concatenate([same, cross], axis=1),
            jnp.concatenate([cross, same], axis=1),
        )


def solution(mesh):
    fine = Mesh(mesh.devices.reshape(SIZES), AXES)
    rows = ("x", "zh", "core")
    cols = ("zl", "y")
    in_specs = (P(rows, cols), P(cols), P(rows, None, cols), P(cols), P(cols))
    return jax.shard_map(body, mesh=fine, in_specs=in_specs, out_specs=P(rows, cols), check_vma=False)
```

```python
import numpy as np
import jax
import jax.numpy as jnp
from jax import lax
from jax.experimental import pallas as pl
from jax.experimental.pallas import tpu as pltpu
from jax.sharding import Mesh, PartitionSpec as P

DH = 128
EPSILON = 1e-06
NX = NZH = NZL = NY = 4
CORES = 2
AXES = ("x", "zh", "core", "zl", "y")
SIZES = (NX, NZH, CORES, NZL, NY)
VMEM_LIMIT = 56 * 1024 * 1024


def shift(values, axes, move):
    sizes = [SIZES[AXES.index(axis)] for axis in axes]
    pairs = [
        (int(np.ravel_multi_index(src, sizes)), int(np.ravel_multi_index(move(src), sizes)))
        for src in np.ndindex(*sizes)
    ]
    return lax.ppermute(values, axes, pairs)


def to_plane(values):
    return shift(values, ("zh", "zl", "y"), lambda i: ((i[2] + i[1]) % NZH, i[1], i[0]))


def to_home(values, cross):
    return shift(
        values,
        ("zh", "core", "zl", "y"),
        lambda i: ((i[0] + i[2] + i[3]) % NZH, i[1] ^ cross, i[2], (i[0] - i[2]) % NY),
    )


def along_z(values, step):
    return shift(values, ("zh", "zl"), lambda i: divmod((i[0] * NZL + i[1] + step) % 16, NZL))


def swap_cores(values):
    return shift(values, ("core",), lambda i: (1 - i[0],))


def spread(values, axes, count):
    return lax.all_to_all(jnp.broadcast_to(values[None], (count,) + values.shape), axes, 0, 0)


def partial_kernel(where, t0, t1, t2a, t2b, t3, stats, gain, w_mine, w_theirs, out, w, acc):
    zl, core, turn = where[0], where[1], where[2]
    half = w_mine.shape[1]
    for x in range(NX):
        w[x, pl.ds(pl.multiple_of(core * half, half), half)] = w_mine[x]
        w[x, pl.ds(pl.multiple_of((1 - core) * half, half), half)] = w_theirs[x]
    pieces = ((t0,), (t1,), (t2a, t2b), (t3,))
    for slot in range(NZL):
        part = lax.rem(zl + slot, NZL)
        row_gain = gain[part]
        normed = []
        for quarter in range(NZH):
            x = [ref[quarter].astype(jnp.float32) for ref in pieces[slot]]
            x = x[0] if len(x) == 1 else jnp.concatenate(x, axis=0)
            center = stats[quarter, :, 0:1]
            scale = stats[quarter, :, 1:2]
            normed.append(((x - center) * scale * row_gain).astype(jnp.bfloat16))
        term = jnp.dot(
            jnp.concatenate(normed, axis=0), w[part], preferred_element_type=jnp.float32
        )
        if slot == 0:
            acc[...] = term
        elif slot < NZL - 1:
            acc[...] += term
        else:
            for quarter in range(NZH):
                rows = slice(quarter * 128, quarter * 128 + 128)
                out[lax.rem(turn + quarter, NZH)] = acc[rows] + term[rows]


def heads_kernel(where, part, head_gain, out):
    core = where[1]
    acc = part[0] + part[1] + part[2] + part[3]

    def head_norm(values, row):
        mid = jnp.mean(values, axis=1, keepdims=True)
        var = jnp.mean(values * values, axis=1, keepdims=True) - mid * mid
        return ((values - mid) * lax.rsqrt(var + EPSILON) * row).astype(jnp.bfloat16)

    for head in range(2):
        slot = lax.rem(core + head, 2)
        cols = [slice(s * 256 + head * DH, s * 256 + head * DH + DH) for s in range(3)]
        out[slot, 0] = head_norm(acc[:, cols[0]], head_gain[0, :, head * DH : head * DH + DH])
        out[slot, 1] = head_norm(acc[:, cols[1]], head_gain[1, :, head * DH : head * DH + DH])
        out[slot, 2] = acc[:, cols[2]].astype(jnp.bfloat16)


def attend_kernel(q, kv, out):
    keys = kv[:, :, 0].reshape(-1, DH)
    values = kv[:, :, 1].reshape(-1, DH)
    queries = q[...].reshape(-1, DH)
    scores = lax.dot_general(
        queries, keys, (((1,), (1,)), ((), ())), preferred_element_type=jnp.float32
    ) * (DH ** -0.5)
    top = jnp.max(scores, axis=1, keepdims=True)
    weights = jnp.exp(scores - top)
    total = jnp.sum(weights, axis=1, keepdims=True)
    mixed = jnp.dot(weights.astype(jnp.bfloat16), values, preferred_element_type=jnp.float32)
    out[...] = (mixed / total).astype(jnp.bfloat16)


def kernel_call(kernel, out_shape, args, scalars=0, scratch=()):
    vmem = pl.BlockSpec(memory_space=pltpu.VMEM)
    smem = pl.BlockSpec(memory_space=pltpu.SMEM)
    return pl.pallas_call(
        kernel,
        out_shape=out_shape,
        in_specs=[smem] * scalars + [vmem] * (len(args) - scalars),
        out_specs=jax.tree.map(lambda _: vmem, out_shape),
        scratch_shapes=scratch,
        compiler_params=pltpu.CompilerParams(vmem_limit_bytes=VMEM_LIMIT),
    )(*args)


def body(tokens, ln_gain, w_qkv, q_gain, k_gain):
    core = lax.axis_index("core")
    zl = lax.axis_index("zl")
    zh = lax.axis_index("zh")
    y_here = lax.axis_index("y")
    turn = (2 * NZH - zh - zl) % NZH
    where = jnp.stack([zl, core, turn]).astype(jnp.int32)

    with jax.named_scope("weights"):
        w_moved = to_plane(w_qkv)

    with jax.named_scope("tokens"):
        t0, w_moved = lax.optimization_barrier((spread(tokens, "zh", NZH), w_moved))
        t1 = along_z(t0, -1)
        t3 = along_z(t0, 1)
        t2a = along_z(t0[:, :64], 2)
        t2b = along_z(t0[:, 64:], -2)

    with jax.named_scope("norm"):
        x = tokens.astype(jnp.float32)
        shared = spread(
            jnp.concatenate(
                [
                    jnp.sum(x, axis=1),
                    jnp.sum(x * x, axis=1),
                    ln_gain.astype(jnp.float32),
                    q_gain,
                    k_gain,
                ]
            )[None],
            ("zl", "y"),
            NZL * NY,
        )[:, 0]
        features = tokens.shape[1] * NZL * NY
        sums = spread(jnp.sum(shared[:, :256], axis=0)[None], "zh", NZH)[:, 0]
        center = sums[:, :128] / features
        var = sums[:, 128:] / features - center * center
        stats = jnp.stack([center, lax.rsqrt(var + EPSILON)], axis=2)
        gain = lax.dynamic_index_in_dim(
            shared[:, 256:640].reshape(NZL, NY, 1, 384), y_here, 1, keepdims=False
        )
        head_gain = lax.dynamic_index_in_dim(
            shared[:, 640:], zl * NY + (zh + NY - zl) % NY, 0, keepdims=False
        ).reshape(2, 1, 256)

    with jax.named_scope("weights"):
        w_mine = spread(w_moved.reshape(192, 768), "x", NX)
        w_theirs = swap_cores(w_mine)

    with jax.named_scope("project"):
        part = kernel_call(
            partial_kernel,
            jax.ShapeDtypeStruct((NZH, 128, 768), jnp.float32),
            (where, t0, t1, t2a, t2b, t3, stats, gain, w_mine, w_theirs),
            scalars=1,
            scratch=[
                pltpu.VMEM((NX, 384, 768), jnp.bfloat16),
                pltpu.VMEM((512, 768), jnp.float32),
            ],
        )
        part = lax.all_to_all(part, "y", 0, 0)
        heads = kernel_call(
            heads_kernel,
            jax.ShapeDtypeStruct((2, 3, 128, DH), jnp.bfloat16),
            (where, part, head_gain),
            scalars=1,
        )
        both = jnp.stack([heads[0], swap_cores(heads[1])])

    with jax.named_scope("keys"):
        kv_all = spread(both[:, 1:], ("x", "y"), NX * NY)

    with jax.named_scope("attend"):
        out = kernel_call(
            attend_kernel, jax.ShapeDtypeStruct((256, DH), jnp.bfloat16), (both[:, 0], kv_all)
        )

    with jax.named_scope("home"):
        same = to_home(out[:128], 0)
        cross = to_home(out[128:], 1)
        return jnp.where(
            core == 0,
            jnp.concatenate([same, cross], axis=1),
            jnp.concatenate([cross, same], axis=1),
        )


def solution(mesh):
    fine = Mesh(mesh.devices.reshape(SIZES), AXES)
    rows = ("x", "zh", "core")
    cols = ("zl", "y")
    in_specs = (P(rows, cols), P(cols), P(rows, None, cols), P(cols), P(cols))
    return jax.shard_map(body, mesh=fine, in_specs=in_specs, out_specs=P(rows, cols), check_vma=False)
```

```python
import numpy as np
import jax
import jax.numpy as jnp
from jax import lax
from jax.experimental import pallas as pl
from jax.experimental.pallas import tpu as pltpu
from jax.sharding import Mesh, PartitionSpec as P

DH = 128
EPSILON = 1e-06
NX = NZH = NZL = NY = 4
CORES = 2
AXES = ("x", "zh", "core", "zl", "y")
SIZES = (NX, NZH, CORES, NZL, NY)
VMEM_LIMIT = 28 * 1024 * 1024


def shift(values, axes, move):
    sizes = [SIZES[AXES.index(axis)] for axis in axes]
    pairs = [
        (int(np.ravel_multi_index(src, sizes)), int(np.ravel_multi_index(move(src), sizes)))
        for src in np.ndindex(*sizes)
    ]
    return lax.ppermute(values, axes, pairs)


def to_plane(values):
    return shift(values, ("zh", "zl", "y"), lambda i: ((i[2] + i[1]) % NZH, i[1], i[0]))


def to_home(values, cross):
    return shift(
        values,
        ("zh", "core", "zl", "y"),
        lambda i: ((i[0] + i[2] + i[3]) % NZH, i[1] ^ cross, i[2], (i[0] - i[2]) % NY),
    )


def along_z(values, step):
    return shift(values, ("zh", "zl"), lambda i: divmod((i[0] * NZL + i[1] + step) % 16, NZL))


def swap_cores(values):
    return shift(values, ("core",), lambda i: (1 - i[0],))


def spread(values, axes, count):
    return lax.all_to_all(jnp.broadcast_to(values[None], (count,) + values.shape), axes, 0, 0)


def partial_kernel(where, t0, t1, t2a, t2b, t3, stats, gain, w_mine, w_theirs, out, w, acc):
    zl, core, turn = where[0], where[1], where[2]
    half = w_mine.shape[1]
    for x in range(NX):
        w[x, pl.ds(pl.multiple_of(core * half, half), half)] = w_mine[x]
        w[x, pl.ds(pl.multiple_of((1 - core) * half, half), half)] = w_theirs[x]
    pieces = ((t0,), (t1,), (t2a, t2b), (t3,))
    for slot in range(NZL):
        part = lax.rem(zl + slot, NZL)
        row_gain = gain[part]
        normed = []
        for quarter in range(NZH):
            x = [ref[quarter].astype(jnp.float32) for ref in pieces[slot]]
            x = x[0] if len(x) == 1 else jnp.concatenate(x, axis=0)
            center = stats[quarter, :, 0:1]
            scale = stats[quarter, :, 1:2]
            normed.append(((x - center) * scale * row_gain).astype(jnp.bfloat16))
        term = jnp.dot(
            jnp.concatenate(normed, axis=0), w[part], preferred_element_type=jnp.float32
        )
        if slot == 0:
            acc[...] = term
        elif slot < NZL - 1:
            acc[...] += term
        else:
            total = acc[...] + term
            for quarter in range(NZH):
                rows = slice(quarter * 128, quarter * 128 + 128)
                for head in range(2):
                    for s in range(3):
                        cols = slice(s * 256 + head * DH, s * 256 + head * DH + DH)
                        out[head, lax.rem(turn + quarter, NZH), :, s * DH : s * DH + DH] = total[
                            rows, cols
                        ]


def heads_kernel(part, head_gain, q_out, kv_out):
    def head_norm(values, row):
        mid = jnp.mean(values, axis=1, keepdims=True)
        var = jnp.mean(values * values, axis=1, keepdims=True) - mid * mid
        return ((values - mid) * lax.rsqrt(var + EPSILON) * row).astype(jnp.bfloat16)

    for source in range(2):
        rows = slice(source * 128, source * 128 + 128)
        acc = part[source, 0] + part[source, 1] + part[source, 2] + part[source, 3]
        q_out[rows] = head_norm(acc[:, :DH], head_gain[0])
        kv_out[0, rows] = head_norm(acc[:, DH : 2 * DH], head_gain[1])
        kv_out[1, rows] = acc[:, 2 * DH :].astype(jnp.bfloat16)


def attend_kernel(q, kv, out):
    keys = kv[:, 0].reshape(-1, DH)
    values = kv[:, 1].reshape(-1, DH)
    scores = lax.dot_general(
        q[...], keys, (((1,), (1,)), ((), ())), preferred_element_type=jnp.float32
    ) * (DH ** -0.5)
    top = jnp.max(scores, axis=1, keepdims=True)
    weights = jnp.exp(scores - top)
    total = jnp.sum(weights, axis=1, keepdims=True)
    mixed = jnp.dot(weights.astype(jnp.bfloat16), values, preferred_element_type=jnp.float32)
    out[...] = (mixed / total).astype(jnp.bfloat16)


def kernel_call(kernel, out_shape, args, scalars=0, scratch=()):
    vmem = pl.BlockSpec(memory_space=pltpu.VMEM)
    smem = pl.BlockSpec(memory_space=pltpu.SMEM)
    return pl.pallas_call(
        kernel,
        out_shape=out_shape,
        in_specs=[smem] * scalars + [vmem] * (len(args) - scalars),
        out_specs=jax.tree.map(lambda _: vmem, out_shape),
        scratch_shapes=scratch,
        compiler_params=pltpu.CompilerParams(vmem_limit_bytes=VMEM_LIMIT),
    )(*args)


def body(tokens, ln_gain, w_qkv, q_gain, k_gain):
    core = lax.axis_index("core")
    zl = lax.axis_index("zl")
    zh = lax.axis_index("zh")
    y_here = lax.axis_index("y")
    turn = (2 * NZH - zh - zl) % NZH
    where = jnp.stack([zl, core, turn]).astype(jnp.int32)

    with jax.named_scope("weights"):
        w_moved = to_plane(w_qkv)

    with jax.named_scope("norm"):
        x = tokens.astype(jnp.float32)
        shared = spread(
            jnp.concatenate(
                [
                    jnp.sum(x, axis=1),
                    jnp.sum(x * x, axis=1),
                    ln_gain.astype(jnp.float32),
                    q_gain,
                    k_gain,
                ]
            )[None],
            ("zl", "y"),
            NZL * NY,
        )[:, 0]
        features = tokens.shape[1] * NZL * NY
        sums = spread(jnp.sum(shared[:, :256], axis=0)[None], "zh", NZH)[:, 0]
        center = sums[:, :128] / features
        var = sums[:, 128:] / features - center * center
        stats = jnp.stack([center, lax.rsqrt(var + EPSILON)], axis=2)
        gain = lax.dynamic_index_in_dim(
            shared[:, 256:640].reshape(NZL, NY, 1, 384), y_here, 1, keepdims=False
        )
        head_gain = lax.dynamic_index_in_dim(
            shared[:, 640:], zl * NY + (zh + NY - zl) % NY, 0, keepdims=False
        )
        head_gain = lax.dynamic_index_in_dim(head_gain.reshape(2, 2, 1, DH), core, 1, keepdims=False)

    with jax.named_scope("tokens"):
        t0, w_moved, stats, gain, head_gain = lax.optimization_barrier(
            (spread(tokens, "zh", NZH), w_moved, stats, gain, head_gain)
        )
        t1 = along_z(t0, -1)
        t3 = along_z(t0, 1)
        t2a = along_z(t0[:, :64], 2)
        t2b = along_z(t0[:, 64:], -2)

    with jax.named_scope("weights"):
        w_mine = spread(w_moved.reshape(192, 768), "x", NX)
        w_theirs = swap_cores(w_mine)

    with jax.named_scope("project"):
        part = kernel_call(
            partial_kernel,
            jax.ShapeDtypeStruct((CORES, NY, 128, 3 * DH), jnp.float32),
            (where, t0, t1, t2a, t2b, t3, stats, gain, w_mine, w_theirs),
            scalars=1,
            scratch=[
                pltpu.VMEM((NX, 384, 768), jnp.bfloat16),
                pltpu.VMEM((512, 768), jnp.float32),
            ],
        )
        part = part.reshape(CORES * NY, 128, 3 * DH)
        part = lax.all_to_all(part, ("core", "y"), 0, 0).reshape(CORES, NY, 128, 3 * DH)
        q, kv = kernel_call(
            heads_kernel,
            (
                jax.ShapeDtypeStruct((256, DH), jnp.bfloat16),
                jax.ShapeDtypeStruct((2, 256, DH), jnp.bfloat16),
            ),
            (part, head_gain),
        )

    with jax.named_scope("keys"):
        kv_all = spread(kv, ("x", "y"), NX * NY)

    with jax.named_scope("attend"):
        out = kernel_call(
            attend_kernel, jax.ShapeDtypeStruct((256, DH), jnp.bfloat16), (q, kv_all)
        )

    with jax.named_scope("home"):
        same = to_home(lax.dynamic_slice_in_dim(out, core * 128, 128), 0)
        cross = to_home(lax.dynamic_slice_in_dim(out, (1 - core) * 128, 128), 1)
        return jnp.where(
            core == 0,
            jnp.concatenate([same, cross], axis=1),
            jnp.concatenate([cross, same], axis=1),
        )


def solution(mesh):
    fine = Mesh(mesh.devices.reshape(SIZES), AXES)
    rows = ("x", "zh", "core")
    cols = ("zl", "y")
    in_specs = (P(rows, cols), P(cols), P(rows, None, cols), P(cols), P(cols))
    return jax.shard_map(body, mesh=fine, in_specs=in_specs, out_specs=P(rows, cols), check_vma=False)
```

```python
import numpy as np
import jax
import jax.numpy as jnp
from jax import lax
from jax.experimental import pallas as pl
from jax.experimental.pallas import tpu as pltpu
from jax.sharding import Mesh, PartitionSpec as P

DH = 128
EPSILON = 1e-06
FEATURES = 6144
NX = NZH = NZL = NY = 4
CORES = 2
AXES = ("x", "zh", "core", "zl", "y")
SIZES = (NX, NZH, CORES, NZL, NY)
VMEM_LIMIT = 28 * 1024 * 1024


def shift(values, axes, move):
    sizes = [SIZES[AXES.index(axis)] for axis in axes]
    pairs = [
        (int(np.ravel_multi_index(src, sizes)), int(np.ravel_multi_index(move(src), sizes)))
        for src in np.ndindex(*sizes)
    ]
    return lax.ppermute(values, axes, pairs)


def to_plane(values):
    return shift(values, ("zh", "zl", "y"), lambda i: ((i[2] + i[1]) % NZH, i[1], i[0]))


def to_home(values, cross):
    return shift(
        values,
        ("zh", "core", "zl", "y"),
        lambda i: ((i[0] + i[2] + i[3]) % NZH, i[1] ^ cross, i[2], (i[0] - i[2]) % NY),
    )


def along_z(values, step):
    return shift(values, ("zh", "zl"), lambda i: divmod((i[0] * NZL + i[1] + step) % 16, NZL))


def swap_cores(values):
    return shift(values, ("core",), lambda i: (1 - i[0],))


def spread(values, axes, count):
    return lax.all_to_all(jnp.broadcast_to(values[None], (count,) + values.shape), axes, 0, 0)


def pieces_of(values):
    high = lax.reduce_precision(values, 8, 7)
    rest = values - high
    mid = lax.reduce_precision(rest, 8, 7)
    return jnp.concatenate([high, mid, rest - mid]).astype(jnp.bfloat16)


def partial_kernel(where, t0, t1, t2a, t2b, t3, w_mine, w_theirs, out, w, acc):
    zl, core, turn, x_here = where[0], where[1], where[2], where[3]
    half = w_mine.shape[2]
    for step in range(NX):
        x = lax.rem(x_here + step, NX)
        for s in range(3):
            cols = slice(s * 256, s * 256 + 256)
            w[x, pl.ds(pl.multiple_of(core * half, half), half), cols] = w_mine[step, s]
            w[x, pl.ds(pl.multiple_of((1 - core) * half, half), half), cols] = w_theirs[step, s]
    tokens = (
        ((t0, 128),),
        ((t1, 128),),
        ((t2a, 80), (t2b, 48)),
        ((t3, 128),),
    )
    extras = ((t0, 128), (t1, 128), (t2b, 48), (t3, 128))

    def extra(slot, quarter):
        ref, row = extras[slot]
        return ref[quarter, row : row + 16].astype(jnp.float32)

    centers, scales = [], []
    for quarter in range(NZH):
        rows = sum(extra(slot, quarter)[:2] for slot in range(NZL))
        sums = (rows[:, :128] + rows[:, 128:256] + rows[:, 256:]) / FEATURES
        center = sums[0:1]
        centers.append(center)
        scales.append(lax.rsqrt(sums[1:2] - center * center + EPSILON))
    stats = jnp.concatenate(centers + scales, axis=0).T

    for slot in range(NZL):
        row_gain = extra(slot, 0)[2:3]
        normed = []
        for quarter in range(NZH):
            x = [ref[quarter, :count].astype(jnp.float32) for ref, count in tokens[slot]]
            x = x[0] if len(x) == 1 else jnp.concatenate(x, axis=0)
            center = stats[:, quarter : quarter + 1]
            scale = stats[:, NZH + quarter : NZH + quarter + 1]
            normed.append(((x - center) * scale * row_gain).astype(jnp.bfloat16))
        term = jnp.dot(
            jnp.concatenate(normed, axis=0),
            w[lax.rem(zl + slot, NZL)],
            preferred_element_type=jnp.float32,
        )
        if slot == 0:
            acc[...] = term
        elif slot < NZL - 1:
            acc[...] += term
        else:
            total = acc[...] + term
            for quarter in range(NZH):
                rows = slice(quarter * 128, quarter * 128 + 128)
                for head in range(2):
                    for s in range(3):
                        cols = slice(s * 256 + head * DH, s * 256 + head * DH + DH)
                        out[head, lax.rem(turn + quarter, NZH), :, s * DH : s * DH + DH] = total[
                            rows, cols
                        ]


def heads_kernel(part, head_gain, q_out, kv_out):
    def head_norm(values, row):
        mid = jnp.mean(values, axis=1, keepdims=True)
        var = jnp.mean(values * values, axis=1, keepdims=True) - mid * mid
        return ((values - mid) * lax.rsqrt(var + EPSILON) * row).astype(jnp.bfloat16)

    for source in range(2):
        rows = slice(source * 128, source * 128 + 128)
        acc = part[source, 0] + part[source, 1] + part[source, 2] + part[source, 3]
        q_out[rows] = head_norm(acc[:, :DH], head_gain[0])
        kv_out[0, rows] = head_norm(acc[:, DH : 2 * DH], head_gain[1])
        kv_out[1, rows] = acc[:, 2 * DH :].astype(jnp.bfloat16)


def attend_kernel(q, kv, out):
    keys = kv[:, 0].reshape(-1, DH)
    values = kv[:, 1].reshape(-1, DH)
    scores = lax.dot_general(
        q[...], keys, (((1,), (1,)), ((), ())), preferred_element_type=jnp.float32
    ) * (DH ** -0.5)
    top = jnp.max(scores, axis=1, keepdims=True)
    weights = jnp.exp(scores - top)
    total = jnp.sum(weights, axis=1, keepdims=True)
    mixed = jnp.dot(weights.astype(jnp.bfloat16), values, preferred_element_type=jnp.float32)
    out[...] = (mixed / total).astype(jnp.bfloat16)


def kernel_call(kernel, out_shape, args, scalars=0, scratch=()):
    vmem = pl.BlockSpec(memory_space=pltpu.VMEM)
    smem = pl.BlockSpec(memory_space=pltpu.SMEM)
    return pl.pallas_call(
        kernel,
        out_shape=out_shape,
        in_specs=[smem] * scalars + [vmem] * (len(args) - scalars),
        out_specs=jax.tree.map(lambda _: vmem, out_shape),
        scratch_shapes=scratch,
        compiler_params=pltpu.CompilerParams(vmem_limit_bytes=VMEM_LIMIT),
    )(*args)


def body(tokens, ln_gain, w_qkv, q_gain, k_gain):
    core = lax.axis_index("core")
    zl = lax.axis_index("zl")
    zh = lax.axis_index("zh")
    turn = (2 * NZH - zh - zl) % NZH
    where = jnp.stack([zl, core, turn, lax.axis_index("x")]).astype(jnp.int32)

    with jax.named_scope("weights"):
        w_moved = to_plane(jnp.transpose(w_qkv, (1, 0, 2)))

    with jax.named_scope("norm"):
        x = tokens.astype(jnp.float32)
        shared = spread(
            jnp.concatenate([jnp.sum(x, axis=1), jnp.sum(x * x, axis=1), q_gain, k_gain])[None],
            "y",
            NY,
        )[:, 0]
        sums = jnp.sum(shared[:, :256], axis=0)
        head_gain = lax.dynamic_index_in_dim(
            shared[:, 256:], (zh + NY - zl) % NY, 0, keepdims=False
        )
        head_gain = lax.dynamic_index_in_dim(head_gain.reshape(2, 2, 1, DH), core, 1, keepdims=False)
        extended = jnp.concatenate(
            [
                tokens,
                pieces_of(sums[:128])[None],
                pieces_of(sums[128:])[None],
                ln_gain[None],
                jnp.zeros((13, 384), jnp.bfloat16),
            ]
        )

    with jax.named_scope("tokens"):
        t0, w_moved = lax.optimization_barrier((spread(extended, "zh", NZH), w_moved))
        t1 = along_z(t0, -1)
        t3 = along_z(t0, 1)
        t2a = along_z(t0[:, :80], 2)
        t2b = along_z(t0[:, 80:], -2)

    with jax.named_scope("weights"):
        along_x = [
            shift(w_moved, ("x",), lambda i, step=step: ((i[0] - step) % NX,)) for step in (1, 2, 3)
        ]
        t2a, t2b, *along_x = lax.optimization_barrier((t2a, t2b, *along_x))
        w_mine = jnp.stack([w_moved] + along_x)
        w_theirs = swap_cores(w_mine)

    with jax.named_scope("project"):
        part = kernel_call(
            partial_kernel,
            jax.ShapeDtypeStruct((CORES, NY, 128, 3 * DH), jnp.float32),
            (where, t0, t1, t2a, t2b, t3, w_mine, w_theirs),
            scalars=1,
            scratch=[
                pltpu.VMEM((NX, 384, 768), jnp.bfloat16),
                pltpu.VMEM((512, 768), jnp.float32),
            ],
        )
        part = part.reshape(CORES * NY, 128, 3 * DH)
        part = lax.all_to_all(part, ("core", "y"), 0, 0).reshape(CORES, NY, 128, 3 * DH)
        q, kv = kernel_call(
            heads_kernel,
            (
                jax.ShapeDtypeStruct((256, DH), jnp.bfloat16),
                jax.ShapeDtypeStruct((2, 256, DH), jnp.bfloat16),
            ),
            (part, head_gain),
        )

    with jax.named_scope("keys"):
        kv_all = spread(kv, ("x", "y"), NX * NY)

    with jax.named_scope("attend"):
        out = kernel_call(
            attend_kernel, jax.ShapeDtypeStruct((256, DH), jnp.bfloat16), (q, kv_all)
        )

    with jax.named_scope("home"):
        same = to_home(lax.dynamic_slice_in_dim(out, core * 128, 128), 0)
        cross = to_home(lax.dynamic_slice_in_dim(out, (1 - core) * 128, 128), 1)
        return jnp.where(
            core == 0,
            jnp.concatenate([same, cross], axis=1),
            jnp.concatenate([cross, same], axis=1),
        )


def solution(mesh):
    fine = Mesh(mesh.devices.reshape(SIZES), AXES)
    rows = ("x", "zh", "core")
    cols = ("zl", "y")
    in_specs = (P(rows, cols), P(cols), P(rows, None, cols), P(cols), P(cols))
    return jax.shard_map(body, mesh=fine, in_specs=in_specs, out_specs=P(rows, cols), check_vma=False)
```

```python
import numpy as np
import jax
import jax.numpy as jnp
from jax import lax
from jax.experimental import pallas as pl
from jax.experimental.pallas import tpu as pltpu
from jax.sharding import Mesh, PartitionSpec as P

DH = 128
EPSILON = 1e-06
FEATURES = 6144
NX = NZH = NZL = NY = 4
CORES = 2
AXES = ("x", "zh", "core", "zl", "y")
SIZES = (NX, NZH, CORES, NZL, NY)
VMEM_LIMIT = 28 * 1024 * 1024


def shift(values, axes, move):
    sizes = [SIZES[AXES.index(axis)] for axis in axes]
    pairs = [
        (int(np.ravel_multi_index(src, sizes)), int(np.ravel_multi_index(move(src), sizes)))
        for src in np.ndindex(*sizes)
    ]
    return lax.ppermute(values, axes, pairs)


def to_plane(values):
    return shift(values, ("zh", "zl", "y"), lambda i: ((i[2] + i[1]) % NZH, i[1], i[0]))


def to_home(values, cross):
    return shift(
        values,
        ("zh", "core", "zl", "y"),
        lambda i: ((i[0] + i[2] + i[3]) % NZH, i[1] ^ cross, i[2], (i[0] - i[2]) % NY),
    )


def along_z(values, step):
    return shift(values, ("zh", "zl"), lambda i: divmod((i[0] * NZL + i[1] + step) % 16, NZL))


def swap_cores(values):
    return shift(values, ("core",), lambda i: (1 - i[0],))


def spread(values, axes, count):
    return lax.all_to_all(jnp.broadcast_to(values[None], (count,) + values.shape), axes, 0, 0)


def pieces_of(values):
    high = lax.reduce_precision(values, 8, 7)
    rest = values - high
    mid = lax.reduce_precision(rest, 8, 7)
    return jnp.concatenate([high, mid, rest - mid]).astype(jnp.bfloat16)


def partial_kernel(where, t0, t1, t2a, t2b, t3, w_mine, w_theirs, out, w, acc):
    zl, core, turn, x_here = where[0], where[1], where[2], where[3]
    half = w_mine.shape[2]
    for step in range(NX):
        x = lax.rem(x_here + step, NX)
        for s in range(3):
            cols = slice(s * 256, s * 256 + 256)
            w[x, pl.ds(pl.multiple_of(core * half, half), half), cols] = w_mine[step, s]
            w[x, pl.ds(pl.multiple_of((1 - core) * half, half), half), cols] = w_theirs[step, s]
    tokens = (
        ((t0, 128),),
        ((t1, 128),),
        ((t2a, 80), (t2b, 48)),
        ((t3, 128),),
    )
    extras = ((t0, 128), (t1, 128), (t2b, 48), (t3, 128))

    def extra(slot, quarter):
        ref, row = extras[slot]
        return ref[quarter, row : row + 16].astype(jnp.float32)

    centers, scales = [], []
    for quarter in range(NZH):
        rows = sum(extra(slot, quarter)[:2] for slot in range(NZL))
        sums = (rows[:, :128] + rows[:, 128:256] + rows[:, 256:]) / FEATURES
        center = sums[0:1]
        centers.append(center)
        scales.append(lax.rsqrt(sums[1:2] - center * center + EPSILON))
    stats = jnp.concatenate(centers + scales, axis=0).T

    for slot in range(NZL):
        row_gain = extra(slot, 0)[2:3]
        normed = []
        for quarter in range(NZH):
            x = [ref[quarter, :count].astype(jnp.float32) for ref, count in tokens[slot]]
            x = x[0] if len(x) == 1 else jnp.concatenate(x, axis=0)
            center = stats[:, quarter : quarter + 1]
            scale = stats[:, NZH + quarter : NZH + quarter + 1]
            normed.append(((x - center) * scale * row_gain).astype(jnp.bfloat16))
        term = jnp.dot(
            jnp.concatenate(normed, axis=0),
            w[lax.rem(zl + slot, NZL)],
            preferred_element_type=jnp.float32,
        )
        if slot == 0:
            acc[...] = term
        elif slot < NZL - 1:
            acc[...] += term
        else:
            total = acc[...] + term
            for quarter in range(NZH):
                rows = slice(quarter * 128, quarter * 128 + 128)
                for head in range(2):
                    for s in range(3):
                        cols = slice(s * 256 + head * DH, s * 256 + head * DH + DH)
                        out[head, lax.rem(turn + quarter, NZH), :, s * DH : s * DH + DH] = total[
                            rows, cols
                        ]


def heads_kernel(part, head_gain, q_out, kv_out):
    def head_norm(values, row):
        mid = jnp.mean(values, axis=1, keepdims=True)
        var = jnp.mean(values * values, axis=1, keepdims=True) - mid * mid
        return ((values - mid) * lax.rsqrt(var + EPSILON) * row).astype(jnp.bfloat16)

    for source in range(2):
        rows = slice(source * 128, source * 128 + 128)
        acc = part[source, 0] + part[source, 1] + part[source, 2] + part[source, 3]
        q_out[rows] = head_norm(acc[:, :DH], head_gain[0])
        kv_out[0, rows] = head_norm(acc[:, DH : 2 * DH], head_gain[1])
        kv_out[1, rows] = acc[:, 2 * DH :].astype(jnp.bfloat16)


def attend_kernel(q, kv, out):
    keys = kv[:, 0].reshape(-1, DH)
    values = kv[:, 1].reshape(-1, DH)
    scores = lax.dot_general(
        q[...], keys, (((1,), (1,)), ((), ())), preferred_element_type=jnp.float32
    ) * (DH ** -0.5)
    top = jnp.max(scores, axis=1, keepdims=True)
    weights = jnp.exp(scores - top)
    total = jnp.sum(weights, axis=1, keepdims=True)
    mixed = jnp.dot(weights.astype(jnp.bfloat16), values, preferred_element_type=jnp.float32)
    out[...] = (mixed / total).astype(jnp.bfloat16)


def kernel_call(kernel, out_shape, args, scalars=0, scratch=()):
    vmem = pl.BlockSpec(memory_space=pltpu.VMEM)
    smem = pl.BlockSpec(memory_space=pltpu.SMEM)
    return pl.pallas_call(
        kernel,
        out_shape=out_shape,
        in_specs=[smem] * scalars + [vmem] * (len(args) - scalars),
        out_specs=jax.tree.map(lambda _: vmem, out_shape),
        scratch_shapes=scratch,
        compiler_params=pltpu.CompilerParams(vmem_limit_bytes=VMEM_LIMIT),
    )(*args)


def body(tokens, ln_gain, w_qkv, q_gain, k_gain):
    core = lax.axis_index("core")
    zl = lax.axis_index("zl")
    zh = lax.axis_index("zh")
    turn = (2 * NZH - zh - zl) % NZH
    where = jnp.stack([zl, core, turn, lax.axis_index("x")]).astype(jnp.int32)

    with jax.named_scope("weights"):
        w_moved = to_plane(jnp.transpose(w_qkv, (1, 0, 2)))

    with jax.named_scope("norm"):
        x = tokens.astype(jnp.float32)
        shared = spread(
            jnp.concatenate([jnp.sum(x, axis=1), jnp.sum(x * x, axis=1), q_gain, k_gain])[None],
            "y",
            NY,
        )[:, 0]
        sums = jnp.sum(shared[:, :256], axis=0)
        head_gain = lax.dynamic_index_in_dim(
            shared[:, 256:], (zh + NY - zl) % NY, 0, keepdims=False
        )
        head_gain = lax.dynamic_index_in_dim(head_gain.reshape(2, 2, 1, DH), core, 1, keepdims=False)
        extended = jnp.concatenate(
            [
                tokens,
                pieces_of(sums[:128])[None],
                pieces_of(sums[128:])[None],
                ln_gain[None],
                jnp.zeros((13, 384), jnp.bfloat16),
            ]
        )

    with jax.named_scope("tokens"):
        extended, w_moved = lax.optimization_barrier((extended, w_moved))
        t0 = spread(extended, "zh", NZH)

    with jax.named_scope("weights"):
        along_x = [
            shift(w_moved, ("x",), lambda i, step=step: ((i[0] - step) % NX,)) for step in (1, 2, 3)
        ]
        t0, *along_x = lax.optimization_barrier((t0, *along_x))
        w_mine = jnp.stack([w_moved] + along_x)
        w_theirs = swap_cores(w_mine)

    with jax.named_scope("tokens"):
        t1 = along_z(t0, -1)
        t3 = along_z(t0, 1)
        t2a = along_z(t0[:, :80], 2)
        t2b = along_z(t0[:, 80:], -2)

    with jax.named_scope("project"):
        part = kernel_call(
            partial_kernel,
            jax.ShapeDtypeStruct((CORES, NY, 128, 3 * DH), jnp.float32),
            (where, t0, t1, t2a, t2b, t3, w_mine, w_theirs),
            scalars=1,
            scratch=[
                pltpu.VMEM((NX, 384, 768), jnp.bfloat16),
                pltpu.VMEM((512, 768), jnp.float32),
            ],
        )
        part = part.reshape(CORES * NY, 128, 3 * DH)
        part = lax.all_to_all(part, ("core", "y"), 0, 0).reshape(CORES, NY, 128, 3 * DH)
        q, kv = kernel_call(
            heads_kernel,
            (
                jax.ShapeDtypeStruct((256, DH), jnp.bfloat16),
                jax.ShapeDtypeStruct((2, 256, DH), jnp.bfloat16),
            ),
            (part, head_gain),
        )

    with jax.named_scope("keys"):
        kv_all = spread(kv, ("x", "y"), NX * NY)

    with jax.named_scope("attend"):
        out = kernel_call(
            attend_kernel, jax.ShapeDtypeStruct((256, DH), jnp.bfloat16), (q, kv_all)
        )

    with jax.named_scope("home"):
        same = to_home(lax.dynamic_slice_in_dim(out, core * 128, 128), 0)
        cross = to_home(lax.dynamic_slice_in_dim(out, (1 - core) * 128, 128), 1)
        return jnp.where(
            core == 0,
            jnp.concatenate([same, cross], axis=1),
            jnp.concatenate([cross, same], axis=1),
        )


def solution(mesh):
    fine = Mesh(mesh.devices.reshape(SIZES), AXES)
    rows = ("x", "zh", "core")
    cols = ("zl", "y")
    in_specs = (P(rows, cols), P(cols), P(rows, None, cols), P(cols), P(cols))
    return jax.shard_map(body, mesh=fine, in_specs=in_specs, out_specs=P(rows, cols), check_vma=False)
```

```python
import numpy as np
import jax
import jax.numpy as jnp
from jax import lax
from jax.experimental import pallas as pl
from jax.experimental.pallas import tpu as pltpu
from jax.sharding import Mesh, PartitionSpec as P

DH = 128
EPSILON = 1e-06
FEATURES = 6144
NX = NZH = NZL = NY = 4
CORES = 2
AXES = ("x", "zh", "core", "zl", "y")
SIZES = (NX, NZH, CORES, NZL, NY)
VMEM_LIMIT = 28 * 1024 * 1024


def shift(values, axes, move):
    sizes = [SIZES[AXES.index(axis)] for axis in axes]
    pairs = [
        (int(np.ravel_multi_index(src, sizes)), int(np.ravel_multi_index(move(src), sizes)))
        for src in np.ndindex(*sizes)
    ]
    return lax.ppermute(values, axes, pairs)


def to_plane(values):
    return shift(values, ("zh", "zl", "y"), lambda i: ((i[2] + i[1]) % NZH, i[1], i[0]))


def to_home(values, cross):
    return shift(
        values,
        ("zh", "core", "zl", "y"),
        lambda i: ((i[0] + i[2] + i[3]) % NZH, i[1] ^ cross, i[2], (i[0] - i[2]) % NY),
    )


def along_z(values, step):
    return shift(values, ("zh", "zl"), lambda i: divmod((i[0] * NZL + i[1] + step) % 16, NZL))


def along_z_two(values):
    def move(i):
        step = 2 if i[1] % 2 == 0 else -2
        return divmod((i[0] * NZL + i[1] + step) % 16, NZL)

    return shift(values, ("zh", "zl"), move)


def swap_cores(values):
    return shift(values, ("core",), lambda i: (1 - i[0],))


def spread(values, axes, count):
    return lax.all_to_all(jnp.broadcast_to(values[None], (count,) + values.shape), axes, 0, 0)


def pieces_of(values):
    high = lax.reduce_precision(values, 8, 7)
    rest = values - high
    mid = lax.reduce_precision(rest, 8, 7)
    return jnp.concatenate([high, mid, rest - mid]).astype(jnp.bfloat16)


def partial_kernel(where, t0, t1, t2, t3, w_mine, w_theirs, out, w, acc):
    zl, core, turn, x_here = where[0], where[1], where[2], where[3]
    half = w_mine.shape[2]
    for step in range(NX):
        x = lax.rem(x_here + step, NX)
        for s in range(3):
            cols = slice(s * 256, s * 256 + 256)
            w[x, pl.ds(pl.multiple_of(core * half, half), half), cols] = w_mine[step, s]
            w[x, pl.ds(pl.multiple_of((1 - core) * half, half), half), cols] = w_theirs[step, s]
    tokens = (t0, t1, t2, t3)

    def extra(slot, quarter):
        return tokens[slot][quarter, 128:144].astype(jnp.float32)

    centers, scales = [], []
    for quarter in range(NZH):
        rows = sum(extra(slot, quarter)[:2] for slot in range(NZL))
        sums = (rows[:, :128] + rows[:, 128:256] + rows[:, 256:]) / FEATURES
        center = sums[0:1]
        centers.append(center)
        scales.append(lax.rsqrt(sums[1:2] - center * center + EPSILON))
    stats = jnp.concatenate(centers + scales, axis=0).T

    for slot in range(NZL):
        row_gain = extra(slot, 0)[2:3]
        normed = []
        for quarter in range(NZH):
            x = tokens[slot][quarter, :128].astype(jnp.float32)
            center = stats[:, quarter : quarter + 1]
            scale = stats[:, NZH + quarter : NZH + quarter + 1]
            normed.append(((x - center) * scale * row_gain).astype(jnp.bfloat16))
        term = jnp.dot(
            jnp.concatenate(normed, axis=0),
            w[lax.rem(zl + slot, NZL)],
            preferred_element_type=jnp.float32,
        )
        if slot == 0:
            acc[...] = term
        elif slot < NZL - 1:
            acc[...] += term
        else:
            total = acc[...] + term
            for quarter in range(NZH):
                rows = slice(quarter * 128, quarter * 128 + 128)
                for head in range(2):
                    for s in range(3):
                        cols = slice(s * 256 + head * DH, s * 256 + head * DH + DH)
                        out[head, lax.rem(turn + quarter, NZH), :, s * DH : s * DH + DH] = total[
                            rows, cols
                        ].astype(jnp.bfloat16)


def heads_kernel(part, head_gain, q_out, kv_out):
    def head_norm(values, row):
        mid = jnp.mean(values, axis=1, keepdims=True)
        var = jnp.mean(values * values, axis=1, keepdims=True) - mid * mid
        return ((values - mid) * lax.rsqrt(var + EPSILON) * row).astype(jnp.bfloat16)

    for source in range(2):
        rows = slice(source * 128, source * 128 + 128)
        acc = sum(part[source, y].astype(jnp.float32) for y in range(NY))
        q_out[rows] = head_norm(acc[:, :DH], head_gain[0])
        key = head_norm(acc[:, DH : 2 * DH], head_gain[1])
        value = acc[:, 2 * DH :].astype(jnp.bfloat16)
        for target in range(NX * NY):
            kv_out[target, 0, rows] = key
            kv_out[target, 1, rows] = value


def attend_kernel(q, kv, out):
    keys = kv[:, 0].reshape(-1, DH)
    values = kv[:, 1].reshape(-1, DH)
    scores = lax.dot_general(
        q[...], keys, (((1,), (1,)), ((), ())), preferred_element_type=jnp.float32
    ) * (DH ** -0.5)
    top = jnp.max(scores, axis=1, keepdims=True)
    weights = jnp.exp(scores - top)
    total = jnp.sum(weights, axis=1, keepdims=True)
    mixed = jnp.dot(weights.astype(jnp.bfloat16), values, preferred_element_type=jnp.float32)
    out[...] = (mixed / total).astype(jnp.bfloat16)


def kernel_call(kernel, out_shape, args, scalars=0, scratch=()):
    vmem = pl.BlockSpec(memory_space=pltpu.VMEM)
    smem = pl.BlockSpec(memory_space=pltpu.SMEM)
    return pl.pallas_call(
        kernel,
        out_shape=out_shape,
        in_specs=[smem] * scalars + [vmem] * (len(args) - scalars),
        out_specs=jax.tree.map(lambda _: vmem, out_shape),
        scratch_shapes=scratch,
        compiler_params=pltpu.CompilerParams(vmem_limit_bytes=VMEM_LIMIT),
    )(*args)


def body(tokens, ln_gain, w_qkv, q_gain, k_gain):
    core = lax.axis_index("core")
    zl = lax.axis_index("zl")
    zh = lax.axis_index("zh")
    turn = (2 * NZH - zh - zl) % NZH
    where = jnp.stack([zl, core, turn, lax.axis_index("x")]).astype(jnp.int32)

    with jax.named_scope("weights"):
        w_moved = to_plane(jnp.transpose(w_qkv, (1, 0, 2)))

    with jax.named_scope("norm"):
        x = tokens.astype(jnp.float32)
        shared = spread(
            jnp.concatenate([jnp.sum(x, axis=1), jnp.sum(x * x, axis=1), q_gain, k_gain])[None],
            "y",
            NY,
        )[:, 0]
        sums = jnp.sum(shared[:, :256], axis=0)
        head_gain = lax.dynamic_index_in_dim(
            shared[:, 256:], (zh + NY - zl) % NY, 0, keepdims=False
        )
        head_gain = lax.dynamic_index_in_dim(head_gain.reshape(2, 2, 1, DH), core, 1, keepdims=False)
        extended = jnp.concatenate(
            [
                tokens,
                pieces_of(sums[:128])[None],
                pieces_of(sums[128:])[None],
                ln_gain[None],
                jnp.zeros((13, 384), jnp.bfloat16),
            ]
        )

    with jax.named_scope("tokens"):
        extended, w_moved = lax.optimization_barrier((extended, w_moved))
        t0 = spread(extended, "zh", NZH)

    with jax.named_scope("weights"):
        along_x = [
            shift(w_moved, ("x",), lambda i, step=step: ((i[0] - step) % NX,)) for step in (1, 2, 3)
        ]
        t0, *along_x = lax.optimization_barrier((t0, *along_x))
        w_mine = jnp.stack([w_moved] + along_x)
        w_theirs = swap_cores(w_mine)

    with jax.named_scope("tokens"):
        t1 = along_z(t0, -1)
        t3 = along_z(t0, 1)
        t2 = along_z_two(t0)

    with jax.named_scope("project"):
        part = kernel_call(
            partial_kernel,
            jax.ShapeDtypeStruct((CORES, NY, 128, 3 * DH), jnp.bfloat16),
            (where, t0, t1, t2, t3, w_mine, w_theirs),
            scalars=1,
            scratch=[
                pltpu.VMEM((NX, 384, 768), jnp.bfloat16),
                pltpu.VMEM((512, 768), jnp.float32),
            ],
        )
        part = part.reshape(CORES * NY, 128, 3 * DH)
        part = lax.all_to_all(part, ("core", "y"), 0, 0).reshape(CORES, NY, 128, 3 * DH)
        q, kv = kernel_call(
            heads_kernel,
            (
                jax.ShapeDtypeStruct((256, DH), jnp.bfloat16),
                jax.ShapeDtypeStruct((NX * NY, 2, 256, DH), jnp.bfloat16),
            ),
            (part, head_gain),
        )

    with jax.named_scope("keys"):
        kv_all = lax.all_to_all(kv, ("x", "y"), 0, 0)

    with jax.named_scope("attend"):
        out = kernel_call(
            attend_kernel, jax.ShapeDtypeStruct((256, DH), jnp.bfloat16), (q, kv_all)
        )

    with jax.named_scope("home"):
        same = to_home(lax.dynamic_slice_in_dim(out, core * 128, 128), 0)
        cross = to_home(lax.dynamic_slice_in_dim(out, (1 - core) * 128, 128), 1)
        return jnp.where(
            core == 0,
            jnp.concatenate([same, cross], axis=1),
            jnp.concatenate([cross, same], axis=1),
        )


def solution(mesh):
    fine = Mesh(mesh.devices.reshape(SIZES), AXES)
    rows = ("x", "zh", "core")
    cols = ("zl", "y")
    in_specs = (P(rows, cols), P(cols), P(rows, None, cols), P(cols), P(cols))
    return jax.shard_map(body, mesh=fine, in_specs=in_specs, out_specs=P(rows, cols), check_vma=False)
```

```python
import numpy as np
import jax
import jax.numpy as jnp
from jax import lax
from jax.experimental import pallas as pl
from jax.experimental.pallas import tpu as pltpu
from jax.sharding import Mesh, PartitionSpec as P

DH = 128
EPSILON = 1e-06
FEATURES = 6144
NX = NZH = NZL = NY = 4
CORES = 2
AXES = ("x", "zh", "core", "zl", "y")
SIZES = (NX, NZH, CORES, NZL, NY)
VMEM_LIMIT = 28 * 1024 * 1024


def shift(values, axes, move):
    sizes = [SIZES[AXES.index(axis)] for axis in axes]
    pairs = [
        (int(np.ravel_multi_index(src, sizes)), int(np.ravel_multi_index(move(src), sizes)))
        for src in np.ndindex(*sizes)
    ]
    return lax.ppermute(values, axes, pairs)


def plane_offset(zl):
    return (0, 1, 0, 2)[zl]


def to_plane(values):
    return shift(
        values,
        ("zh", "zl", "y"),
        lambda i: ((i[2] + plane_offset(i[1])) % NZH, (i[1] + 2) % NZL, i[0]),
    )


def to_home(values, cross):
    def move(i):
        zh, core, zl, y = i
        zh_home, zl_home = divmod((zh * NZL + zl + 4 * ((y + zl) % 4) + 2) % 16, NZL)
        return zh_home, core ^ cross, zl_home, (zh - plane_offset(zl_home)) % NY

    return shift(values, ("zh", "core", "zl", "y"), move)


def along_z(values, step):
    return shift(values, ("zh", "zl"), lambda i: divmod((i[0] * NZL + i[1] + step) % 16, NZL))


def along_z_two(values):
    def move(i):
        step = 2 if i[1] % 2 == 0 else -2
        return divmod((i[0] * NZL + i[1] + step) % 16, NZL)

    return shift(values, ("zh", "zl"), move)


def swap_cores(values):
    return shift(values, ("core",), lambda i: (1 - i[0],))


def spread(values, axes, count):
    return lax.all_to_all(jnp.broadcast_to(values[None], (count,) + values.shape), axes, 0, 0)


def pieces_of(values):
    high = lax.reduce_precision(values, 8, 7)
    rest = values - high
    mid = lax.reduce_precision(rest, 8, 7)
    return jnp.concatenate([high, mid, rest - mid]).astype(jnp.bfloat16)


def partial_kernel(where, t0, t1, t2, t3, gain, w_mine, w_theirs, out, w, acc):
    zl, core, turn, x_here = where[0], where[1], where[2], where[3]
    half = w_mine.shape[2]
    for step in range(NX):
        x = lax.rem(x_here + step, NX)
        for s in range(3):
            cols = slice(s * 256, s * 256 + 256)
            w[x, pl.ds(pl.multiple_of(core * half, half), half), cols] = w_mine[step, s]
            w[x, pl.ds(pl.multiple_of((1 - core) * half, half), half), cols] = w_theirs[step, s]
    tokens = (t0, t1, t2, t3)

    centers, scales = [], []
    for quarter in range(NZH):
        rows = t0[quarter, 128:144].astype(jnp.float32)
        sums = (rows[:, :128] + rows[:, 128:256] + rows[:, 256:]) / FEATURES
        center = sums[0:1]
        centers.append(center)
        scales.append(lax.rsqrt(sums[1:2] - center * center + EPSILON))
    stats = jnp.concatenate(centers + scales, axis=0).T

    for slot in range(NZL):
        part = lax.rem(zl + slot, NZL)
        row_gain = gain[part]
        normed = []
        for quarter in range(NZH):
            x = tokens[slot][quarter, :128].astype(jnp.float32)
            center = stats[:, quarter : quarter + 1]
            scale = stats[:, NZH + quarter : NZH + quarter + 1]
            normed.append(((x - center) * scale * row_gain).astype(jnp.bfloat16))
        term = jnp.dot(
            jnp.concatenate(normed, axis=0),
            w[part],
            preferred_element_type=jnp.float32,
        )
        if slot == 0:
            acc[...] = term
        elif slot < NZL - 1:
            acc[...] += term
        else:
            total = acc[...] + term
            for quarter in range(NZH):
                rows = slice(quarter * 128, quarter * 128 + 128)
                for head in range(2):
                    for s in range(3):
                        cols = slice(s * 256 + head * DH, s * 256 + head * DH + DH)
                        out[head, lax.rem(turn + quarter, NZH), :, s * DH : s * DH + DH] = total[
                            rows, cols
                        ].astype(jnp.bfloat16)


def heads_kernel(part, head_gain, q_out, kv_out):
    def head_norm(values, row):
        mid = jnp.mean(values, axis=1, keepdims=True)
        var = jnp.mean(values * values, axis=1, keepdims=True) - mid * mid
        return ((values - mid) * lax.rsqrt(var + EPSILON) * row).astype(jnp.bfloat16)

    for source in range(2):
        rows = slice(source * 128, source * 128 + 128)
        acc = sum(part[source, y].astype(jnp.float32) for y in range(NY))
        q_out[rows] = head_norm(acc[:, :DH], head_gain[0])
        key = head_norm(acc[:, DH : 2 * DH], head_gain[1])
        value = acc[:, 2 * DH :].astype(jnp.bfloat16)
        for target in range(NX * NY):
            kv_out[target, 0, rows] = key
            kv_out[target, 1, rows] = value


def attend_kernel(q, kv, out):
    keys = kv[:, 0].reshape(-1, DH)
    values = kv[:, 1].reshape(-1, DH)
    scores = lax.dot_general(
        q[...], keys, (((1,), (1,)), ((), ())), preferred_element_type=jnp.float32
    ) * (DH ** -0.5)
    top = jnp.max(scores, axis=1, keepdims=True)
    weights = jnp.exp(scores - top)
    total = jnp.sum(weights, axis=1, keepdims=True)
    mixed = jnp.dot(weights.astype(jnp.bfloat16), values, preferred_element_type=jnp.float32)
    out[...] = (mixed / total).astype(jnp.bfloat16)


def kernel_call(kernel, out_shape, args, scalars=0, scratch=()):
    vmem = pl.BlockSpec(memory_space=pltpu.VMEM)
    smem = pl.BlockSpec(memory_space=pltpu.SMEM)
    return pl.pallas_call(
        kernel,
        out_shape=out_shape,
        in_specs=[smem] * scalars + [vmem] * (len(args) - scalars),
        out_specs=jax.tree.map(lambda _: vmem, out_shape),
        scratch_shapes=scratch,
        compiler_params=pltpu.CompilerParams(vmem_limit_bytes=VMEM_LIMIT),
    )(*args)


def body(tokens, ln_gain, w_qkv, q_gain, k_gain):
    core = lax.axis_index("core")
    zl = lax.axis_index("zl")
    zh = lax.axis_index("zh")
    y_here = lax.axis_index("y")
    head_zl = (zl + 2) % NZL
    head_y = (zh + NY - jnp.where(head_zl == 1, 1, jnp.where(head_zl == 3, 2, 0))) % NY
    turn = (3 * NZH - zh - zl - (zl >= 2)) % NZH
    where = jnp.stack([zl, core, turn, lax.axis_index("x")]).astype(jnp.int32)

    with jax.named_scope("weights"):
        w_moved = to_plane(jnp.transpose(w_qkv, (1, 0, 2)))

    with jax.named_scope("norm"):
        x = tokens.astype(jnp.float32)
        shared = spread(
            jnp.concatenate(
                [
                    jnp.sum(x, axis=1),
                    jnp.sum(x * x, axis=1),
                    ln_gain.astype(jnp.float32),
                    q_gain,
                    k_gain,
                ]
            )[None],
            ("zl", "y"),
            NZL * NY,
        )[:, 0]
        sums = jnp.sum(shared[:, :256], axis=0)
        extended = jnp.concatenate(
            [
                tokens,
                pieces_of(sums[:128])[None],
                pieces_of(sums[128:])[None],
                jnp.zeros((14, 384), jnp.bfloat16),
            ]
        )
        gain = lax.dynamic_index_in_dim(
            shared[:, 256:640].reshape(NZL, NY, 1, 384), y_here, 1, keepdims=False
        )
        head_gain = lax.dynamic_index_in_dim(
            shared[:, 640:], head_zl * NY + head_y, 0, keepdims=False
        )
        head_gain = lax.dynamic_index_in_dim(head_gain.reshape(2, 2, 1, DH), core, 1, keepdims=False)

    with jax.named_scope("tokens"):
        extended, w_moved = lax.optimization_barrier((extended, w_moved))
        t0 = spread(extended, "zh", NZH)

    with jax.named_scope("weights"):
        along_x = [
            shift(w_moved, ("x",), lambda i, step=step: ((i[0] - step) % NX,)) for step in (1, 2, 3)
        ]
        t0, *along_x = lax.optimization_barrier((t0, *along_x))

    with jax.named_scope("tokens"):
        block = t0[:, :128]
        t1 = along_z(block, -1)
        t3 = along_z(block, 1)
        t2 = along_z_two(block)

    with jax.named_scope("weights"):
        t3, *along_x = lax.optimization_barrier((t3, *along_x))
        w_mine = jnp.stack([w_moved] + along_x)
        w_theirs = swap_cores(w_mine)

    with jax.named_scope("project"):
        part = kernel_call(
            partial_kernel,
            jax.ShapeDtypeStruct((CORES, NY, 128, 3 * DH), jnp.bfloat16),
            (where, t0, t1, t2, t3, gain, w_mine, w_theirs),
            scalars=1,
            scratch=[
                pltpu.VMEM((NX, 384, 768), jnp.bfloat16),
                pltpu.VMEM((512, 768), jnp.float32),
            ],
        )
        part = part.reshape(CORES * NY, 128, 3 * DH)
        part = lax.all_to_all(part, ("core", "y"), 0, 0).reshape(CORES, NY, 128, 3 * DH)
        q, kv = kernel_call(
            heads_kernel,
            (
                jax.ShapeDtypeStruct((256, DH), jnp.bfloat16),
                jax.ShapeDtypeStruct((NX * NY, 2, 256, DH), jnp.bfloat16),
            ),
            (part, head_gain),
        )

    with jax.named_scope("keys"):
        kv_all = lax.all_to_all(kv, ("x", "y"), 0, 0)

    with jax.named_scope("attend"):
        out = kernel_call(
            attend_kernel, jax.ShapeDtypeStruct((256, DH), jnp.bfloat16), (q, kv_all)
        )

    with jax.named_scope("home"):
        same = to_home(lax.dynamic_slice_in_dim(out, core * 128, 128), 0)
        cross = to_home(lax.dynamic_slice_in_dim(out, (1 - core) * 128, 128), 1)
        return jnp.where(
            core == 0,
            jnp.concatenate([same, cross], axis=1),
            jnp.concatenate([cross, same], axis=1),
        )


def solution(mesh):
    fine = Mesh(mesh.devices.reshape(SIZES), AXES)
    rows = ("x", "zh", "core")
    cols = ("zl", "y")
    in_specs = (P(rows, cols), P(cols), P(rows, None, cols), P(cols), P(cols))
    return jax.shard_map(body, mesh=fine, in_specs=in_specs, out_specs=P(rows, cols), check_vma=False)
```

```python
import numpy as np
import jax
import jax.numpy as jnp
from jax import lax
from jax.experimental import pallas as pl
from jax.experimental.pallas import tpu as pltpu
from jax.sharding import Mesh, PartitionSpec as P

DH = 128
EPSILON = 1e-06
FEATURES = 6144
NX = NZH = NZL = NY = 4
CORES = 2
AXES = ("x", "zh", "core", "zl", "yh", "yl")
SIZES = (NX, NZH, CORES, NZL, 2, 2)
Y = ("yh", "yl")
VMEM_LIMIT = 28 * 1024 * 1024


def shift(values, axes, move):
    sizes = [SIZES[AXES.index(axis)] for axis in axes]
    pairs = [
        (int(np.ravel_multi_index(src, sizes)), int(np.ravel_multi_index(move(src), sizes)))
        for src in np.ndindex(*sizes)
    ]
    return lax.ppermute(values, axes, pairs)


def to_plane(values):
    def move(i):
        zh, zl, yh, yl = i
        return ((yh * 2 + yl + zl) % NZH, zl) + divmod(zh, 2)

    return shift(values, ("zh", "zl") + Y, move)


def to_home(values, cross):
    def move(i):
        zh, core, zl, yh, yl = i
        zh_home = (zh + zl + yh * 2 + yl + 2 * core) % NZH
        return (zh_home, core ^ cross, zl) + divmod((zh - zl) % NY, 2)

    return shift(values, ("zh", "core", "zl") + Y, move)


def along_z(values, step):
    return shift(values, ("zh", "zl"), lambda i: divmod((i[0] * NZL + i[1] + step) % 16, NZL))


def along_z_two(values):
    def move(i):
        step = 2 if i[1] % 2 == 0 else -2
        return divmod((i[0] * NZL + i[1] + step) % 16, NZL)

    return shift(values, ("zh", "zl"), move)


def swap_cores(values):
    return shift(values, ("core",), lambda i: (1 - i[0],))


def spread(values, axes, count):
    return lax.all_to_all(jnp.broadcast_to(values[None], (count,) + values.shape), axes, 0, 0)


def pieces_of(values):
    high = lax.reduce_precision(values, 8, 7)
    rest = values - high
    mid = lax.reduce_precision(rest, 8, 7)
    return jnp.concatenate([high, mid, rest - mid]).astype(jnp.bfloat16)


def partial_kernel(where, t0, t1, t2, t3, w_mine, w_theirs, out, w, acc):
    zl, core, turn, x_here = where[0], where[1], where[2], where[3]
    half = w_mine.shape[2]
    for step in range(NX):
        x = lax.rem(x_here + step, NX)
        for s in range(3):
            cols = slice(s * 256, s * 256 + 256)
            w[x, pl.ds(pl.multiple_of(core * half, half), half), cols] = w_mine[step, s]
            w[x, pl.ds(pl.multiple_of((1 - core) * half, half), half), cols] = w_theirs[step, s]
    tokens = (t0, t1, t2, t3)

    def extra(slot, quarter):
        return tokens[slot][quarter, 128:144].astype(jnp.float32)

    centers, scales = [], []
    for quarter in range(NZH):
        rows = sum(extra(slot, quarter)[:2] for slot in range(NZL))
        sums = (rows[:, :128] + rows[:, 128:256] + rows[:, 256:]) / FEATURES
        center = sums[0:1]
        centers.append(center)
        scales.append(lax.rsqrt(sums[1:2] - center * center + EPSILON))
    stats = jnp.concatenate(centers + scales, axis=0).T

    for slot in range(NZL):
        row_gain = extra(slot, 0)[2:3]
        normed = []
        for quarter in range(NZH):
            x = tokens[slot][quarter, :128].astype(jnp.float32)
            center = stats[:, quarter : quarter + 1]
            scale = stats[:, NZH + quarter : NZH + quarter + 1]
            normed.append(((x - center) * scale * row_gain).astype(jnp.bfloat16))
        term = jnp.dot(
            jnp.concatenate(normed, axis=0),
            w[lax.rem(zl + slot, NZL)],
            preferred_element_type=jnp.float32,
        )
        if slot == 0:
            acc[...] = term
        else:
            acc[...] += term
    for core_to in range(CORES):
        for y_to in range(NY):
            quarter = lax.rem(turn + y_to + 2 * core_to, NZH)
            rows = pl.ds(pl.multiple_of(quarter * 128, 128), 128)
            head = y_to // 2
            for s in range(3):
                cols = slice(s * 256 + head * DH, s * 256 + head * DH + DH)
                out[core_to, y_to, :, s * DH : s * DH + DH] = acc[rows, cols].astype(jnp.bfloat16)


def heads_kernel(part, head_gain, q_out, kv_out):
    def head_norm(values, row):
        mid = jnp.mean(values, axis=1, keepdims=True)
        var = jnp.mean(values * values, axis=1, keepdims=True) - mid * mid
        return ((values - mid) * lax.rsqrt(var + EPSILON) * row).astype(jnp.bfloat16)

    for source in range(2):
        rows = slice(source * 128, source * 128 + 128)
        acc = sum(part[source, y].astype(jnp.float32) for y in range(NY))
        q_out[rows] = head_norm(acc[:, :DH], head_gain[0])
        key = head_norm(acc[:, DH : 2 * DH], head_gain[1])
        value = acc[:, 2 * DH :].astype(jnp.bfloat16)
        for target in range(NX * 2):
            kv_out[target, 0, rows] = key
            kv_out[target, 1, rows] = value


def attend_kernel(q, kv_mine, kv_theirs, out):
    scores = [
        lax.dot_general(
            q[...],
            kv[:, 0].reshape(-1, DH),
            (((1,), (1,)), ((), ())),
            preferred_element_type=jnp.float32,
        )
        * (DH ** -0.5)
        for kv in (kv_mine, kv_theirs)
    ]
    top = jnp.maximum(*[jnp.max(part, axis=1, keepdims=True) for part in scores])
    weights = [jnp.exp(part - top) for part in scores]
    total = sum(jnp.sum(part, axis=1, keepdims=True) for part in weights)
    mixed = sum(
        jnp.dot(
            part.astype(jnp.bfloat16), kv[:, 1].reshape(-1, DH), preferred_element_type=jnp.float32
        )
        for part, kv in zip(weights, (kv_mine, kv_theirs))
    )
    out[...] = (mixed / total).astype(jnp.bfloat16)


def kernel_call(kernel, out_shape, args, scalars=0, scratch=()):
    vmem = pl.BlockSpec(memory_space=pltpu.VMEM)
    smem = pl.BlockSpec(memory_space=pltpu.SMEM)
    return pl.pallas_call(
        kernel,
        out_shape=out_shape,
        in_specs=[smem] * scalars + [vmem] * (len(args) - scalars),
        out_specs=jax.tree.map(lambda _: vmem, out_shape),
        scratch_shapes=scratch,
        compiler_params=pltpu.CompilerParams(vmem_limit_bytes=VMEM_LIMIT),
    )(*args)


def body(tokens, ln_gain, w_qkv, q_gain, k_gain):
    core = lax.axis_index("core")
    zl = lax.axis_index("zl")
    zh = lax.axis_index("zh")
    y_high = lax.axis_index("yh")
    y_here = y_high * 2 + lax.axis_index("yl")
    turn = (zh + zl) % NZH
    where = jnp.stack([zl, core, turn, lax.axis_index("x")]).astype(jnp.int32)

    with jax.named_scope("weights"):
        w_moved = to_plane(jnp.transpose(w_qkv, (1, 0, 2)))

    with jax.named_scope("norm"):
        x = tokens.astype(jnp.float32)
        shared = spread(
            jnp.concatenate([jnp.sum(x, axis=1), jnp.sum(x * x, axis=1), q_gain, k_gain])[None],
            Y,
            NY,
        )[:, 0]
        sums = jnp.sum(shared[:, :256], axis=0)
        head_gain = lax.dynamic_index_in_dim(
            shared[:, 256:], (zh + NY - zl) % NY, 0, keepdims=False
        )
        head_gain = lax.dynamic_index_in_dim(
            head_gain.reshape(2, 2, 1, DH), y_high, 1, keepdims=False
        )
        extended = jnp.concatenate(
            [
                tokens,
                pieces_of(sums[:128])[None],
                pieces_of(sums[128:])[None],
                ln_gain[None],
                jnp.zeros((13, 384), jnp.bfloat16),
            ]
        )

    with jax.named_scope("tokens"):
        extended, w_moved = lax.optimization_barrier((extended, w_moved))
        t0 = spread(extended, "zh", NZH)

    with jax.named_scope("weights"):
        along_x = [
            shift(w_moved, ("x",), lambda i, step=step: ((i[0] - step) % NX,)) for step in (1, 2, 3)
        ]
        w_mine = jnp.stack([w_moved] + along_x)
        w_theirs = swap_cores(w_mine)
        t0, w_mine, w_theirs = lax.optimization_barrier((t0, w_mine, w_theirs))

    with jax.named_scope("tokens"):
        t1 = along_z(t0, -1)
        t3 = along_z(t0, 1)
        t2 = along_z_two(t0)

    with jax.named_scope("project"):
        part = kernel_call(
            partial_kernel,
            jax.ShapeDtypeStruct((CORES, NY, 128, 3 * DH), jnp.bfloat16),
            (where, t0, t1, t2, t3, w_mine, w_theirs),
            scalars=1,
            scratch=[
                pltpu.VMEM((NX, 384, 768), jnp.bfloat16),
                pltpu.VMEM((512, 768), jnp.float32),
            ],
        )
        part = part.reshape(CORES * NY, 128, 3 * DH)
        part = lax.all_to_all(part, ("core",) + Y, 0, 0).reshape(CORES, NY, 128, 3 * DH)
        q, kv = kernel_call(
            heads_kernel,
            (
                jax.ShapeDtypeStruct((256, DH), jnp.bfloat16),
                jax.ShapeDtypeStruct((NX * 2, 2, 256, DH), jnp.bfloat16),
            ),
            (part, head_gain),
        )

    with jax.named_scope("keys"):
        kv_mine = lax.all_to_all(kv, ("x", "yl"), 0, 0)
        kv_theirs = swap_cores(kv_mine)

    with jax.named_scope("attend"):
        out = kernel_call(
            attend_kernel, jax.ShapeDtypeStruct((256, DH), jnp.bfloat16), (q, kv_mine, kv_theirs)
        )

    with jax.named_scope("home"):
        same = to_home(lax.dynamic_slice_in_dim(out, core * 128, 128), 0)
        cross = to_home(lax.dynamic_slice_in_dim(out, (1 - core) * 128, 128), 1)
        first = (zh + 3 * NY - y_here - 2 * zl - 2 * core) % NY < 2
        return jnp.where(
            first,
            jnp.concatenate([same, cross], axis=1),
            jnp.concatenate([cross, same], axis=1),
        )


def solution(mesh):
    fine = Mesh(mesh.devices.reshape(SIZES), AXES)
    rows = ("x", "zh", "core")
    cols = ("zl",) + Y
    in_specs = (P(rows, cols), P(cols), P(rows, None, cols), P(cols), P(cols))
    return jax.shard_map(body, mesh=fine, in_specs=in_specs, out_specs=P(rows, cols), check_vma=False)
```

```python
import numpy as np
import jax
import jax.numpy as jnp
from jax import lax
from jax.experimental import pallas as pl
from jax.experimental.pallas import tpu as pltpu
from jax.sharding import Mesh, PartitionSpec as P

DH = 128
EPSILON = 1e-06
FEATURES = 6144
NX = NZH = NZL = NY = 4
CORES = 2
AXES = ("x", "zh", "core", "zl", "yh", "yl")
SIZES = (NX, NZH, CORES, NZL, 2, 2)
Y = ("yh", "yl")
VMEM_LIMIT = 28 * 1024 * 1024


def shift(values, axes, move):
    sizes = [SIZES[AXES.index(axis)] for axis in axes]
    pairs = [
        (int(np.ravel_multi_index(src, sizes)), int(np.ravel_multi_index(move(src), sizes)))
        for src in np.ndindex(*sizes)
    ]
    return lax.ppermute(values, axes, pairs)


def to_plane(values):
    def move(i):
        zh, zl, yh, yl = i
        return ((yh * 2 + yl + zl) % NZH, zl) + divmod(zh, 2)

    return shift(values, ("zh", "zl") + Y, move)


def to_home(values):
    def move(i):
        zh, core, zl, yh, yl = i
        zh_home = (zh + zl + yh * 2 + yl + 2 * core) % NZH
        return (zh_home, core, zl) + divmod((zh - zl) % NY, 2)

    return shift(values, ("zh", "core", "zl") + Y, move)


def along_z(values, step):
    return shift(values, ("zh", "zl"), lambda i: divmod((i[0] * NZL + i[1] + step) % 16, NZL))


def along_z_two(values):
    def move(i):
        step = 2 if i[1] % 2 == 0 else -2
        return divmod((i[0] * NZL + i[1] + step) % 16, NZL)

    return shift(values, ("zh", "zl"), move)


def swap_cores(values):
    return shift(values, ("core",), lambda i: (1 - i[0],))


def spread(values, axes, count):
    return lax.all_to_all(jnp.broadcast_to(values[None], (count,) + values.shape), axes, 0, 0)


def pieces_of(values):
    high = lax.reduce_precision(values, 8, 7)
    rest = values - high
    mid = lax.reduce_precision(rest, 8, 7)
    return jnp.concatenate([high, mid, rest - mid]).astype(jnp.bfloat16)


def partial_kernel(where, t0, t1, t2, t3, w_mine, w_theirs, out, w, acc):
    zl, core, turn, x_here = where[0], where[1], where[2], where[3]
    half = w_mine.shape[2]
    for step in range(NX):
        x = lax.rem(x_here + step, NX)
        for s in range(3):
            cols = slice(s * 256, s * 256 + 256)
            w[x, pl.ds(pl.multiple_of(core * half, half), half), cols] = w_mine[step, s]
            w[x, pl.ds(pl.multiple_of((1 - core) * half, half), half), cols] = w_theirs[step, s]
    tokens = (t0, t1, t2, t3)

    def extra(slot, quarter):
        return tokens[slot][quarter, 128:144].astype(jnp.float32)

    centers, scales = [], []
    for quarter in range(NZH):
        rows = sum(extra(slot, quarter)[:2] for slot in range(NZL))
        sums = (rows[:, :128] + rows[:, 128:256] + rows[:, 256:]) / FEATURES
        center = sums[0:1]
        centers.append(center)
        scales.append(lax.rsqrt(sums[1:2] - center * center + EPSILON))
    stats = jnp.concatenate(centers + scales, axis=0).T

    for slot in range(NZL):
        row_gain = extra(slot, 0)[2:3]
        normed = []
        for quarter in range(NZH):
            x = tokens[slot][quarter, :128].astype(jnp.float32)
            center = stats[:, quarter : quarter + 1]
            scale = stats[:, NZH + quarter : NZH + quarter + 1]
            normed.append(((x - center) * scale * row_gain).astype(jnp.bfloat16))
        term = jnp.dot(
            jnp.concatenate(normed, axis=0),
            w[lax.rem(zl + slot, NZL)],
            preferred_element_type=jnp.float32,
        )
        if slot == 0:
            acc[...] = term
        else:
            acc[...] += term
    for core_to in range(CORES):
        for y_to in range(NY):
            quarter = lax.rem(turn + y_to + 2 * core_to, NZH)
            rows = pl.ds(pl.multiple_of(quarter * 128, 128), 128)
            head = y_to // 2
            for s in range(3):
                cols = slice(s * 256 + head * DH, s * 256 + head * DH + DH)
                out[core_to, y_to, :, s * DH : s * DH + DH] = acc[rows, cols].astype(jnp.bfloat16)


def heads_kernel(part, head_gain, q_out, kv_out):
    def head_norm(values, row):
        mid = jnp.mean(values, axis=1, keepdims=True)
        var = jnp.mean(values * values, axis=1, keepdims=True) - mid * mid
        return ((values - mid) * lax.rsqrt(var + EPSILON) * row).astype(jnp.bfloat16)

    for source in range(2):
        rows = slice(source * 128, source * 128 + 128)
        acc = sum(part[source, y].astype(jnp.float32) for y in range(NY))
        q_out[rows] = head_norm(acc[:, :DH], head_gain[0])
        key = head_norm(acc[:, DH : 2 * DH], head_gain[1])
        value = acc[:, 2 * DH :].astype(jnp.bfloat16)
        for target in range(NX * 2):
            kv_out[target, 0, rows] = key
            kv_out[target, 1, rows] = value


def attend_kernel(q, kv_mine, kv_theirs, out):
    scores = [
        lax.dot_general(
            q[...],
            kv[:, 0].reshape(-1, DH),
            (((1,), (1,)), ((), ())),
            preferred_element_type=jnp.float32,
        )
        * (DH ** -0.5)
        for kv in (kv_mine, kv_theirs)
    ]
    top = jnp.maximum(*[jnp.max(part, axis=1, keepdims=True) for part in scores])
    weights = [jnp.exp(part - top) for part in scores]
    total = sum(jnp.sum(part, axis=1, keepdims=True) for part in weights)
    mixed = sum(
        jnp.dot(
            part.astype(jnp.bfloat16), kv[:, 1].reshape(-1, DH), preferred_element_type=jnp.float32
        )
        for part, kv in zip(weights, (kv_mine, kv_theirs))
    )
    out[...] = (mixed / total).astype(jnp.bfloat16)


def kernel_call(kernel, out_shape, args, scalars=0, scratch=()):
    vmem = pl.BlockSpec(memory_space=pltpu.VMEM)
    smem = pl.BlockSpec(memory_space=pltpu.SMEM)
    return pl.pallas_call(
        kernel,
        out_shape=out_shape,
        in_specs=[smem] * scalars + [vmem] * (len(args) - scalars),
        out_specs=jax.tree.map(lambda _: vmem, out_shape),
        scratch_shapes=scratch,
        compiler_params=pltpu.CompilerParams(vmem_limit_bytes=VMEM_LIMIT),
    )(*args)


def body(tokens, ln_gain, w_qkv, q_gain, k_gain):
    core = lax.axis_index("core")
    zl = lax.axis_index("zl")
    zh = lax.axis_index("zh")
    y_high = lax.axis_index("yh")
    y_here = y_high * 2 + lax.axis_index("yl")
    turn = (zh + zl) % NZH
    where = jnp.stack([zl, core, turn, lax.axis_index("x")]).astype(jnp.int32)

    with jax.named_scope("weights"):
        w_moved = to_plane(jnp.transpose(w_qkv, (1, 0, 2)))

    with jax.named_scope("norm"):
        x = tokens.astype(jnp.float32)
        shared = spread(
            jnp.concatenate([jnp.sum(x, axis=1), jnp.sum(x * x, axis=1), q_gain, k_gain])[None],
            Y,
            NY,
        )[:, 0]
        sums = jnp.sum(shared[:, :256], axis=0)
        head_gain = lax.dynamic_index_in_dim(
            shared[:, 256:], (zh + NY - zl) % NY, 0, keepdims=False
        )
        head_gain = lax.dynamic_index_in_dim(
            head_gain.reshape(2, 2, 1, DH), y_high, 1, keepdims=False
        )
        extended = jnp.concatenate(
            [
                tokens,
                pieces_of(sums[:128])[None],
                pieces_of(sums[128:])[None],
                ln_gain[None],
                jnp.zeros((13, 384), jnp.bfloat16),
            ]
        )

    with jax.named_scope("tokens"):
        extended, w_moved = lax.optimization_barrier((extended, w_moved))
        t0 = spread(extended, "zh", NZH)

    with jax.named_scope("weights"):
        along_x = [
            shift(w_moved, ("x",), lambda i, step=step: ((i[0] - step) % NX,)) for step in (1, 2, 3)
        ]
        t0, *along_x = lax.optimization_barrier((t0, *along_x))
        w_mine = jnp.stack([w_moved] + along_x)
        w_theirs = swap_cores(w_mine)

    with jax.named_scope("tokens"):
        t1 = along_z(t0, -1)
        t3 = along_z(t0, 1)
        t2 = along_z_two(t0)

    with jax.named_scope("project"):
        part = kernel_call(
            partial_kernel,
            jax.ShapeDtypeStruct((CORES, NY, 128, 3 * DH), jnp.bfloat16),
            (where, t0, t1, t2, t3, w_mine, w_theirs),
            scalars=1,
            scratch=[
                pltpu.VMEM((NX, 384, 768), jnp.bfloat16),
                pltpu.VMEM((512, 768), jnp.float32),
            ],
        )
        part = part.reshape(CORES * NY, 128, 3 * DH)
        part = lax.all_to_all(part, ("core",) + Y, 0, 0).reshape(CORES, NY, 128, 3 * DH)
        q, kv = kernel_call(
            heads_kernel,
            (
                jax.ShapeDtypeStruct((256, DH), jnp.bfloat16),
                jax.ShapeDtypeStruct((NX * 2, 2, 256, DH), jnp.bfloat16),
            ),
            (part, head_gain),
        )

    with jax.named_scope("keys"):
        kv_mine = lax.all_to_all(kv, ("x", "yl"), 0, 0)
        kv_theirs = swap_cores(kv_mine)

    with jax.named_scope("attend"):
        out = kernel_call(
            attend_kernel, jax.ShapeDtypeStruct((256, DH), jnp.bfloat16), (q, kv_mine, kv_theirs)
        )

    with jax.named_scope("home"):
        arrived = to_home(out)
        same = lax.dynamic_slice_in_dim(arrived, core * 128, 128)
        cross = swap_cores(lax.dynamic_slice_in_dim(arrived, (1 - core) * 128, 128))
        first = (zh + 3 * NY - y_here - 2 * zl - 2 * core) % NY < 2
        return jnp.where(
            first,
            jnp.concatenate([same, cross], axis=1),
            jnp.concatenate([cross, same], axis=1),
        )


def solution(mesh):
    fine = Mesh(mesh.devices.reshape(SIZES), AXES)
    rows = ("x", "zh", "core")
    cols = ("zl",) + Y
    in_specs = (P(rows, cols), P(cols), P(rows, None, cols), P(cols), P(cols))
    return jax.shard_map(body, mesh=fine, in_specs=in_specs, out_specs=P(rows, cols), check_vma=False)
```

```python
import numpy as np
import jax
import jax.numpy as jnp
from jax import lax
from jax.experimental import pallas as pl
from jax.experimental.pallas import tpu as pltpu
from jax.sharding import Mesh, PartitionSpec as P

DH = 128
EPSILON = 1e-06
FEATURES = 6144
NX = NZH = NZL = NY = 4
CORES = 2
AXES = ("x", "zh", "core", "zl", "yh", "yl")
SIZES = (NX, NZH, CORES, NZL, 2, 2)
Y = ("yh", "yl")
VMEM_LIMIT = 28 * 1024 * 1024


def shift(values, axes, move):
    sizes = [SIZES[AXES.index(axis)] for axis in axes]
    pairs = [
        (int(np.ravel_multi_index(src, sizes)), int(np.ravel_multi_index(move(src), sizes)))
        for src in np.ndindex(*sizes)
    ]
    return lax.ppermute(values, axes, pairs)


def plane_turn(zl):
    return (0, 1, 0, 2)[zl]


def to_plane(values):
    def move(i):
        zh, zl, yh, yl = i
        return ((yh * 2 + yl + plane_turn(zl)) % NZH, (zl + 2) % NZL) + divmod(zh, 2)

    return shift(values, ("zh", "zl") + Y, move)


def to_home(values):
    def move(i):
        zh, core, zl, yh, yl = i
        step = 4 * ((yh * 2 + yl + 2 * core + zl) % 4) + 2
        zh_home, zl_home = divmod((zh * NZL + zl + step) % 16, NZL)
        return (zh_home, core, zl_home) + divmod((zh - plane_turn(zl_home)) % NY, 2)

    return shift(values, ("zh", "core", "zl") + Y, move)


def along_z(values, step):
    return shift(values, ("zh", "zl"), lambda i: divmod((i[0] * NZL + i[1] + step) % 16, NZL))


def along_z_two(values):
    def move(i):
        step = 2 if i[1] % 2 == 0 else -2
        return divmod((i[0] * NZL + i[1] + step) % 16, NZL)

    return shift(values, ("zh", "zl"), move)


def swap_cores(values):
    return shift(values, ("core",), lambda i: (1 - i[0],))


def spread(values, axes, count):
    return lax.all_to_all(jnp.broadcast_to(values[None], (count,) + values.shape), axes, 0, 0)


def pieces_of(values):
    high = lax.reduce_precision(values, 8, 7)
    rest = values - high
    mid = lax.reduce_precision(rest, 8, 7)
    return jnp.concatenate([high, mid, rest - mid]).astype(jnp.bfloat16)


def partial_kernel(where, t0, t1, t2, t3, w_mine, w_theirs, out, w, acc):
    zl, core, turn, x_here = where[0], where[1], where[2], where[3]
    half = w_mine.shape[2]
    for step in range(NX):
        x = lax.rem(x_here + step, NX)
        for s in range(3):
            cols = slice(s * 256, s * 256 + 256)
            w[x, pl.ds(pl.multiple_of(core * half, half), half), cols] = w_mine[step, s]
            w[x, pl.ds(pl.multiple_of((1 - core) * half, half), half), cols] = w_theirs[step, s]
    tokens = (t0, t1, t2, t3)

    def extra(slot, quarter):
        return tokens[slot][quarter, 128:144].astype(jnp.float32)

    centers, scales = [], []
    for quarter in range(NZH):
        rows = sum(extra(slot, quarter)[:2] for slot in range(NZL))
        sums = (rows[:, :128] + rows[:, 128:256] + rows[:, 256:]) / FEATURES
        center = sums[0:1]
        centers.append(center)
        scales.append(lax.rsqrt(sums[1:2] - center * center + EPSILON))
    stats = jnp.concatenate(centers + scales, axis=0).T

    for slot in range(NZL):
        row_gain = extra(slot, 0)[2:3]
        normed = []
        for quarter in range(NZH):
            x = tokens[slot][quarter, :128].astype(jnp.float32)
            center = stats[:, quarter : quarter + 1]
            scale = stats[:, NZH + quarter : NZH + quarter + 1]
            normed.append(((x - center) * scale * row_gain).astype(jnp.bfloat16))
        term = jnp.dot(
            jnp.concatenate(normed, axis=0),
            w[lax.rem(zl + slot, NZL)],
            preferred_element_type=jnp.float32,
        )
        if slot == 0:
            acc[...] = term
        else:
            acc[...] += term
    for core_to in range(CORES):
        for y_to in range(NY):
            quarter = lax.rem(turn + y_to + 2 * core_to, NZH)
            rows = pl.ds(pl.multiple_of(quarter * 128, 128), 128)
            head = y_to // 2
            for s in range(3):
                cols = slice(s * 256 + head * DH, s * 256 + head * DH + DH)
                out[core_to, y_to, :, s * DH : s * DH + DH] = acc[rows, cols].astype(jnp.bfloat16)


def heads_kernel(part, head_gain, q_out, kv_out):
    def head_norm(values, row):
        mid = jnp.mean(values, axis=1, keepdims=True)
        var = jnp.mean(values * values, axis=1, keepdims=True) - mid * mid
        return ((values - mid) * lax.rsqrt(var + EPSILON) * row).astype(jnp.bfloat16)

    for source in range(2):
        rows = slice(source * 128, source * 128 + 128)
        acc = sum(part[source, y].astype(jnp.float32) for y in range(NY))
        q_out[rows] = head_norm(acc[:, :DH], head_gain[0])
        key = head_norm(acc[:, DH : 2 * DH], head_gain[1])
        value = acc[:, 2 * DH :].astype(jnp.bfloat16)
        for target in range(NX * 2):
            kv_out[target, 0, rows] = key
            kv_out[target, 1, rows] = value


def attend_kernel(q, kv_mine, kv_theirs, out):
    scores = [
        lax.dot_general(
            q[...],
            kv[:, 0].reshape(-1, DH),
            (((1,), (1,)), ((), ())),
            preferred_element_type=jnp.float32,
        )
        * (DH ** -0.5)
        for kv in (kv_mine, kv_theirs)
    ]
    top = jnp.maximum(*[jnp.max(part, axis=1, keepdims=True) for part in scores])
    weights = [jnp.exp(part - top) for part in scores]
    total = sum(jnp.sum(part, axis=1, keepdims=True) for part in weights)
    mixed = sum(
        jnp.dot(
            part.astype(jnp.bfloat16), kv[:, 1].reshape(-1, DH), preferred_element_type=jnp.float32
        )
        for part, kv in zip(weights, (kv_mine, kv_theirs))
    )
    out[...] = (mixed / total).astype(jnp.bfloat16)


def kernel_call(kernel, out_shape, args, scalars=0, scratch=()):
    vmem = pl.BlockSpec(memory_space=pltpu.VMEM)
    smem = pl.BlockSpec(memory_space=pltpu.SMEM)
    return pl.pallas_call(
        kernel,
        out_shape=out_shape,
        in_specs=[smem] * scalars + [vmem] * (len(args) - scalars),
        out_specs=jax.tree.map(lambda _: vmem, out_shape),
        scratch_shapes=scratch,
        compiler_params=pltpu.CompilerParams(vmem_limit_bytes=VMEM_LIMIT),
    )(*args)


def body(tokens, ln_gain, w_qkv, q_gain, k_gain):
    core = lax.axis_index("core")
    zl = lax.axis_index("zl")
    zh = lax.axis_index("zh")
    y_high = lax.axis_index("yh")
    y_here = y_high * 2 + lax.axis_index("yl")
    turn = (zh + zl + (zl >= 2)) % NZH
    where = jnp.stack([zl, core, turn, lax.axis_index("x")]).astype(jnp.int32)

    with jax.named_scope("weights"):
        w_moved = to_plane(jnp.transpose(w_qkv, (1, 0, 2)))
        head_gain = to_plane(jnp.concatenate([q_gain, k_gain]).reshape(2, 2, 1, DH))
        head_gain = lax.dynamic_index_in_dim(head_gain, y_high, 1, keepdims=False)

    with jax.named_scope("norm"):
        x = tokens.astype(jnp.float32)
        shared = spread(
            jnp.concatenate([jnp.sum(x, axis=1), jnp.sum(x * x, axis=1)])[None], Y, NY
        )
        sums = jnp.sum(shared[:, 0], axis=0)
        extended = jnp.concatenate(
            [
                tokens,
                pieces_of(sums[:128])[None],
                pieces_of(sums[128:])[None],
                ln_gain[None],
                jnp.zeros((13, 384), jnp.bfloat16),
            ]
        )

    with jax.named_scope("tokens"):
        extended, w_moved = lax.optimization_barrier((extended, w_moved))
        t0 = spread(extended, "zh", NZH)

    with jax.named_scope("weights"):
        along_x = [
            shift(w_moved, ("x",), lambda i, step=step: ((i[0] - step) % NX,)) for step in (1, 2, 3)
        ]
        t0, *along_x = lax.optimization_barrier((t0, *along_x))
        w_mine = jnp.stack([w_moved] + along_x)
        w_theirs = swap_cores(w_mine)

    with jax.named_scope("tokens"):
        t1 = along_z(t0, -1)
        t3 = along_z(t0, 1)
        t2 = along_z_two(t0)

    with jax.named_scope("project"):
        part = kernel_call(
            partial_kernel,
            jax.ShapeDtypeStruct((CORES, NY, 128, 3 * DH), jnp.bfloat16),
            (where, t0, t1, t2, t3, w_mine, w_theirs),
            scalars=1,
            scratch=[
                pltpu.VMEM((NX, 384, 768), jnp.bfloat16),
                pltpu.VMEM((512, 768), jnp.float32),
            ],
        )
        part = part.reshape(CORES * NY, 128, 3 * DH)
        part = lax.all_to_all(part, ("core",) + Y, 0, 0).reshape(CORES, NY, 128, 3 * DH)
        q, kv = kernel_call(
            heads_kernel,
            (
                jax.ShapeDtypeStruct((256, DH), jnp.bfloat16),
                jax.ShapeDtypeStruct((NX * 2, 2, 256, DH), jnp.bfloat16),
            ),
            (part, head_gain),
        )

    with jax.named_scope("keys"):
        kv_mine = lax.all_to_all(kv, ("x", "yl"), 0, 0)
        kv_theirs = swap_cores(kv_mine)

    with jax.named_scope("attend"):
        out = kernel_call(
            attend_kernel, jax.ShapeDtypeStruct((256, DH), jnp.bfloat16), (q, kv_mine, kv_theirs)
        )

    with jax.named_scope("home"):
        arrived = to_home(out)
        same = lax.dynamic_slice_in_dim(arrived, core * 128, 128)
        cross = swap_cores(lax.dynamic_slice_in_dim(arrived, (1 - core) * 128, 128))
        zl_from = (zl + 2) % NZL
        zh_from = y_here + jnp.where(zl == 1, 1, jnp.where(zl == 3, 2, 0))
        y_from = zh + 4 * NY - zh_from - zl_from - (zl_from >= 2) - 2 * core
        first = y_from % NY < 2
        return jnp.where(
            first,
            jnp.concatenate([same, cross], axis=1),
            jnp.concatenate([cross, same], axis=1),
        )


def solution(mesh):
    fine = Mesh(mesh.devices.reshape(SIZES), AXES)
    rows = ("x", "zh", "core")
    cols = ("zl",) + Y
    in_specs = (P(rows, cols), P(cols), P(rows, None, cols), P(cols), P(cols))
    return jax.shard_map(body, mesh=fine, in_specs=in_specs, out_specs=P(rows, cols), check_vma=False)
```

```python
import numpy as np
import jax
import jax.numpy as jnp
from jax import lax
from jax.experimental import pallas as pl
from jax.experimental.pallas import tpu as pltpu
from jax.sharding import Mesh, PartitionSpec as P

DH = 128
EPSILON = 1e-06
FEATURES = 6144
SUMS_FLOPS = 20_000_000_000
NX = NZH = NZL = NY = 4
CORES = 2
AXES = ("x", "zh", "core", "zl", "yh", "yl")
SIZES = (NX, NZH, CORES, NZL, 2, 2)
Y = ("yh", "yl")
VMEM_LIMIT = 28 * 1024 * 1024


def shift(values, axes, move):
    sizes = [SIZES[AXES.index(axis)] for axis in axes]
    pairs = [
        (int(np.ravel_multi_index(src, sizes)), int(np.ravel_multi_index(move(src), sizes)))
        for src in np.ndindex(*sizes)
    ]
    return lax.ppermute(values, axes, pairs)


def to_plane(values):
    def move(i):
        zh, zl, yh, yl = i
        return ((yh * 2 + yl + zl) % NZH, zl) + divmod(zh, 2)

    return shift(values, ("zh", "zl") + Y, move)


def to_home(values):
    def move(i):
        zh, core, zl, yh, yl = i
        zh_home = (zh + zl + yh * 2 + yl + 2 * core) % NZH
        return (zh_home, core, zl) + divmod((zh - zl) % NY, 2)

    return shift(values, ("zh", "core", "zl") + Y, move)


def along_z(values, step):
    return shift(values, ("zh", "zl"), lambda i: divmod((i[0] * NZL + i[1] + step) % 16, NZL))


def along_z_two(values):
    def move(i):
        step = 2 if i[1] % 2 == 0 else -2
        return divmod((i[0] * NZL + i[1] + step) % 16, NZL)

    return shift(values, ("zh", "zl"), move)


def swap_cores(values):
    return shift(values, ("core",), lambda i: (1 - i[0],))


def spread(values, axes, count):
    return lax.all_to_all(jnp.broadcast_to(values[None], (count,) + values.shape), axes, 0, 0)


def pieces_of(values):
    high = lax.reduce_precision(values, 8, 7)
    rest = values - high
    mid = lax.reduce_precision(rest, 8, 7)
    return jnp.concatenate([high, mid, rest - mid]).astype(jnp.bfloat16)


def sums_kernel(tokens, out):
    x = tokens[...].astype(jnp.float32)
    first = jnp.sum(x, axis=1, keepdims=True)
    second = jnp.sum(x * x, axis=1, keepdims=True)
    lane = lax.broadcasted_iota(jnp.int32, (128, 128), 1)
    out[...] = jnp.where(lane == 0, first, second).T[:8]


def partial_kernel(where, t0, t1, t2, t3, w_mine, w_theirs, out, w, acc):
    zl, core, turn, x_here = where[0], where[1], where[2], where[3]
    half = w_mine.shape[2]
    for step in range(NX):
        x = lax.rem(x_here + step, NX)
        for s in range(3):
            cols = slice(s * 256, s * 256 + 256)
            w[x, pl.ds(pl.multiple_of(core * half, half), half), cols] = w_mine[step, s]
            w[x, pl.ds(pl.multiple_of((1 - core) * half, half), half), cols] = w_theirs[step, s]
    tokens = (t0, t1, t2, t3)

    def extra(slot, quarter):
        return tokens[slot][quarter, 128:144].astype(jnp.float32)

    centers, scales = [], []
    for quarter in range(NZH):
        rows = sum(extra(slot, quarter)[:2] for slot in range(NZL))
        sums = (rows[:, :128] + rows[:, 128:256] + rows[:, 256:]) / FEATURES
        center = sums[0:1]
        centers.append(center)
        scales.append(lax.rsqrt(sums[1:2] - center * center + EPSILON))
    stats = jnp.concatenate(centers + scales, axis=0).T

    for slot in range(NZL):
        row_gain = extra(slot, 0)[2:3]
        normed = []
        for quarter in range(NZH):
            x = tokens[slot][quarter, :128].astype(jnp.float32)
            center = stats[:, quarter : quarter + 1]
            scale = stats[:, NZH + quarter : NZH + quarter + 1]
            normed.append(((x - center) * scale * row_gain).astype(jnp.bfloat16))
        term = jnp.dot(
            jnp.concatenate(normed, axis=0),
            w[lax.rem(zl + slot, NZL)],
            preferred_element_type=jnp.float32,
        )
        if slot == 0:
            acc[...] = term
        else:
            acc[...] += term
    for core_to in range(CORES):
        for y_to in range(NY):
            quarter = lax.rem(turn + y_to + 2 * core_to, NZH)
            rows = pl.ds(pl.multiple_of(quarter * 128, 128), 128)
            head = y_to // 2
            for s in range(3):
                cols = slice(s * 256 + head * DH, s * 256 + head * DH + DH)
                out[core_to, y_to, :, s * DH : s * DH + DH] = acc[rows, cols].astype(jnp.bfloat16)


def heads_kernel(part, head_gain, q_out, kv_out):
    def head_norm(values, row):
        mid = jnp.mean(values, axis=1, keepdims=True)
        var = jnp.mean(values * values, axis=1, keepdims=True) - mid * mid
        return ((values - mid) * lax.rsqrt(var + EPSILON) * row).astype(jnp.bfloat16)

    for source in range(2):
        rows = slice(source * 128, source * 128 + 128)
        acc = sum(part[source, y].astype(jnp.float32) for y in range(NY))
        q_out[rows] = head_norm(acc[:, :DH], head_gain[0])
        key = head_norm(acc[:, DH : 2 * DH], head_gain[1])
        value = acc[:, 2 * DH :].astype(jnp.bfloat16)
        for target in range(NX * 2):
            kv_out[target, 0, rows] = key
            kv_out[target, 1, rows] = value


def attend_kernel(q, kv_mine, kv_theirs, out):
    scores = [
        lax.dot_general(
            q[...],
            kv[:, 0].reshape(-1, DH),
            (((1,), (1,)), ((), ())),
            preferred_element_type=jnp.float32,
        )
        * (DH ** -0.5)
        for kv in (kv_mine, kv_theirs)
    ]
    top = jnp.maximum(*[jnp.max(part, axis=1, keepdims=True) for part in scores])
    weights = [jnp.exp(part - top) for part in scores]
    total = sum(jnp.sum(part, axis=1, keepdims=True) for part in weights)
    mixed = sum(
        jnp.dot(
            part.astype(jnp.bfloat16), kv[:, 1].reshape(-1, DH), preferred_element_type=jnp.float32
        )
        for part, kv in zip(weights, (kv_mine, kv_theirs))
    )
    out[...] = (mixed / total).astype(jnp.bfloat16)


def kernel_call(kernel, out_shape, args, scalars=0, scratch=(), flops=None):
    vmem = pl.BlockSpec(memory_space=pltpu.VMEM)
    smem = pl.BlockSpec(memory_space=pltpu.SMEM)
    return pl.pallas_call(
        kernel,
        out_shape=out_shape,
        in_specs=[smem] * scalars + [vmem] * (len(args) - scalars),
        out_specs=jax.tree.map(lambda _: vmem, out_shape),
        scratch_shapes=scratch,
        cost_estimate=flops and pl.CostEstimate(flops=flops, bytes_accessed=0, transcendentals=0),
        compiler_params=pltpu.CompilerParams(vmem_limit_bytes=VMEM_LIMIT),
    )(*args)


def body(tokens, ln_gain, w_qkv, q_gain, k_gain):
    core = lax.axis_index("core")
    zl = lax.axis_index("zl")
    zh = lax.axis_index("zh")
    y_high = lax.axis_index("yh")
    y_here = y_high * 2 + lax.axis_index("yl")
    turn = (zh + zl) % NZH
    where = jnp.stack([zl, core, turn, lax.axis_index("x")]).astype(jnp.int32)

    with jax.named_scope("weights"):
        w_moved = to_plane(jnp.transpose(w_qkv, (1, 0, 2)))

    with jax.named_scope("norm"):
        own = kernel_call(
            sums_kernel, jax.ShapeDtypeStruct((8, 128), jnp.float32), (tokens,), flops=SUMS_FLOPS
        )
        shared = spread(
            jnp.concatenate([own[:2].reshape(-1), q_gain, k_gain])[None],
            Y,
            NY,
        )[:, 0]
        sums = jnp.sum(shared[:, :256], axis=0)
        head_gain = lax.dynamic_index_in_dim(
            shared[:, 256:], (zh + NY - zl) % NY, 0, keepdims=False
        )
        head_gain = lax.dynamic_index_in_dim(
            head_gain.reshape(2, 2, 1, DH), y_high, 1, keepdims=False
        )
        extended = jnp.concatenate(
            [
                tokens,
                pieces_of(sums[:128])[None],
                pieces_of(sums[128:])[None],
                ln_gain[None],
                jnp.zeros((13, 384), jnp.bfloat16),
            ]
        )

    with jax.named_scope("tokens"):
        extended, w_moved = lax.optimization_barrier((extended, w_moved))
        t0 = spread(extended, "zh", NZH)

    with jax.named_scope("weights"):
        along_x = [
            shift(w_moved, ("x",), lambda i, step=step: ((i[0] - step) % NX,)) for step in (1, 2, 3)
        ]
        t0, *along_x = lax.optimization_barrier((t0, *along_x))
        w_mine = jnp.stack([w_moved] + along_x)
        w_theirs = swap_cores(w_mine)

    with jax.named_scope("tokens"):
        t1 = along_z(t0, -1)
        t3 = along_z(t0, 1)
        t2 = along_z_two(t0)

    with jax.named_scope("project"):
        part = kernel_call(
            partial_kernel,
            jax.ShapeDtypeStruct((CORES, NY, 128, 3 * DH), jnp.bfloat16),
            (where, t0, t1, t2, t3, w_mine, w_theirs),
            scalars=1,
            scratch=[
                pltpu.VMEM((NX, 384, 768), jnp.bfloat16),
                pltpu.VMEM((512, 768), jnp.float32),
            ],
        )
        part = part.reshape(CORES * NY, 128, 3 * DH)
        part = lax.all_to_all(part, ("core",) + Y, 0, 0).reshape(CORES, NY, 128, 3 * DH)
        q, kv = kernel_call(
            heads_kernel,
            (
                jax.ShapeDtypeStruct((256, DH), jnp.bfloat16),
                jax.ShapeDtypeStruct((NX * 2, 2, 256, DH), jnp.bfloat16),
            ),
            (part, head_gain),
        )

    with jax.named_scope("keys"):
        kv_mine = lax.all_to_all(kv, ("x", "yl"), 0, 0)
        kv_theirs = swap_cores(kv_mine)

    with jax.named_scope("attend"):
        out = kernel_call(
            attend_kernel, jax.ShapeDtypeStruct((256, DH), jnp.bfloat16), (q, kv_mine, kv_theirs)
        )

    with jax.named_scope("home"):
        arrived = to_home(out)
        same = lax.dynamic_slice_in_dim(arrived, core * 128, 128)
        cross = swap_cores(lax.dynamic_slice_in_dim(arrived, (1 - core) * 128, 128))
        first = (zh + 3 * NY - y_here - 2 * zl - 2 * core) % NY < 2
        return jnp.where(
            first,
            jnp.concatenate([same, cross], axis=1),
            jnp.concatenate([cross, same], axis=1),
        )


def solution(mesh):
    fine = Mesh(mesh.devices.reshape(SIZES), AXES)
    rows = ("x", "zh", "core")
    cols = ("zl",) + Y
    in_specs = (P(rows, cols), P(cols), P(rows, None, cols), P(cols), P(cols))
    return jax.shard_map(body, mesh=fine, in_specs=in_specs, out_specs=P(rows, cols), check_vma=False)
```

```python
import numpy as np
import jax
import jax.numpy as jnp
from jax import lax
from jax.experimental import pallas as pl
from jax.experimental.pallas import tpu as pltpu
from jax.sharding import Mesh, PartitionSpec as P

DH = 128
EPSILON = 1e-06
FEATURES = 6144
NX = NZH = NZL = NY = 4
CORES = 2
AXES = ("x", "zh", "core", "zl", "yh", "yl")
SIZES = (NX, NZH, CORES, NZL, 2, 2)
Y = ("yh", "yl")
VMEM_LIMIT = 28 * 1024 * 1024


def shift(values, axes, move):
    sizes = [SIZES[AXES.index(axis)] for axis in axes]
    pairs = [
        (int(np.ravel_multi_index(src, sizes)), int(np.ravel_multi_index(move(src), sizes)))
        for src in np.ndindex(*sizes)
    ]
    return lax.ppermute(values, axes, pairs)


def plane_turn(zl):
    return (0, 1, 0, 2)[zl]


def to_plane(values):
    def move(i):
        zh, zl, yh, yl = i
        return ((yh * 2 + yl + plane_turn(zl)) % NZH, (zl + 2) % NZL) + divmod(zh, 2)

    return shift(values, ("zh", "zl") + Y, move)


def to_home(values):
    def move(i):
        zh, core, zl, yh, yl = i
        step = 4 * ((yh * 2 + yl + 2 * core + zl) % 4) + 2
        zh_home, zl_home = divmod((zh * NZL + zl + step) % 16, NZL)
        return (zh_home, core, zl_home) + divmod((zh - plane_turn(zl_home)) % NY, 2)

    return shift(values, ("zh", "core", "zl") + Y, move)


def along_z(values, step):
    return shift(values, ("zh", "zl"), lambda i: divmod((i[0] * NZL + i[1] + step) % 16, NZL))


def along_z_two(values):
    def move(i):
        step = 2 if i[1] % 2 == 0 else -2
        return divmod((i[0] * NZL + i[1] + step) % 16, NZL)

    return shift(values, ("zh", "zl"), move)


def swap_cores(values):
    return shift(values, ("core",), lambda i: (1 - i[0],))


def spread(values, axes, count):
    return lax.all_to_all(jnp.broadcast_to(values[None], (count,) + values.shape), axes, 0, 0)


def sums_kernel(tokens, out):
    lane = lax.broadcasted_iota(jnp.int32, (128, 128), 1)
    columns = jnp.zeros((128, 128), jnp.float32)
    for quarter in range(NZH):
        x = tokens[quarter].astype(jnp.float32)
        columns = jnp.where(lane == quarter, jnp.sum(x, axis=1, keepdims=True), columns)
        columns = jnp.where(lane == quarter + NZH, jnp.sum(x * x, axis=1, keepdims=True), columns)
    out[...] = columns.T[: 2 * NZH]


def partial_kernel(where, t0, t1, t2, t3, sums, gain, w_mine, w_theirs, out, w, acc):
    zl, core, turn, x_here = where[0], where[1], where[2], where[3]
    half = w_mine.shape[2]
    for step in range(NX):
        x = lax.rem(x_here + step, NX)
        for s in range(3):
            cols = slice(s * 256, s * 256 + 256)
            w[x, pl.ds(pl.multiple_of(core * half, half), half), cols] = w_mine[step, s]
            w[x, pl.ds(pl.multiple_of((1 - core) * half, half), half), cols] = w_theirs[step, s]
    tokens = (t0, t1, t2, t3)

    center = sums[:NZH] / FEATURES
    scale = lax.rsqrt(sums[NZH:] / FEATURES - center * center + EPSILON)
    stats = jnp.concatenate([center, scale], axis=0).T

    for slot in range(NZL):
        part = lax.rem(zl + slot, NZL)
        row_gain = gain[part]
        normed = []
        for quarter in range(NZH):
            x = tokens[slot][quarter].astype(jnp.float32)
            center = stats[:, quarter : quarter + 1]
            scale = stats[:, NZH + quarter : NZH + quarter + 1]
            normed.append(((x - center) * scale * row_gain).astype(jnp.bfloat16))
        term = jnp.dot(
            jnp.concatenate(normed, axis=0),
            w[part],
            preferred_element_type=jnp.float32,
        )
        if slot == 0:
            acc[...] = term
        else:
            acc[...] += term
    for core_to in range(CORES):
        for y_to in range(NY):
            quarter = lax.rem(turn + y_to + 2 * core_to, NZH)
            rows = pl.ds(pl.multiple_of(quarter * 128, 128), 128)
            head = y_to // 2
            for s in range(3):
                cols = slice(s * 256 + head * DH, s * 256 + head * DH + DH)
                out[core_to, y_to, :, s * DH : s * DH + DH] = acc[rows, cols].astype(jnp.bfloat16)


def heads_kernel(part, head_gain, q_out, kv_out):
    def head_norm(values, row):
        mid = jnp.mean(values, axis=1, keepdims=True)
        var = jnp.mean(values * values, axis=1, keepdims=True) - mid * mid
        return ((values - mid) * lax.rsqrt(var + EPSILON) * row).astype(jnp.bfloat16)

    for source in range(2):
        rows = slice(source * 128, source * 128 + 128)
        acc = sum(part[source, y].astype(jnp.float32) for y in range(NY))
        q_out[rows] = head_norm(acc[:, :DH], head_gain[0])
        key = head_norm(acc[:, DH : 2 * DH], head_gain[1])
        value = acc[:, 2 * DH :].astype(jnp.bfloat16)
        for target in range(NX * 2):
            kv_out[target, 0, rows] = key
            kv_out[target, 1, rows] = value


def attend_kernel(q, kv_mine, kv_theirs, out):
    scores = [
        lax.dot_general(
            q[...],
            kv[:, 0].reshape(-1, DH),
            (((1,), (1,)), ((), ())),
            preferred_element_type=jnp.float32,
        )
        * (DH ** -0.5)
        for kv in (kv_mine, kv_theirs)
    ]
    top = jnp.maximum(*[jnp.max(part, axis=1, keepdims=True) for part in scores])
    weights = [jnp.exp(part - top) for part in scores]
    total = sum(jnp.sum(part, axis=1, keepdims=True) for part in weights)
    mixed = sum(
        jnp.dot(
            part.astype(jnp.bfloat16), kv[:, 1].reshape(-1, DH), preferred_element_type=jnp.float32
        )
        for part, kv in zip(weights, (kv_mine, kv_theirs))
    )
    out[...] = (mixed / total).astype(jnp.bfloat16)


def kernel_call(kernel, out_shape, args, scalars=0, scratch=()):
    vmem = pl.BlockSpec(memory_space=pltpu.VMEM)
    smem = pl.BlockSpec(memory_space=pltpu.SMEM)
    return pl.pallas_call(
        kernel,
        out_shape=out_shape,
        in_specs=[smem] * scalars + [vmem] * (len(args) - scalars),
        out_specs=jax.tree.map(lambda _: vmem, out_shape),
        scratch_shapes=scratch,
        compiler_params=pltpu.CompilerParams(vmem_limit_bytes=VMEM_LIMIT),
    )(*args)


def body(tokens, ln_gain, w_qkv, q_gain, k_gain):
    core = lax.axis_index("core")
    zl = lax.axis_index("zl")
    zh = lax.axis_index("zh")
    y_high = lax.axis_index("yh")
    y_here = y_high * 2 + lax.axis_index("yl")
    turn = (zh + zl + (zl >= 2)) % NZH
    head_zl = (zl + 2) % NZL
    head_y = (zh + NY - jnp.where(head_zl == 1, 1, jnp.where(head_zl == 3, 2, 0))) % NY
    where = jnp.stack([zl, core, turn, lax.axis_index("x")]).astype(jnp.int32)

    with jax.named_scope("weights"):
        w_moved = to_plane(jnp.transpose(w_qkv, (1, 0, 2)))

    with jax.named_scope("tokens"):
        tokens, w_moved = lax.optimization_barrier((tokens, w_moved))
        t0 = spread(tokens, "zh", NZH)

    with jax.named_scope("weights"):
        along_x = [
            shift(w_moved, ("x",), lambda i, step=step: ((i[0] - step) % NX,)) for step in (1, 2, 3)
        ]
        t0, *along_x = lax.optimization_barrier((t0, *along_x))
        w_mine = jnp.stack([w_moved] + along_x)
        w_theirs = swap_cores(w_mine)

    with jax.named_scope("tokens"):
        t1 = along_z(t0, -1)
        t3 = along_z(t0, 1)
        t2 = along_z_two(t0)

    with jax.named_scope("norm"):
        own = kernel_call(sums_kernel, jax.ShapeDtypeStruct((2 * NZH, 128), jnp.float32), (t0,))
        shared = spread(
            jnp.concatenate([own.reshape(-1), ln_gain.astype(jnp.float32), q_gain, k_gain])[None],
            ("zl",) + Y,
            NZL * NY,
        )[:, 0]
        sums = jnp.sum(shared[:, :1024], axis=0).reshape(2 * NZH, 128)
        gain = lax.dynamic_index_in_dim(
            shared[:, 1024:1408].reshape(NZL, NY, 1, 384), y_here, 1, keepdims=False
        )
        head_gain = lax.dynamic_index_in_dim(
            shared[:, 1408:], head_zl * NY + head_y, 0, keepdims=False
        )
        head_gain = lax.dynamic_index_in_dim(
            head_gain.reshape(2, 2, 1, DH), y_high, 1, keepdims=False
        )

    with jax.named_scope("project"):
        part = kernel_call(
            partial_kernel,
            jax.ShapeDtypeStruct((CORES, NY, 128, 3 * DH), jnp.bfloat16),
            (where, t0, t1, t2, t3, sums, gain, w_mine, w_theirs),
            scalars=1,
            scratch=[
                pltpu.VMEM((NX, 384, 768), jnp.bfloat16),
                pltpu.VMEM((512, 768), jnp.float32),
            ],
        )
        part = part.reshape(CORES * NY, 128, 3 * DH)
        part = lax.all_to_all(part, ("core",) + Y, 0, 0).reshape(CORES, NY, 128, 3 * DH)
        q, kv = kernel_call(
            heads_kernel,
            (
                jax.ShapeDtypeStruct((256, DH), jnp.bfloat16),
                jax.ShapeDtypeStruct((NX * 2, 2, 256, DH), jnp.bfloat16),
            ),
            (part, head_gain),
        )

    with jax.named_scope("keys"):
        kv_mine = lax.all_to_all(kv, ("x", "yl"), 0, 0)
        kv_theirs = swap_cores(kv_mine)

    with jax.named_scope("attend"):
        out = kernel_call(
            attend_kernel, jax.ShapeDtypeStruct((256, DH), jnp.bfloat16), (q, kv_mine, kv_theirs)
        )

    with jax.named_scope("home"):
        arrived = to_home(out)
        same = lax.dynamic_slice_in_dim(arrived, core * 128, 128)
        cross = swap_cores(lax.dynamic_slice_in_dim(arrived, (1 - core) * 128, 128))
        zl_from = (zl + 2) % NZL
        zh_from = y_here + jnp.where(zl == 1, 1, jnp.where(zl == 3, 2, 0))
        y_from = zh + 4 * NY - zh_from - zl_from - (zl_from >= 2) - 2 * core
        first = y_from % NY < 2
        return jnp.where(
            first,
            jnp.concatenate([same, cross], axis=1),
            jnp.concatenate([cross, same], axis=1),
        )


def solution(mesh):
    fine = Mesh(mesh.devices.reshape(SIZES), AXES)
    rows = ("x", "zh", "core")
    cols = ("zl",) + Y
    in_specs = (P(rows, cols), P(cols), P(rows, None, cols), P(cols), P(cols))
    return jax.shard_map(body, mesh=fine, in_specs=in_specs, out_specs=P(rows, cols), check_vma=False)
```

```python
import numpy as np
import jax
import jax.numpy as jnp
from jax import lax
from jax.experimental import pallas as pl
from jax.experimental.pallas import tpu as pltpu
from jax.sharding import Mesh, PartitionSpec as P

DH = 128
EPSILON = 1e-06
FEATURES = 6144
NX = NZH = NZL = NY = 4
CORES = 2
AXES = ("x", "zh", "core", "zl", "yh", "yl")
SIZES = (NX, NZH, CORES, NZL, 2, 2)
Y = ("yh", "yl")
VMEM_LIMIT = 28 * 1024 * 1024


def shift(values, axes, move):
    sizes = [SIZES[AXES.index(axis)] for axis in axes]
    pairs = [
        (int(np.ravel_multi_index(src, sizes)), int(np.ravel_multi_index(move(src), sizes)))
        for src in np.ndindex(*sizes)
    ]
    return lax.ppermute(values, axes, pairs)


def plane_turn(zl):
    return (0, 1, 0, 2)[zl]


def to_plane(values):
    def move(i):
        zh, zl, yh, yl = i
        return ((yh * 2 + yl + plane_turn(zl)) % NZH, (zl + 2) % NZL) + divmod(zh, 2)

    return shift(values, ("zh", "zl") + Y, move)


def to_home(values):
    def move(i):
        zh, core, zl, yh, yl = i
        step = 4 * ((yh * 2 + yl + 2 * core + zl) % 4) + 2
        zh_home, zl_home = divmod((zh * NZL + zl + step) % 16, NZL)
        return (zh_home, core, zl_home) + divmod((zh - plane_turn(zl_home)) % NY, 2)

    return shift(values, ("zh", "core", "zl") + Y, move)


def along_z(values, step):
    return shift(values, ("zh", "zl"), lambda i: divmod((i[0] * NZL + i[1] + step) % 16, NZL))


def along_z_two(values):
    def move(i):
        step = 2 if i[1] % 2 == 0 else -2
        return divmod((i[0] * NZL + i[1] + step) % 16, NZL)

    return shift(values, ("zh", "zl"), move)


def swap_cores(values):
    return shift(values, ("core",), lambda i: (1 - i[0],))


def spread(values, axes, count):
    return lax.all_to_all(jnp.broadcast_to(values[None], (count,) + values.shape), axes, 0, 0)


def share_kernel(tokens, ln_gain, q_gain, k_gain, out):
    lane = lax.broadcasted_iota(jnp.int32, (128, 128), 1)
    columns = jnp.zeros((128, 128), jnp.float32)
    for quarter in range(NZH):
        x = tokens[quarter].astype(jnp.float32)
        columns = jnp.where(lane == quarter, jnp.sum(x, axis=1, keepdims=True), columns)
        columns = jnp.where(lane == quarter + NZH, jnp.sum(x * x, axis=1, keepdims=True), columns)
    sums = columns.T[: 2 * NZH]
    for target in range(NZL * NY):
        out[target, 0:8] = sums
        out[target, 8:11] = ln_gain[...].astype(jnp.float32)
        out[target, 11:13] = q_gain[...]
        out[target, 13:15] = k_gain[...]
        out[target, 15:16] = jnp.zeros((1, 128), jnp.float32)


def partial_kernel(where, t0, t1, t2, t3, shared, w_mine, w_theirs, out, w, acc):
    zl, core, turn, x_here, y_here = (where[i] for i in range(5))
    half = w_mine.shape[2]
    for step in range(NX):
        x = lax.rem(x_here + step, NX)
        for s in range(3):
            cols = slice(s * 256, s * 256 + 256)
            w[x, pl.ds(pl.multiple_of(core * half, half), half), cols] = w_mine[step, s]
            w[x, pl.ds(pl.multiple_of((1 - core) * half, half), half), cols] = w_theirs[step, s]
    tokens = (t0, t1, t2, t3)

    sums = shared[0, 0:8]
    for group in range(1, NZL * NY):
        sums += shared[group, 0:8]
    center = sums[:NZH] / FEATURES
    scale = lax.rsqrt(sums[NZH:] / FEATURES - center * center + EPSILON)
    stats = jnp.concatenate([center, scale], axis=0).T

    for slot in range(NZL):
        part = lax.rem(zl + slot, NZL)
        rows = shared[part * NY + y_here, 8:11]
        row_gain = jnp.concatenate([rows[0:1], rows[1:2], rows[2:3]], axis=1)
        normed = []
        for quarter in range(NZH):
            x = tokens[slot][quarter].astype(jnp.float32)
            center = stats[:, quarter : quarter + 1]
            scale = stats[:, NZH + quarter : NZH + quarter + 1]
            normed.append(((x - center) * scale * row_gain).astype(jnp.bfloat16))
        term = jnp.dot(
            jnp.concatenate(normed, axis=0),
            w[part],
            preferred_element_type=jnp.float32,
        )
        if slot == 0:
            acc[...] = term
        else:
            acc[...] += term
    for core_to in range(CORES):
        for y_to in range(NY):
            quarter = lax.rem(turn + y_to + 2 * core_to, NZH)
            rows = pl.ds(pl.multiple_of(quarter * 128, 128), 128)
            head = y_to // 2
            for s in range(3):
                cols = slice(s * 256 + head * DH, s * 256 + head * DH + DH)
                out[core_to, y_to, :, s * DH : s * DH + DH] = acc[rows, cols].astype(jnp.bfloat16)


def heads_kernel(where, part, shared, q_out, kv_out):
    rows = shared[where[5], 11:15]
    high = where[6] > 0
    q_row = jnp.where(high, rows[1:2], rows[0:1])
    k_row = jnp.where(high, rows[3:4], rows[2:3])

    def head_norm(values, row):
        mid = jnp.mean(values, axis=1, keepdims=True)
        var = jnp.mean(values * values, axis=1, keepdims=True) - mid * mid
        return ((values - mid) * lax.rsqrt(var + EPSILON) * row).astype(jnp.bfloat16)

    for source in range(2):
        rows = slice(source * 128, source * 128 + 128)
        acc = sum(part[source, y].astype(jnp.float32) for y in range(NY))
        q_out[rows] = head_norm(acc[:, :DH], q_row)
        key = head_norm(acc[:, DH : 2 * DH], k_row)
        value = acc[:, 2 * DH :].astype(jnp.bfloat16)
        for target in range(NX * 2):
            kv_out[target, 0, rows] = key
            kv_out[target, 1, rows] = value


def attend_kernel(q, kv_mine, kv_theirs, out):
    scores = [
        lax.dot_general(
            q[...],
            kv[:, 0].reshape(-1, DH),
            (((1,), (1,)), ((), ())),
            preferred_element_type=jnp.float32,
        )
        * (DH ** -0.5)
        for kv in (kv_mine, kv_theirs)
    ]
    top = jnp.maximum(*[jnp.max(part, axis=1, keepdims=True) for part in scores])
    weights = [jnp.exp(part - top) for part in scores]
    total = sum(jnp.sum(part, axis=1, keepdims=True) for part in weights)
    mixed = sum(
        jnp.dot(
            part.astype(jnp.bfloat16), kv[:, 1].reshape(-1, DH), preferred_element_type=jnp.float32
        )
        for part, kv in zip(weights, (kv_mine, kv_theirs))
    )
    out[...] = (mixed / total).astype(jnp.bfloat16)


def kernel_call(kernel, out_shape, args, scalars=0, scratch=()):
    vmem = pl.BlockSpec(memory_space=pltpu.VMEM)
    smem = pl.BlockSpec(memory_space=pltpu.SMEM)
    return pl.pallas_call(
        kernel,
        out_shape=out_shape,
        in_specs=[smem] * scalars + [vmem] * (len(args) - scalars),
        out_specs=jax.tree.map(lambda _: vmem, out_shape),
        scratch_shapes=scratch,
        compiler_params=pltpu.CompilerParams(vmem_limit_bytes=VMEM_LIMIT),
    )(*args)


def body(tokens, ln_gain, w_qkv, q_gain, k_gain):
    core = lax.axis_index("core")
    zl = lax.axis_index("zl")
    zh = lax.axis_index("zh")
    y_high = lax.axis_index("yh")
    y_here = y_high * 2 + lax.axis_index("yl")
    turn = (zh + zl + (zl >= 2)) % NZH
    head_zl = (zl + 2) % NZL
    head_y = (zh + NY - jnp.where(head_zl == 1, 1, jnp.where(head_zl == 3, 2, 0))) % NY
    where = jnp.stack(
        [zl, core, turn, lax.axis_index("x"), y_here, head_zl * NY + head_y, y_high]
    ).astype(jnp.int32)

    with jax.named_scope("weights"):
        w_moved = to_plane(jnp.transpose(w_qkv, (1, 0, 2)))

    with jax.named_scope("tokens"):
        tokens, w_moved = lax.optimization_barrier((tokens, w_moved))
        t0 = spread(tokens, "zh", NZH)

    with jax.named_scope("weights"):
        along_x = [
            shift(w_moved, ("x",), lambda i, step=step: ((i[0] - step) % NX,)) for step in (1, 2, 3)
        ]
        t0, *along_x = lax.optimization_barrier((t0, *along_x))
        w_mine = jnp.stack([w_moved] + along_x)
        w_theirs = swap_cores(w_mine)

    with jax.named_scope("tokens"):
        t1 = along_z(t0, -1)
        t3 = along_z(t0, 1)
        t2 = along_z_two(t0)

    with jax.named_scope("norm"):
        shared = kernel_call(
            share_kernel,
            jax.ShapeDtypeStruct((NZL * NY, 16, 128), jnp.float32),
            (t0, ln_gain.reshape(3, 128), q_gain.reshape(2, 128), k_gain.reshape(2, 128)),
        )
        shared = lax.all_to_all(shared, ("zl",) + Y, 0, 0)

    with jax.named_scope("project"):
        part = kernel_call(
            partial_kernel,
            jax.ShapeDtypeStruct((CORES, NY, 128, 3 * DH), jnp.bfloat16),
            (where, t0, t1, t2, t3, shared, w_mine, w_theirs),
            scalars=1,
            scratch=[
                pltpu.VMEM((NX, 384, 768), jnp.bfloat16),
                pltpu.VMEM((512, 768), jnp.float32),
            ],
        )
        part = part.reshape(CORES * NY, 128, 3 * DH)
        part = lax.all_to_all(part, ("core",) + Y, 0, 0).reshape(CORES, NY, 128, 3 * DH)
        q, kv = kernel_call(
            heads_kernel,
            (
                jax.ShapeDtypeStruct((256, DH), jnp.bfloat16),
                jax.ShapeDtypeStruct((NX * 2, 2, 256, DH), jnp.bfloat16),
            ),
            (where, part, shared),
            scalars=1,
        )

    with jax.named_scope("keys"):
        kv_mine = lax.all_to_all(kv, ("x", "yl"), 0, 0)
        kv_theirs = swap_cores(kv_mine)

    with jax.named_scope("attend"):
        out = kernel_call(
            attend_kernel, jax.ShapeDtypeStruct((256, DH), jnp.bfloat16), (q, kv_mine, kv_theirs)
        )

    with jax.named_scope("home"):
        arrived = to_home(out)
        same = lax.dynamic_slice_in_dim(arrived, core * 128, 128)
        cross = swap_cores(lax.dynamic_slice_in_dim(arrived, (1 - core) * 128, 128))
        zl_from = (zl + 2) % NZL
        zh_from = y_here + jnp.where(zl == 1, 1, jnp.where(zl == 3, 2, 0))
        y_from = zh + 4 * NY - zh_from - zl_from - (zl_from >= 2) - 2 * core
        first = y_from % NY < 2
        return jnp.where(
            first,
            jnp.concatenate([same, cross], axis=1),
            jnp.concatenate([cross, same], axis=1),
        )


def solution(mesh):
    fine = Mesh(mesh.devices.reshape(SIZES), AXES)
    rows = ("x", "zh", "core")
    cols = ("zl",) + Y
    in_specs = (P(rows, cols), P(cols), P(rows, None, cols), P(cols), P(cols))
    return jax.shard_map(body, mesh=fine, in_specs=in_specs, out_specs=P(rows, cols), check_vma=False)
```

```python
import numpy as np
import jax
import jax.numpy as jnp
from jax import lax
from jax.experimental import pallas as pl
from jax.experimental.pallas import tpu as pltpu
from jax.sharding import Mesh, PartitionSpec as P

DH = 128
EPSILON = 1e-06
FEATURES = 6144
NX = NZH = NZL = NY = 4
CORES = 2
AXES = ("x", "zh", "core", "zl", "yh", "yl")
SIZES = (NX, NZH, CORES, NZL, 2, 2)
Y = ("yh", "yl")
VMEM_LIMIT = 28 * 1024 * 1024


def shift(values, axes, move):
    sizes = [SIZES[AXES.index(axis)] for axis in axes]
    pairs = [
        (int(np.ravel_multi_index(src, sizes)), int(np.ravel_multi_index(move(src), sizes)))
        for src in np.ndindex(*sizes)
    ]
    return lax.ppermute(values, axes, pairs)


def plane_turn(zl):
    return (0, 1, 0, 2)[zl]


def to_plane(values):
    def move(i):
        zh, zl, yh, yl = i
        return ((yh * 2 + yl + plane_turn(zl)) % NZH, (zl + 2) % NZL) + divmod(zh, 2)

    return shift(values, ("zh", "zl") + Y, move)


def to_home(values):
    def move(i):
        zh, core, zl, yh, yl = i
        step = 4 * ((yh * 2 + yl + 2 * core + zl) % 4) + 2
        zh_home, zl_home = divmod((zh * NZL + zl + step) % 16, NZL)
        return (zh_home, core, zl_home) + divmod((zh - plane_turn(zl_home)) % NY, 2)

    return shift(values, ("zh", "core", "zl") + Y, move)


def along_z(values, step):
    return shift(values, ("zh", "zl"), lambda i: divmod((i[0] * NZL + i[1] + step) % 16, NZL))


def along_z_two(values):
    def move(i):
        step = 2 if i[1] % 2 == 0 else -2
        return divmod((i[0] * NZL + i[1] + step) % 16, NZL)

    return shift(values, ("zh", "zl"), move)


def swap_cores(values):
    return shift(values, ("core",), lambda i: (1 - i[0],))


def spread(values, axes, count):
    return lax.all_to_all(jnp.broadcast_to(values[None], (count,) + values.shape), axes, 0, 0)


def share_kernel(tokens, ln_gain, out):
    lane = lax.broadcasted_iota(jnp.int32, (128, 128), 1)
    columns = jnp.zeros((128, 128), jnp.float32)
    for quarter in range(NZH):
        x = tokens[quarter].astype(jnp.float32)
        columns = jnp.where(lane == quarter, jnp.sum(x, axis=1, keepdims=True), columns)
        columns = jnp.where(lane == quarter + NZH, jnp.sum(x * x, axis=1, keepdims=True), columns)
    sums = columns.T[: 2 * NZH]
    for target in range(NZL * NY):
        out[target, 0:8] = sums
        out[target, 8:11] = ln_gain[...].astype(jnp.float32)


def partial_kernel(where, t0, t1, t2, t3, shared, w_mine, w_theirs, out, w, acc):
    zl, core, turn, x_here, y_here = (where[i] for i in range(5))
    half = w_mine.shape[2]
    for step in range(NX):
        x = lax.rem(x_here + step, NX)
        for s in range(3):
            cols = slice(s * 256, s * 256 + 256)
            w[x, pl.ds(pl.multiple_of(core * half, half), half), cols] = w_mine[step, s]
            w[x, pl.ds(pl.multiple_of((1 - core) * half, half), half), cols] = w_theirs[step, s]
    tokens = (t0, t1, t2, t3)

    sums = shared[0, 0:8]
    for group in range(1, NZL * NY):
        sums += shared[group, 0:8]
    center = sums[:NZH] / FEATURES
    scale = lax.rsqrt(sums[NZH:] / FEATURES - center * center + EPSILON)
    stats = jnp.concatenate([center, scale], axis=0).T

    for slot in range(NZL):
        part = lax.rem(zl + slot, NZL)
        rows = shared[part * NY + y_here, 8:11]
        row_gain = jnp.concatenate([rows[0:1], rows[1:2], rows[2:3]], axis=1)
        normed = []
        for quarter in range(NZH):
            x = tokens[slot][quarter].astype(jnp.float32)
            center = stats[:, quarter : quarter + 1]
            scale = stats[:, NZH + quarter : NZH + quarter + 1]
            normed.append(((x - center) * scale * row_gain).astype(jnp.bfloat16))
        term = jnp.dot(
            jnp.concatenate(normed, axis=0),
            w[part],
            preferred_element_type=jnp.float32,
        )
        if slot == 0:
            acc[...] = term
        else:
            acc[...] += term
    for core_to in range(CORES):
        for y_to in range(NY):
            quarter = lax.rem(turn + y_to + 2 * core_to, NZH)
            rows = pl.ds(pl.multiple_of(quarter * 128, 128), 128)
            head = y_to // 2
            for s in range(3):
                cols = slice(s * 256 + head * DH, s * 256 + head * DH + DH)
                out[core_to, y_to, :, s * DH : s * DH + DH] = acc[rows, cols].astype(jnp.bfloat16)


def heads_kernel(where, part, head_gain, q_out, kv_out):
    high = where[5] > 0
    q_row = jnp.where(high, head_gain[1:2], head_gain[0:1])
    k_row = jnp.where(high, head_gain[3:4], head_gain[2:3])

    def head_norm(values, row):
        mid = jnp.mean(values, axis=1, keepdims=True)
        var = jnp.mean(values * values, axis=1, keepdims=True) - mid * mid
        return ((values - mid) * lax.rsqrt(var + EPSILON) * row).astype(jnp.bfloat16)

    for source in range(2):
        rows = slice(source * 128, source * 128 + 128)
        acc = sum(part[source, y].astype(jnp.float32) for y in range(NY))
        q_out[rows] = head_norm(acc[:, :DH], q_row)
        key = head_norm(acc[:, DH : 2 * DH], k_row)
        value = acc[:, 2 * DH :].astype(jnp.bfloat16)
        for target in range(NX * 2):
            kv_out[target, 0, rows] = key
            kv_out[target, 1, rows] = value


def attend_kernel(q, kv_mine, kv_theirs, out):
    scores = [
        lax.dot_general(
            q[...],
            kv[:, 0].reshape(-1, DH),
            (((1,), (1,)), ((), ())),
            preferred_element_type=jnp.float32,
        )
        * (DH ** -0.5)
        for kv in (kv_mine, kv_theirs)
    ]
    top = jnp.maximum(*[jnp.max(part, axis=1, keepdims=True) for part in scores])
    weights = [jnp.exp(part - top) for part in scores]
    total = sum(jnp.sum(part, axis=1, keepdims=True) for part in weights)
    mixed = sum(
        jnp.dot(
            part.astype(jnp.bfloat16), kv[:, 1].reshape(-1, DH), preferred_element_type=jnp.float32
        )
        for part, kv in zip(weights, (kv_mine, kv_theirs))
    )
    out[...] = (mixed / total).astype(jnp.bfloat16)


def kernel_call(kernel, out_shape, args, scalars=0, scratch=()):
    vmem = pl.BlockSpec(memory_space=pltpu.VMEM)
    smem = pl.BlockSpec(memory_space=pltpu.SMEM)
    return pl.pallas_call(
        kernel,
        out_shape=out_shape,
        in_specs=[smem] * scalars + [vmem] * (len(args) - scalars),
        out_specs=jax.tree.map(lambda _: vmem, out_shape),
        scratch_shapes=scratch,
        compiler_params=pltpu.CompilerParams(vmem_limit_bytes=VMEM_LIMIT),
    )(*args)


def body(tokens, ln_gain, w_qkv, q_gain, k_gain):
    core = lax.axis_index("core")
    zl = lax.axis_index("zl")
    zh = lax.axis_index("zh")
    y_high = lax.axis_index("yh")
    y_here = y_high * 2 + lax.axis_index("yl")
    turn = (zh + zl + (zl >= 2)) % NZH
    where = jnp.stack(
        [zl, core, turn, lax.axis_index("x"), y_here, y_high]
    ).astype(jnp.int32)

    with jax.named_scope("weights"):
        w_moved = to_plane(jnp.transpose(w_qkv, (1, 0, 2)))
        head_gain = to_plane(jnp.concatenate([q_gain, k_gain]).reshape(4, DH))

    with jax.named_scope("tokens"):
        tokens, w_moved, head_gain = lax.optimization_barrier((tokens, w_moved, head_gain))
        t0 = spread(tokens, "zh", NZH)

    with jax.named_scope("weights"):
        along_x = [
            shift(w_moved, ("x",), lambda i, step=step: ((i[0] - step) % NX,)) for step in (1, 2, 3)
        ]
        t0, *along_x = lax.optimization_barrier((t0, *along_x))
        w_mine = jnp.stack([w_moved] + along_x)
        w_theirs = swap_cores(w_mine)

    with jax.named_scope("tokens"):
        t1 = along_z(t0, -1)
        t3 = along_z(t0, 1)
        t2 = along_z_two(t0)

    with jax.named_scope("norm"):
        shared = kernel_call(
            share_kernel,
            jax.ShapeDtypeStruct((NZL * NY, 11, 128), jnp.float32),
            (t0, ln_gain.reshape(3, 128)),
        )
        shared = lax.all_to_all(shared, ("zl",) + Y, 0, 0)

    with jax.named_scope("project"):
        part = kernel_call(
            partial_kernel,
            jax.ShapeDtypeStruct((CORES, NY, 128, 3 * DH), jnp.bfloat16),
            (where, t0, t1, t2, t3, shared, w_mine, w_theirs),
            scalars=1,
            scratch=[
                pltpu.VMEM((NX, 384, 768), jnp.bfloat16),
                pltpu.VMEM((512, 768), jnp.float32),
            ],
        )
        part = part.reshape(CORES * NY, 128, 3 * DH)
        part = lax.all_to_all(part, ("core",) + Y, 0, 0).reshape(CORES, NY, 128, 3 * DH)
        q, kv = kernel_call(
            heads_kernel,
            (
                jax.ShapeDtypeStruct((256, DH), jnp.bfloat16),
                jax.ShapeDtypeStruct((NX * 2, 2, 256, DH), jnp.bfloat16),
            ),
            (where, part, head_gain),
            scalars=1,
        )

    with jax.named_scope("keys"):
        kv_mine = lax.all_to_all(kv, ("x", "yl"), 0, 0)
        kv_theirs = swap_cores(kv_mine)

    with jax.named_scope("attend"):
        out = kernel_call(
            attend_kernel, jax.ShapeDtypeStruct((256, DH), jnp.bfloat16), (q, kv_mine, kv_theirs)
        )

    with jax.named_scope("home"):
        arrived = to_home(out)
        same = lax.dynamic_slice_in_dim(arrived, core * 128, 128)
        cross = swap_cores(lax.dynamic_slice_in_dim(arrived, (1 - core) * 128, 128))
        zl_from = (zl + 2) % NZL
        zh_from = y_here + jnp.where(zl == 1, 1, jnp.where(zl == 3, 2, 0))
        y_from = zh + 4 * NY - zh_from - zl_from - (zl_from >= 2) - 2 * core
        first = y_from % NY < 2
        return jnp.where(
            first,
            jnp.concatenate([same, cross], axis=1),
            jnp.concatenate([cross, same], axis=1),
        )


def solution(mesh):
    fine = Mesh(mesh.devices.reshape(SIZES), AXES)
    rows = ("x", "zh", "core")
    cols = ("zl",) + Y
    in_specs = (P(rows, cols), P(cols), P(rows, None, cols), P(cols), P(cols))
    return jax.shard_map(body, mesh=fine, in_specs=in_specs, out_specs=P(rows, cols), check_vma=False)
```

```python
import numpy as np
import jax
import jax.numpy as jnp
from jax import lax
from jax.experimental import pallas as pl
from jax.experimental.pallas import tpu as pltpu
from jax.sharding import Mesh, PartitionSpec as P

DH = 128
EPSILON = 1e-06
FEATURES = 6144
NX = NZH = NZL = NY = 4
CORES = 2
AXES = ("x", "zh", "core", "zl", "yh", "yl")
SIZES = (NX, NZH, CORES, NZL, 2, 2)
Y = ("yh", "yl")
VMEM_LIMIT = 28 * 1024 * 1024


def shift(values, axes, move):
    sizes = [SIZES[AXES.index(axis)] for axis in axes]
    pairs = [
        (int(np.ravel_multi_index(src, sizes)), int(np.ravel_multi_index(move(src), sizes)))
        for src in np.ndindex(*sizes)
    ]
    return lax.ppermute(values, axes, pairs)


def plane_turn(zl):
    return (0, 1, 0, 2)[zl]


def to_plane(values):
    def move(i):
        zh, zl, yh, yl = i
        return ((yh * 2 + yl + plane_turn(zl)) % NZH, (zl + 2) % NZL) + divmod(zh, 2)

    return shift(values, ("zh", "zl") + Y, move)


def to_home(values):
    def move(i):
        zh, core, zl, yh, yl = i
        step = 4 * ((yh * 2 + yl + 2 * core + zl) % 4) + 2
        zh_home, zl_home = divmod((zh * NZL + zl + step) % 16, NZL)
        return (zh_home, core, zl_home) + divmod((zh - plane_turn(zl_home)) % NY, 2)

    return shift(values, ("zh", "core", "zl") + Y, move)


def along_z(values, step):
    return shift(values, ("zh", "zl"), lambda i: divmod((i[0] * NZL + i[1] + step) % 16, NZL))


def along_z_two(values):
    def move(i):
        step = 2 if i[1] % 2 == 0 else -2
        return divmod((i[0] * NZL + i[1] + step) % 16, NZL)

    return shift(values, ("zh", "zl"), move)


def swap_cores(values):
    return shift(values, ("core",), lambda i: (1 - i[0],))


def spread(values, axes, count):
    return lax.all_to_all(jnp.broadcast_to(values[None], (count,) + values.shape), axes, 0, 0)


def share_kernel(tokens, ln_gain, out):
    lane = lax.broadcasted_iota(jnp.int32, (128, 128), 1)
    columns = jnp.zeros((128, 128), jnp.float32)
    for quarter in range(NZH):
        x = tokens[quarter].astype(jnp.float32)
        columns = jnp.where(lane == quarter, jnp.sum(x, axis=1, keepdims=True), columns)
        columns = jnp.where(lane == quarter + NZH, jnp.sum(x * x, axis=1, keepdims=True), columns)
    sums = columns.T[: 2 * NZH]
    for target in range(NZL * NY):
        out[target, 0:8] = sums
        out[target, 8:11] = ln_gain[...].astype(jnp.float32)


def partial_kernel(where, t0, t1, t2, t3, shared, w_mine, w_theirs, out, w, acc):
    zl, core, turn, x_here, y_here = (where[i] for i in range(5))
    half = w_mine.shape[2]
    for step in range(NX):
        x = lax.rem(x_here + step, NX)
        for s in range(3):
            cols = slice(s * 256, s * 256 + 256)
            w[x, pl.ds(pl.multiple_of(core * half, half), half), cols] = w_mine[step, s]
            w[x, pl.ds(pl.multiple_of((1 - core) * half, half), half), cols] = w_theirs[step, s]
    tokens = (t0, t1, t2, t3)

    sums = shared[0, 0:8]
    for group in range(1, NZL * NY):
        sums += shared[group, 0:8]
    center = sums[:NZH] / FEATURES
    scale = lax.rsqrt(sums[NZH:] / FEATURES - center * center + EPSILON)
    stats = jnp.concatenate([center, scale], axis=0).T

    for slot in range(NZL):
        part = lax.rem(zl + slot, NZL)
        rows = shared[part * NY + y_here, 8:11]
        row_gain = jnp.concatenate([rows[0:1], rows[1:2], rows[2:3]], axis=1)
        normed = []
        for quarter in range(NZH):
            x = tokens[slot][quarter].astype(jnp.float32)
            center = stats[:, quarter : quarter + 1]
            scale = stats[:, NZH + quarter : NZH + quarter + 1]
            normed.append(((x - center) * scale * row_gain).astype(jnp.bfloat16))
        term = jnp.dot(
            jnp.concatenate(normed, axis=0),
            w[part],
            preferred_element_type=jnp.float32,
        )
        if slot == 0:
            acc[...] = term
        else:
            acc[...] += term
    for core_to in range(CORES):
        for y_to in range(NY):
            quarter = lax.rem(turn + y_to + 2 * core_to, NZH)
            rows = pl.ds(pl.multiple_of(quarter * 128, 128), 128)
            head = y_to // 2
            for s in range(3):
                cols = slice(s * 256 + head * DH, s * 256 + head * DH + DH)
                out[core_to, y_to, :, s * DH : s * DH + DH] = acc[rows, cols]


def heads_kernel(where, part, head_gain, q_out, kv_out):
    high = where[5] > 0
    q_row = jnp.where(high, head_gain[1:2], head_gain[0:1])
    k_row = jnp.where(high, head_gain[3:4], head_gain[2:3])

    def head_norm(values, row):
        mid = jnp.mean(values, axis=1, keepdims=True)
        var = jnp.mean(values * values, axis=1, keepdims=True) - mid * mid
        return ((values - mid) * lax.rsqrt(var + EPSILON) * row).astype(jnp.bfloat16)

    for source in range(2):
        rows = slice(source * 128, source * 128 + 128)
        acc = sum(part[source, y].astype(jnp.float32) for y in range(NY))
        q_out[rows] = head_norm(acc[:, :DH], q_row)
        key = head_norm(acc[:, DH : 2 * DH], k_row)
        value = acc[:, 2 * DH :].astype(jnp.bfloat16)
        for target in range(NX * 2):
            kv_out[target, 0, rows] = key
            kv_out[target, 1, rows] = value


def attend_kernel(q, kv_mine, kv_theirs, out):
    scores = [
        lax.dot_general(
            q[...],
            kv[:, 0].reshape(-1, DH),
            (((1,), (1,)), ((), ())),
            preferred_element_type=jnp.float32,
        )
        * (DH ** -0.5)
        for kv in (kv_mine, kv_theirs)
    ]
    top = jnp.maximum(*[jnp.max(part, axis=1, keepdims=True) for part in scores])
    weights = [jnp.exp(part - top) for part in scores]
    total = sum(jnp.sum(part, axis=1, keepdims=True) for part in weights)
    mixed = sum(
        jnp.dot(
            part.astype(jnp.bfloat16), kv[:, 1].reshape(-1, DH), preferred_element_type=jnp.float32
        )
        for part, kv in zip(weights, (kv_mine, kv_theirs))
    )
    out[...] = (mixed / total).astype(jnp.bfloat16)


def kernel_call(kernel, out_shape, args, scalars=0, scratch=()):
    vmem = pl.BlockSpec(memory_space=pltpu.VMEM)
    smem = pl.BlockSpec(memory_space=pltpu.SMEM)
    return pl.pallas_call(
        kernel,
        out_shape=out_shape,
        in_specs=[smem] * scalars + [vmem] * (len(args) - scalars),
        out_specs=jax.tree.map(lambda _: vmem, out_shape),
        scratch_shapes=scratch,
        compiler_params=pltpu.CompilerParams(vmem_limit_bytes=VMEM_LIMIT),
    )(*args)


def body(tokens, ln_gain, w_qkv, q_gain, k_gain):
    core = lax.axis_index("core")
    zl = lax.axis_index("zl")
    zh = lax.axis_index("zh")
    y_high = lax.axis_index("yh")
    y_here = y_high * 2 + lax.axis_index("yl")
    turn = (zh + zl + (zl >= 2)) % NZH
    where = jnp.stack(
        [zl, core, turn, lax.axis_index("x"), y_here, y_high]
    ).astype(jnp.int32)

    with jax.named_scope("weights"):
        w_moved = to_plane(jnp.transpose(w_qkv, (1, 0, 2)))
        head_gain = to_plane(jnp.concatenate([q_gain, k_gain]).reshape(4, DH))

    with jax.named_scope("tokens"):
        tokens, w_moved, head_gain = lax.optimization_barrier((tokens, w_moved, head_gain))
        t0 = spread(tokens, "zh", NZH)

    with jax.named_scope("weights"):
        along_x = [
            shift(w_moved, ("x",), lambda i, step=step: ((i[0] - step) % NX,)) for step in (1, 2, 3)
        ]
        t0, *along_x = lax.optimization_barrier((t0, *along_x))
        w_mine = jnp.stack([w_moved] + along_x)
        w_theirs = swap_cores(w_mine)

    with jax.named_scope("tokens"):
        t1 = along_z(t0, -1)
        t3 = along_z(t0, 1)
        t2 = along_z_two(t0)

    with jax.named_scope("norm"):
        shared = kernel_call(
            share_kernel,
            jax.ShapeDtypeStruct((NZL * NY, 11, 128), jnp.float32),
            (t0, ln_gain.reshape(3, 128)),
        )
        shared = lax.all_to_all(shared, ("zl",) + Y, 0, 0)

    with jax.named_scope("project"):
        part = kernel_call(
            partial_kernel,
            jax.ShapeDtypeStruct((CORES, NY, 128, 3 * DH), jnp.float32),
            (where, t0, t1, t2, t3, shared, w_mine, w_theirs),
            scalars=1,
            scratch=[
                pltpu.VMEM((NX, 384, 768), jnp.bfloat16),
                pltpu.VMEM((512, 768), jnp.float32),
            ],
        )
        part = part.reshape(CORES * NY, 128, 3 * DH)
        part = lax.all_to_all(part, ("core",) + Y, 0, 0).reshape(CORES, NY, 128, 3 * DH)
        q, kv = kernel_call(
            heads_kernel,
            (
                jax.ShapeDtypeStruct((256, DH), jnp.bfloat16),
                jax.ShapeDtypeStruct((NX * 2, 2, 256, DH), jnp.bfloat16),
            ),
            (where, part, head_gain),
            scalars=1,
        )

    with jax.named_scope("keys"):
        kv_mine = lax.all_to_all(kv, ("x", "yl"), 0, 0)
        kv_theirs = swap_cores(kv_mine)

    with jax.named_scope("attend"):
        out = kernel_call(
            attend_kernel, jax.ShapeDtypeStruct((256, DH), jnp.bfloat16), (q, kv_mine, kv_theirs)
        )

    with jax.named_scope("home"):
        arrived = to_home(out)
        same = lax.dynamic_slice_in_dim(arrived, core * 128, 128)
        cross = swap_cores(lax.dynamic_slice_in_dim(arrived, (1 - core) * 128, 128))
        zl_from = (zl + 2) % NZL
        zh_from = y_here + jnp.where(zl == 1, 1, jnp.where(zl == 3, 2, 0))
        y_from = zh + 4 * NY - zh_from - zl_from - (zl_from >= 2) - 2 * core
        first = y_from % NY < 2
        return jnp.where(
            first,
            jnp.concatenate([same, cross], axis=1),
            jnp.concatenate([cross, same], axis=1),
        )


def solution(mesh):
    fine = Mesh(mesh.devices.reshape(SIZES), AXES)
    rows = ("x", "zh", "core")
    cols = ("zl",) + Y
    in_specs = (P(rows, cols), P(cols), P(rows, None, cols), P(cols), P(cols))
    return jax.shard_map(body, mesh=fine, in_specs=in_specs, out_specs=P(rows, cols), check_vma=False)
```

```python
import numpy as np
import jax
import jax.numpy as jnp
from jax import lax
from jax.experimental import pallas as pl
from jax.experimental.pallas import tpu as pltpu
from jax.sharding import Mesh, PartitionSpec as P

DH = 128
EPSILON = 1e-06
FEATURES = 6144
NX = NZH = NZL = NY = 4
CORES = 2
AXES = ("x", "zh", "core", "zl", "yh", "yl")
SIZES = (NX, NZH, CORES, NZL, 2, 2)
Y = ("yh", "yl")
VMEM_LIMIT = 28 * 1024 * 1024


def shift(values, axes, move):
    sizes = [SIZES[AXES.index(axis)] for axis in axes]
    pairs = [
        (int(np.ravel_multi_index(src, sizes)), int(np.ravel_multi_index(move(src), sizes)))
        for src in np.ndindex(*sizes)
    ]
    return lax.ppermute(values, axes, pairs)


def plane_turn(zl):
    return (0, 1, 0, 2)[zl]


def to_plane(values):
    def move(i):
        zh, zl, yh, yl = i
        return ((yh * 2 + yl + plane_turn(zl)) % NZH, (zl + 2) % NZL) + divmod(zh, 2)

    return shift(values, ("zh", "zl") + Y, move)


def to_home(values):
    def move(i):
        zh, core, zl, yh, yl = i
        step = 4 * ((yh * 2 + yl + 2 * core + zl) % 4) + 2
        zh_home, zl_home = divmod((zh * NZL + zl + step) % 16, NZL)
        return (zh_home, core, zl_home) + divmod((zh - plane_turn(zl_home)) % NY, 2)

    return shift(values, ("zh", "core", "zl") + Y, move)


def along_z(values, step):
    return shift(values, ("zh", "zl"), lambda i: divmod((i[0] * NZL + i[1] + step) % 16, NZL))


def along_z_two(values):
    def move(i):
        step = 2 if i[1] % 2 == 0 else -2
        return divmod((i[0] * NZL + i[1] + step) % 16, NZL)

    return shift(values, ("zh", "zl"), move)


def swap_cores(values):
    return shift(values, ("core",), lambda i: (1 - i[0],))


def spread(values, axes, count):
    return lax.all_to_all(jnp.broadcast_to(values[None], (count,) + values.shape), axes, 0, 0)


def share_kernel(tokens, ln_gain, out):
    lane = lax.broadcasted_iota(jnp.int32, (128, 128), 1)
    columns = jnp.zeros((128, 128), jnp.float32)
    for quarter in range(NZH):
        x = tokens[quarter].astype(jnp.float32)
        columns = jnp.where(lane == quarter, jnp.sum(x, axis=1, keepdims=True), columns)
        columns = jnp.where(lane == quarter + NZH, jnp.sum(x * x, axis=1, keepdims=True), columns)
    sums = columns.T[: 2 * NZH]
    for target in range(NZL * NY):
        out[target, 0:8] = sums
        out[target, 8:11] = ln_gain[...].astype(jnp.float32)


def layout_kernel(where, w_mine, w_theirs, w):
    core, x_here = where[1], where[3]
    half = w_mine.shape[2]
    for step in range(NX):
        x = lax.rem(x_here + step, NX)
        for s in range(3):
            cols = slice(s * 256, s * 256 + 256)
            w[x, pl.ds(pl.multiple_of(core * half, half), half), cols] = w_mine[step, s]
            w[x, pl.ds(pl.multiple_of((1 - core) * half, half), half), cols] = w_theirs[step, s]


def partial_kernel(where, t0, t1, t2, t3, shared, w, out, acc):
    zl, turn, y_here = where[0], where[2], where[4]
    tokens = (t0, t1, t2, t3)

    sums = shared[0, 0:8]
    for group in range(1, NZL * NY):
        sums += shared[group, 0:8]
    center = sums[:NZH] / FEATURES
    scale = lax.rsqrt(sums[NZH:] / FEATURES - center * center + EPSILON)
    stats = jnp.concatenate([center, scale], axis=0).T

    for slot in range(NZL):
        part = lax.rem(zl + slot, NZL)
        rows = shared[part * NY + y_here, 8:11]
        row_gain = jnp.concatenate([rows[0:1], rows[1:2], rows[2:3]], axis=1)
        normed = []
        for quarter in range(NZH):
            x = tokens[slot][quarter].astype(jnp.float32)
            center = stats[:, quarter : quarter + 1]
            scale = stats[:, NZH + quarter : NZH + quarter + 1]
            normed.append(((x - center) * scale * row_gain).astype(jnp.bfloat16))
        term = jnp.dot(
            jnp.concatenate(normed, axis=0),
            w[part],
            preferred_element_type=jnp.float32,
        )
        if slot == 0:
            acc[...] = term
        else:
            acc[...] += term
    for core_to in range(CORES):
        for y_to in range(NY):
            quarter = lax.rem(turn + y_to + 2 * core_to, NZH)
            rows = pl.ds(pl.multiple_of(quarter * 128, 128), 128)
            head = y_to // 2
            for s in range(3):
                cols = slice(s * 256 + head * DH, s * 256 + head * DH + DH)
                out[core_to, y_to, :, s * DH : s * DH + DH] = acc[rows, cols].astype(jnp.bfloat16)


def heads_kernel(where, part, head_gain, q_out, kv_out):
    high = where[5] > 0
    q_row = jnp.where(high, head_gain[1:2], head_gain[0:1])
    k_row = jnp.where(high, head_gain[3:4], head_gain[2:3])

    def head_norm(values, row):
        mid = jnp.mean(values, axis=1, keepdims=True)
        var = jnp.mean(values * values, axis=1, keepdims=True) - mid * mid
        return ((values - mid) * lax.rsqrt(var + EPSILON) * row).astype(jnp.bfloat16)

    for source in range(2):
        rows = slice(source * 128, source * 128 + 128)
        acc = sum(part[source, y].astype(jnp.float32) for y in range(NY))
        q_out[rows] = head_norm(acc[:, :DH], q_row)
        key = head_norm(acc[:, DH : 2 * DH], k_row)
        value = acc[:, 2 * DH :].astype(jnp.bfloat16)
        for target in range(NX * 2):
            kv_out[target, 0, rows] = key
            kv_out[target, 1, rows] = value


def head_scores(q, kv):
    keys = kv[:, 0].reshape(-1, DH)
    return lax.dot_general(
        q[...], keys, (((1,), (1,)), ((), ())), preferred_element_type=jnp.float32
    ) * (DH ** -0.5)


def attend_first_kernel(q, kv, mixed, extremes):
    scores = head_scores(q, kv)
    top = jnp.max(scores, axis=1, keepdims=True)
    weights = jnp.exp(scores - top)
    total = jnp.sum(weights, axis=1, keepdims=True)
    lane = lax.broadcasted_iota(jnp.int32, extremes.shape, 1)
    extremes[...] = jnp.where(lane == 0, top, total)
    mixed[...] = jnp.dot(
        weights.astype(jnp.bfloat16), kv[:, 1].reshape(-1, DH), preferred_element_type=jnp.float32
    )


def attend_second_kernel(where, q, kv, mixed, extremes, out):
    scores = head_scores(q, kv)
    top_before = extremes[:, 0:1]
    top = jnp.maximum(top_before, jnp.max(scores, axis=1, keepdims=True))
    scale = jnp.exp(top_before - top)
    weights = jnp.exp(scores - top)
    total = extremes[:, 1:2] * scale + jnp.sum(weights, axis=1, keepdims=True)
    both = mixed[...] * scale + jnp.dot(
        weights.astype(jnp.bfloat16), kv[:, 1].reshape(-1, DH), preferred_element_type=jnp.float32
    )
    rows = (both / total).astype(jnp.bfloat16)
    for half in range(2):
        place = lax.rem(where[1] + half, 2)
        out[pl.ds(pl.multiple_of(place * 128, 128), 128)] = rows[half * 128 : half * 128 + 128]


def kernel_call(kernel, out_shape, args, scalars=0, scratch=()):
    vmem = pl.BlockSpec(memory_space=pltpu.VMEM)
    smem = pl.BlockSpec(memory_space=pltpu.SMEM)
    return pl.pallas_call(
        kernel,
        out_shape=out_shape,
        in_specs=[smem] * scalars + [vmem] * (len(args) - scalars),
        out_specs=jax.tree.map(lambda _: vmem, out_shape),
        scratch_shapes=scratch,
        compiler_params=pltpu.CompilerParams(vmem_limit_bytes=VMEM_LIMIT),
    )(*args)


def body(tokens, ln_gain, w_qkv, q_gain, k_gain):
    core = lax.axis_index("core")
    zl = lax.axis_index("zl")
    zh = lax.axis_index("zh")
    y_high = lax.axis_index("yh")
    y_here = y_high * 2 + lax.axis_index("yl")
    turn = (zh + zl + (zl >= 2)) % NZH
    where = jnp.stack(
        [zl, core, turn, lax.axis_index("x"), y_here, y_high]
    ).astype(jnp.int32)

    with jax.named_scope("weights"):
        w_moved = to_plane(jnp.transpose(w_qkv, (1, 0, 2)))
        head_gain = to_plane(jnp.concatenate([q_gain, k_gain]).reshape(4, DH))

    with jax.named_scope("tokens"):
        tokens, w_moved, head_gain = lax.optimization_barrier((tokens, w_moved, head_gain))
        t0 = spread(tokens, "zh", NZH)

    with jax.named_scope("weights"):
        along_x = [
            shift(w_moved, ("x",), lambda i, step=step: ((i[0] - step) % NX,)) for step in (1, 2, 3)
        ]
        t0, *along_x = lax.optimization_barrier((t0, *along_x))
        w_mine = jnp.stack([w_moved] + along_x)
        w_theirs = swap_cores(w_mine)

    with jax.named_scope("tokens"):
        t1 = along_z(t0, -1)
        t3 = along_z(t0, 1)
        t2 = along_z_two(t0)

    with jax.named_scope("norm"):
        shared = kernel_call(
            share_kernel,
            jax.ShapeDtypeStruct((NZL * NY, 11, 128), jnp.float32),
            (t0, ln_gain.reshape(3, 128)),
        )
        shared = lax.all_to_all(shared, ("zl",) + Y, 0, 0)

    with jax.named_scope("project"):
        w = kernel_call(
            layout_kernel,
            jax.ShapeDtypeStruct((NX, 384, 768), jnp.bfloat16),
            (where, w_mine, w_theirs),
            scalars=1,
        )
        part = kernel_call(
            partial_kernel,
            jax.ShapeDtypeStruct((CORES, NY, 128, 3 * DH), jnp.bfloat16),
            (where, t0, t1, t2, t3, shared, w),
            scalars=1,
            scratch=[
                pltpu.VMEM((512, 768), jnp.float32),
            ],
        )
        part = part.reshape(CORES * NY, 128, 3 * DH)
        part = lax.all_to_all(part, ("core",) + Y, 0, 0).reshape(CORES, NY, 128, 3 * DH)
        q, kv = kernel_call(
            heads_kernel,
            (
                jax.ShapeDtypeStruct((256, DH), jnp.bfloat16),
                jax.ShapeDtypeStruct((NX * 2, 2, 256, DH), jnp.bfloat16),
            ),
            (where, part, head_gain),
            scalars=1,
        )

    with jax.named_scope("keys"):
        kv_mine = lax.all_to_all(kv, ("x", "yl"), 0, 0)
        kv_theirs = swap_cores(kv_mine)

    with jax.named_scope("attend"):
        partial = kernel_call(
            attend_first_kernel,
            (
                jax.ShapeDtypeStruct((256, DH), jnp.float32),
                jax.ShapeDtypeStruct((256, DH), jnp.float32),
            ),
            (q, kv_mine),
        )
        out = kernel_call(
            attend_second_kernel,
            jax.ShapeDtypeStruct((256, DH), jnp.bfloat16),
            (where, q, kv_theirs, *partial),
            scalars=1,
        )

    with jax.named_scope("home"):
        arrived = to_home(out)
        same = arrived[:128]
        cross = swap_cores(arrived[128:])
        zl_from = (zl + 2) % NZL
        zh_from = y_here + jnp.where(zl == 1, 1, jnp.where(zl == 3, 2, 0))
        y_from = zh + 4 * NY - zh_from - zl_from - (zl_from >= 2) - 2 * core
        first = y_from % NY < 2
        return jnp.where(
            first,
            jnp.concatenate([same, cross], axis=1),
            jnp.concatenate([cross, same], axis=1),
        )


def solution(mesh):
    fine = Mesh(mesh.devices.reshape(SIZES), AXES)
    rows = ("x", "zh", "core")
    cols = ("zl",) + Y
    in_specs = (P(rows, cols), P(cols), P(rows, None, cols), P(cols), P(cols))
    return jax.shard_map(body, mesh=fine, in_specs=in_specs, out_specs=P(rows, cols), check_vma=False)
```

```python
import numpy as np
import jax
import jax.numpy as jnp
from jax import lax
from jax.experimental import pallas as pl
from jax.experimental.pallas import tpu as pltpu
from jax.sharding import Mesh, PartitionSpec as P

DH = 128
EPSILON = 1e-06
FEATURES = 6144
NX = NZH = NZL = NY = 4
CORES = 2
AXES = ("x", "zh", "core", "zl", "yh", "yl")
SIZES = (NX, NZH, CORES, NZL, 2, 2)
Y = ("yh", "yl")
VMEM_LIMIT = 28 * 1024 * 1024


def shift(values, axes, move):
    sizes = [SIZES[AXES.index(axis)] for axis in axes]
    pairs = [
        (int(np.ravel_multi_index(src, sizes)), int(np.ravel_multi_index(move(src), sizes)))
        for src in np.ndindex(*sizes)
    ]
    return lax.ppermute(values, axes, pairs)


def plane_turn(zl):
    return (0, 1, 0, 2)[zl]


def to_plane(values):
    def move(i):
        zh, zl, yh, yl = i
        return ((yh * 2 + yl + plane_turn(zl)) % NZH, (zl + 2) % NZL) + divmod(zh, 2)

    return shift(values, ("zh", "zl") + Y, move)


def to_home(values):
    def move(i):
        zh, core, zl, yh, yl = i
        step = 4 * ((yh * 2 + yl + 2 * core + zl) % 4) + 2
        zh_home, zl_home = divmod((zh * NZL + zl + step) % 16, NZL)
        return (zh_home, core, zl_home) + divmod((zh - plane_turn(zl_home)) % NY, 2)

    return shift(values, ("zh", "core", "zl") + Y, move)


def along_z(values, step):
    return shift(values, ("zh", "zl"), lambda i: divmod((i[0] * NZL + i[1] + step) % 16, NZL))


def along_z_two(values):
    def move(i):
        step = 2 if i[1] % 2 == 0 else -2
        return divmod((i[0] * NZL + i[1] + step) % 16, NZL)

    return shift(values, ("zh", "zl"), move)


def swap_cores(values):
    return shift(values, ("core",), lambda i: (1 - i[0],))


def spread(values, axes, count):
    return lax.all_to_all(jnp.broadcast_to(values[None], (count,) + values.shape), axes, 0, 0)


def copies_kernel(tokens, out):
    for target in range(NZH):
        out[target] = tokens[...]


def share_kernel(tokens, ln_gain, out):
    lane = lax.broadcasted_iota(jnp.int32, (128, 128), 1)
    columns = jnp.zeros((128, 128), jnp.float32)
    for quarter in range(NZH):
        x = tokens[quarter].astype(jnp.float32)
        columns = jnp.where(lane == quarter, jnp.sum(x, axis=1, keepdims=True), columns)
        columns = jnp.where(lane == quarter + NZH, jnp.sum(x * x, axis=1, keepdims=True), columns)
    sums = columns.T[: 2 * NZH]
    for target in range(NZL * NY):
        out[target, 0:8] = sums
        out[target, 8:11] = ln_gain[...].astype(jnp.float32)


def layout_kernel(where, w_mine, w_theirs, w):
    core, x_here = where[1], where[3]
    half = w_mine.shape[2]
    for step in range(NX):
        x = lax.rem(x_here + step, NX)
        for s in range(3):
            cols = slice(s * 256, s * 256 + 256)
            w[x, pl.ds(pl.multiple_of(core * half, half), half), cols] = w_mine[step, s]
            w[x, pl.ds(pl.multiple_of((1 - core) * half, half), half), cols] = w_theirs[step, s]


def partial_kernel(where, t0, t1, t2, t3, shared, w, out, acc):
    zl, turn, y_here = where[0], where[2], where[4]
    tokens = (t0, t1, t2, t3)

    sums = shared[0, 0:8]
    for group in range(1, NZL * NY):
        sums += shared[group, 0:8]
    center = sums[:NZH] / FEATURES
    scale = lax.rsqrt(sums[NZH:] / FEATURES - center * center + EPSILON)
    stats = jnp.concatenate([center, scale], axis=0).T

    for slot in range(NZL):
        part = lax.rem(zl + slot, NZL)
        rows = shared[part * NY + y_here, 8:11]
        row_gain = jnp.concatenate([rows[0:1], rows[1:2], rows[2:3]], axis=1)
        normed = []
        for quarter in range(NZH):
            x = tokens[slot][quarter].astype(jnp.float32)
            center = stats[:, quarter : quarter + 1]
            scale = stats[:, NZH + quarter : NZH + quarter + 1]
            normed.append(((x - center) * scale * row_gain).astype(jnp.bfloat16))
        term = jnp.dot(
            jnp.concatenate(normed, axis=0),
            w[part],
            preferred_element_type=jnp.float32,
        )
        if slot == 0:
            acc[...] = term
        else:
            acc[...] += term
    for core_to in range(CORES):
        for y_to in range(NY):
            quarter = lax.rem(turn + y_to + 2 * core_to, NZH)
            rows = pl.ds(pl.multiple_of(quarter * 128, 128), 128)
            head = y_to // 2
            for s in range(3):
                cols = slice(s * 256 + head * DH, s * 256 + head * DH + DH)
                out[core_to, y_to, :, s * DH : s * DH + DH] = acc[rows, cols].astype(jnp.bfloat16)


def heads_kernel(where, part, head_gain, q_out, kv_out):
    high = where[5] > 0
    q_row = jnp.where(high, head_gain[1:2], head_gain[0:1])
    k_row = jnp.where(high, head_gain[3:4], head_gain[2:3])

    def head_norm(values, row):
        mid = jnp.mean(values, axis=1, keepdims=True)
        var = jnp.mean(values * values, axis=1, keepdims=True) - mid * mid
        return ((values - mid) * lax.rsqrt(var + EPSILON) * row).astype(jnp.bfloat16)

    for source in range(2):
        rows = slice(source * 128, source * 128 + 128)
        acc = sum(part[source, y].astype(jnp.float32) for y in range(NY))
        q_out[rows] = head_norm(acc[:, :DH], q_row)
        key = head_norm(acc[:, DH : 2 * DH], k_row)
        value = acc[:, 2 * DH :].astype(jnp.bfloat16)
        for target in range(NX * 2):
            kv_out[target, 0, rows] = key
            kv_out[target, 1, rows] = value


def head_scores(q, kv):
    keys = kv[:, 0].reshape(-1, DH)
    return lax.dot_general(
        q[...], keys, (((1,), (1,)), ((), ())), preferred_element_type=jnp.float32
    ) * (DH ** -0.5)


def attend_first_kernel(q, kv, mixed, extremes):
    scores = head_scores(q, kv)
    top = jnp.max(scores, axis=1, keepdims=True)
    weights = jnp.exp(scores - top)
    total = jnp.sum(weights, axis=1, keepdims=True)
    lane = lax.broadcasted_iota(jnp.int32, extremes.shape, 1)
    extremes[...] = jnp.where(lane == 0, top, total)
    mixed[...] = jnp.dot(
        weights.astype(jnp.bfloat16), kv[:, 1].reshape(-1, DH), preferred_element_type=jnp.float32
    )


def attend_second_kernel(where, q, kv, mixed, extremes, out):
    scores = head_scores(q, kv)
    top_before = extremes[:, 0:1]
    top = jnp.maximum(top_before, jnp.max(scores, axis=1, keepdims=True))
    scale = jnp.exp(top_before - top)
    weights = jnp.exp(scores - top)
    total = extremes[:, 1:2] * scale + jnp.sum(weights, axis=1, keepdims=True)
    both = mixed[...] * scale + jnp.dot(
        weights.astype(jnp.bfloat16), kv[:, 1].reshape(-1, DH), preferred_element_type=jnp.float32
    )
    rows = (both / total).astype(jnp.bfloat16)
    for half in range(2):
        place = lax.rem(where[1] + half, 2)
        out[pl.ds(pl.multiple_of(place * 128, 128), 128)] = rows[half * 128 : half * 128 + 128]


def kernel_call(kernel, out_shape, args, scalars=0, scratch=()):
    vmem = pl.BlockSpec(memory_space=pltpu.VMEM)
    smem = pl.BlockSpec(memory_space=pltpu.SMEM)
    return pl.pallas_call(
        kernel,
        out_shape=out_shape,
        in_specs=[smem] * scalars + [vmem] * (len(args) - scalars),
        out_specs=jax.tree.map(lambda _: vmem, out_shape),
        scratch_shapes=scratch,
        compiler_params=pltpu.CompilerParams(vmem_limit_bytes=VMEM_LIMIT),
    )(*args)


def body(tokens, ln_gain, w_qkv, q_gain, k_gain):
    core = lax.axis_index("core")
    zl = lax.axis_index("zl")
    zh = lax.axis_index("zh")
    y_high = lax.axis_index("yh")
    y_here = y_high * 2 + lax.axis_index("yl")
    turn = (zh + zl + (zl >= 2)) % NZH
    where = jnp.stack(
        [zl, core, turn, lax.axis_index("x"), y_here, y_high]
    ).astype(jnp.int32)

    with jax.named_scope("weights"):
        w_moved = to_plane(jnp.transpose(w_qkv, (1, 0, 2)))
        head_gain = to_plane(jnp.concatenate([q_gain, k_gain]).reshape(4, DH))

    with jax.named_scope("tokens"):
        copies = kernel_call(
            copies_kernel,
            jax.ShapeDtypeStruct((NZH,) + tokens.shape, jnp.bfloat16),
            (tokens,),
        )
        copies, w_moved, head_gain = lax.optimization_barrier((copies, w_moved, head_gain))
        t0 = lax.all_to_all(copies, "zh", 0, 0)

    with jax.named_scope("weights"):
        along_x = [
            shift(w_moved, ("x",), lambda i, step=step: ((i[0] - step) % NX,)) for step in (1, 2, 3)
        ]
        t0, *along_x = lax.optimization_barrier((t0, *along_x))
        w_mine = jnp.stack([w_moved] + along_x)
        w_theirs = swap_cores(w_mine)

    with jax.named_scope("tokens"):
        t1 = along_z(t0, -1)
        t3 = along_z(t0, 1)
        t2 = along_z_two(t0)

    with jax.named_scope("norm"):
        shared = kernel_call(
            share_kernel,
            jax.ShapeDtypeStruct((NZL * NY, 11, 128), jnp.float32),
            (t0, ln_gain.reshape(3, 128)),
        )
        shared = lax.all_to_all(shared, ("zl",) + Y, 0, 0)

    with jax.named_scope("project"):
        w = kernel_call(
            layout_kernel,
            jax.ShapeDtypeStruct((NX, 384, 768), jnp.bfloat16),
            (where, w_mine, w_theirs),
            scalars=1,
        )
        part = kernel_call(
            partial_kernel,
            jax.ShapeDtypeStruct((CORES, NY, 128, 3 * DH), jnp.bfloat16),
            (where, t0, t1, t2, t3, shared, w),
            scalars=1,
            scratch=[
                pltpu.VMEM((512, 768), jnp.float32),
            ],
        )
        part = part.reshape(CORES * NY, 128, 3 * DH)
        part = lax.all_to_all(part, ("core",) + Y, 0, 0).reshape(CORES, NY, 128, 3 * DH)
        q, kv = kernel_call(
            heads_kernel,
            (
                jax.ShapeDtypeStruct((256, DH), jnp.bfloat16),
                jax.ShapeDtypeStruct((NX * 2, 2, 256, DH), jnp.bfloat16),
            ),
            (where, part, head_gain),
            scalars=1,
        )

    with jax.named_scope("keys"):
        kv_mine = lax.all_to_all(kv, ("x", "yl"), 0, 0)
        kv_theirs = swap_cores(kv_mine)

    with jax.named_scope("attend"):
        partial = kernel_call(
            attend_first_kernel,
            (
                jax.ShapeDtypeStruct((256, DH), jnp.float32),
                jax.ShapeDtypeStruct((256, DH), jnp.float32),
            ),
            (q, kv_mine),
        )
        out = kernel_call(
            attend_second_kernel,
            jax.ShapeDtypeStruct((256, DH), jnp.bfloat16),
            (where, q, kv_theirs, *partial),
            scalars=1,
        )

    with jax.named_scope("home"):
        arrived = to_home(out)
        same = arrived[:128]
        cross = swap_cores(arrived[128:])
        zl_from = (zl + 2) % NZL
        zh_from = y_here + jnp.where(zl == 1, 1, jnp.where(zl == 3, 2, 0))
        y_from = zh + 4 * NY - zh_from - zl_from - (zl_from >= 2) - 2 * core
        first = y_from % NY < 2
        return jnp.where(
            first,
            jnp.concatenate([same, cross], axis=1),
            jnp.concatenate([cross, same], axis=1),
        )


def solution(mesh):
    fine = Mesh(mesh.devices.reshape(SIZES), AXES)
    rows = ("x", "zh", "core")
    cols = ("zl",) + Y
    in_specs = (P(rows, cols), P(cols), P(rows, None, cols), P(cols), P(cols))
    return jax.shard_map(body, mesh=fine, in_specs=in_specs, out_specs=P(rows, cols), check_vma=False)
```

```python
import numpy as np
import jax
import jax.numpy as jnp
from jax import lax
from jax.experimental import pallas as pl
from jax.experimental.pallas import tpu as pltpu
from jax.sharding import Mesh, PartitionSpec as P

DH = 128
EPSILON = 1e-06
FEATURES = 6144
NX = NZH = NZL = NY = 4
CORES = 2
AXES = ("x", "zh", "core", "zl", "yh", "yl")
SIZES = (NX, NZH, CORES, NZL, 2, 2)
Y = ("yh", "yl")
VMEM_LIMIT = 28 * 1024 * 1024


def shift(values, axes, move):
    sizes = [SIZES[AXES.index(axis)] for axis in axes]
    pairs = [
        (int(np.ravel_multi_index(src, sizes)), int(np.ravel_multi_index(move(src), sizes)))
        for src in np.ndindex(*sizes)
    ]
    return lax.ppermute(values, axes, pairs)


def plane_turn(zl):
    return (0, 1, 0, 2)[zl]


def to_plane(values):
    def move(i):
        zh, zl, yh, yl = i
        return ((yh * 2 + yl + plane_turn(zl)) % NZH, (zl + 2) % NZL) + divmod(zh, 2)

    return shift(values, ("zh", "zl") + Y, move)


def to_home(values):
    def move(i):
        zh, core, zl, yh, yl = i
        step = 4 * ((yh * 2 + yl + 2 * core + zl) % 4) + 2
        zh_home, zl_home = divmod((zh * NZL + zl + step) % 16, NZL)
        return (zh_home, core, zl_home) + divmod((zh - plane_turn(zl_home)) % NY, 2)

    return shift(values, ("zh", "core", "zl") + Y, move)


def along_z(values, step):
    return shift(values, ("zh", "zl"), lambda i: divmod((i[0] * NZL + i[1] + step) % 16, NZL))


def along_z_two(values):
    def move(i):
        step = 2 if i[1] % 2 == 0 else -2
        return divmod((i[0] * NZL + i[1] + step) % 16, NZL)

    return shift(values, ("zh", "zl"), move)


def swap_cores(values):
    return shift(values, ("core",), lambda i: (1 - i[0],))


def spread(values, axes, count):
    return lax.all_to_all(jnp.broadcast_to(values[None], (count,) + values.shape), axes, 0, 0)


def copies_kernel(tokens, out):
    for target in range(NZH):
        out[target] = tokens[...]


def share_kernel(tokens, ln_gain, out):
    lane = lax.broadcasted_iota(jnp.int32, (128, 128), 1)
    columns = jnp.zeros((128, 128), jnp.float32)
    for quarter in range(NZH):
        x = tokens[quarter].astype(jnp.float32)
        columns = jnp.where(lane == quarter, jnp.sum(x, axis=1, keepdims=True), columns)
        columns = jnp.where(lane == quarter + NZH, jnp.sum(x * x, axis=1, keepdims=True), columns)
    sums = columns.T[: 2 * NZH]
    for target in range(NZL * NY):
        out[target, 0:8] = sums
        out[target, 8:11] = ln_gain[...].astype(jnp.float32)


def layout_kernel(where, w_mine, w_theirs, w):
    core, x_here = where[1], where[3]
    half = w_mine.shape[2]
    for step in range(NX):
        x = lax.rem(x_here + step, NX)
        for s in range(3):
            cols = slice(s * 256, s * 256 + 256)
            w[x, pl.ds(pl.multiple_of(core * half, half), half), cols] = w_mine[step, s]
            w[x, pl.ds(pl.multiple_of((1 - core) * half, half), half), cols] = w_theirs[step, s]


def partial_kernel(where, t0, t1, t2, t3, shared, w, out, acc):
    zl, turn, y_here = where[0], where[2], where[4]
    tokens = (t0, t1, t2, t3)

    sums = shared[0, 0:8]
    for group in range(1, NZL * NY):
        sums += shared[group, 0:8]
    center = sums[:NZH] / FEATURES
    scale = lax.rsqrt(sums[NZH:] / FEATURES - center * center + EPSILON)
    stats = jnp.concatenate([center, scale], axis=0).T

    for slot in range(NZL):
        part = lax.rem(zl + slot, NZL)
        rows = shared[part * NY + y_here, 8:11]
        row_gain = jnp.concatenate([rows[0:1], rows[1:2], rows[2:3]], axis=1)
        normed = []
        for quarter in range(NZH):
            x = tokens[slot][quarter].astype(jnp.float32)
            center = stats[:, quarter : quarter + 1]
            scale = stats[:, NZH + quarter : NZH + quarter + 1]
            normed.append(((x - center) * scale * row_gain).astype(jnp.bfloat16))
        term = jnp.dot(
            jnp.concatenate(normed, axis=0),
            w[part],
            preferred_element_type=jnp.float32,
        )
        if slot == 0:
            acc[...] = term
        else:
            acc[...] += term
    for core_to in range(CORES):
        for y_to in range(NY):
            quarter = lax.rem(turn + y_to + 2 * core_to, NZH)
            rows = pl.ds(pl.multiple_of(quarter * 128, 128), 128)
            head = y_to // 2
            for s in range(3):
                cols = slice(s * 256 + head * DH, s * 256 + head * DH + DH)
                out[core_to, y_to, :, s * DH : s * DH + DH] = acc[rows, cols]


def heads_kernel(where, part, head_gain, q_out, kv_out):
    high = where[5] > 0
    q_row = jnp.where(high, head_gain[1:2], head_gain[0:1])
    k_row = jnp.where(high, head_gain[3:4], head_gain[2:3])

    def head_norm(values, row):
        mid = jnp.mean(values, axis=1, keepdims=True)
        var = jnp.mean(values * values, axis=1, keepdims=True) - mid * mid
        return ((values - mid) * lax.rsqrt(var + EPSILON) * row).astype(jnp.bfloat16)

    for source in range(2):
        rows = slice(source * 128, source * 128 + 128)
        acc = sum(part[source, y].astype(jnp.float32) for y in range(NY))
        q_out[rows] = head_norm(acc[:, :DH], q_row)
        key = head_norm(acc[:, DH : 2 * DH], k_row)
        value = acc[:, 2 * DH :].astype(jnp.bfloat16)
        for target in range(NX * 2):
            kv_out[target, 0, rows] = key
            kv_out[target, 1, rows] = value


def head_scores(q, kv):
    keys = kv[:, 0].reshape(-1, DH)
    return lax.dot_general(
        q[...], keys, (((1,), (1,)), ((), ())), preferred_element_type=jnp.float32
    ) * (DH ** -0.5)


def attend_first_kernel(q, kv, mixed, extremes):
    scores = head_scores(q, kv)
    top = jnp.max(scores, axis=1, keepdims=True)
    weights = jnp.exp(scores - top)
    total = jnp.sum(weights, axis=1, keepdims=True)
    lane = lax.broadcasted_iota(jnp.int32, extremes.shape, 1)
    extremes[...] = jnp.where(lane == 0, top, total)
    mixed[...] = jnp.dot(
        weights.astype(jnp.bfloat16), kv[:, 1].reshape(-1, DH), preferred_element_type=jnp.float32
    )


def attend_second_kernel(where, q, kv, mixed, extremes, out):
    scores = head_scores(q, kv)
    top_before = extremes[:, 0:1]
    top = jnp.maximum(top_before, jnp.max(scores, axis=1, keepdims=True))
    scale = jnp.exp(top_before - top)
    weights = jnp.exp(scores - top)
    total = extremes[:, 1:2] * scale + jnp.sum(weights, axis=1, keepdims=True)
    both = mixed[...] * scale + jnp.dot(
        weights.astype(jnp.bfloat16), kv[:, 1].reshape(-1, DH), preferred_element_type=jnp.float32
    )
    rows = (both / total).astype(jnp.bfloat16)
    for half in range(2):
        place = lax.rem(where[1] + half, 2)
        out[pl.ds(pl.multiple_of(place * 128, 128), 128)] = rows[half * 128 : half * 128 + 128]


def kernel_call(kernel, out_shape, args, scalars=0, scratch=()):
    vmem = pl.BlockSpec(memory_space=pltpu.VMEM)
    smem = pl.BlockSpec(memory_space=pltpu.SMEM)
    return pl.pallas_call(
        kernel,
        out_shape=out_shape,
        in_specs=[smem] * scalars + [vmem] * (len(args) - scalars),
        out_specs=jax.tree.map(lambda _: vmem, out_shape),
        scratch_shapes=scratch,
        compiler_params=pltpu.CompilerParams(vmem_limit_bytes=VMEM_LIMIT),
    )(*args)


def body(tokens, ln_gain, w_qkv, q_gain, k_gain):
    core = lax.axis_index("core")
    zl = lax.axis_index("zl")
    zh = lax.axis_index("zh")
    y_high = lax.axis_index("yh")
    y_here = y_high * 2 + lax.axis_index("yl")
    turn = (zh + zl + (zl >= 2)) % NZH
    where = jnp.stack(
        [zl, core, turn, lax.axis_index("x"), y_here, y_high]
    ).astype(jnp.int32)

    with jax.named_scope("weights"):
        w_moved = to_plane(jnp.transpose(w_qkv, (1, 0, 2)))
        head_gain = to_plane(jnp.concatenate([q_gain, k_gain]).reshape(4, DH))

    with jax.named_scope("tokens"):
        copies = kernel_call(
            copies_kernel,
            jax.ShapeDtypeStruct((NZH,) + tokens.shape, jnp.bfloat16),
            (tokens,),
        )
        copies, w_moved, head_gain = lax.optimization_barrier((copies, w_moved, head_gain))
        t0 = lax.all_to_all(copies, "zh", 0, 0)

    with jax.named_scope("weights"):
        along_x = [
            shift(w_moved, ("x",), lambda i, step=step: ((i[0] - step) % NX,)) for step in (1, 2, 3)
        ]
        t0, *along_x = lax.optimization_barrier((t0, *along_x))
        w_mine = jnp.stack([w_moved] + along_x)
        w_theirs = swap_cores(w_mine)

    with jax.named_scope("tokens"):
        t1 = along_z(t0, -1)
        t3 = along_z(t0, 1)
        t2 = along_z_two(t0)

    with jax.named_scope("norm"):
        shared = kernel_call(
            share_kernel,
            jax.ShapeDtypeStruct((NZL * NY, 11, 128), jnp.float32),
            (t0, ln_gain.reshape(3, 128)),
        )
        shared = lax.all_to_all(shared, ("zl",) + Y, 0, 0)

    with jax.named_scope("project"):
        w = kernel_call(
            layout_kernel,
            jax.ShapeDtypeStruct((NX, 384, 768), jnp.bfloat16),
            (where, w_mine, w_theirs),
            scalars=1,
        )
        part = kernel_call(
            partial_kernel,
            jax.ShapeDtypeStruct((CORES, NY, 128, 3 * DH), jnp.float32),
            (where, t0, t1, t2, t3, shared, w),
            scalars=1,
            scratch=[
                pltpu.VMEM((512, 768), jnp.float32),
            ],
        )
        part = part.reshape(CORES * NY, 128, 3 * DH)
        part = lax.all_to_all(part, ("core",) + Y, 0, 0).reshape(CORES, NY, 128, 3 * DH)
        q, kv = kernel_call(
            heads_kernel,
            (
                jax.ShapeDtypeStruct((256, DH), jnp.bfloat16),
                jax.ShapeDtypeStruct((NX * 2, 2, 256, DH), jnp.bfloat16),
            ),
            (where, part, head_gain),
            scalars=1,
        )

    with jax.named_scope("keys"):
        kv_mine = lax.all_to_all(kv, ("x", "yl"), 0, 0)
        kv_theirs = swap_cores(kv_mine)

    with jax.named_scope("attend"):
        partial = kernel_call(
            attend_first_kernel,
            (
                jax.ShapeDtypeStruct((256, DH), jnp.float32),
                jax.ShapeDtypeStruct((256, DH), jnp.float32),
            ),
            (q, kv_mine),
        )
        out = kernel_call(
            attend_second_kernel,
            jax.ShapeDtypeStruct((256, DH), jnp.bfloat16),
            (where, q, kv_theirs, *partial),
            scalars=1,
        )

    with jax.named_scope("home"):
        arrived = to_home(out)
        same = arrived[:128]
        cross = swap_cores(arrived[128:])
        zl_from = (zl + 2) % NZL
        zh_from = y_here + jnp.where(zl == 1, 1, jnp.where(zl == 3, 2, 0))
        y_from = zh + 4 * NY - zh_from - zl_from - (zl_from >= 2) - 2 * core
        first = y_from % NY < 2
        return jnp.where(
            first,
            jnp.concatenate([same, cross], axis=1),
            jnp.concatenate([cross, same], axis=1),
        )


def solution(mesh):
    fine = Mesh(mesh.devices.reshape(SIZES), AXES)
    rows = ("x", "zh", "core")
    cols = ("zl",) + Y
    in_specs = (P(rows, cols), P(cols), P(rows, None, cols), P(cols), P(cols))
    return jax.shard_map(body, mesh=fine, in_specs=in_specs, out_specs=P(rows, cols), check_vma=False)
```

```python
import numpy as np
import jax
import jax.numpy as jnp
from jax import lax
from jax.experimental import pallas as pl
from jax.experimental.pallas import tpu as pltpu
from jax.sharding import Mesh, PartitionSpec as P

DH = 128
EPSILON = 1e-06
FEATURES = 6144
SCORE_SCALE = DH ** -0.5 * 1.4426950408889634
NX = NZH = NZL = NY = 4
CORES = 2
AXES = ("x", "zh", "core", "zl", "yh", "yl")
SIZES = (NX, NZH, CORES, NZL, 2, 2)
Y = ("yh", "yl")
VMEM_LIMIT = 28 * 1024 * 1024


def shift(values, axes, move):
    sizes = [SIZES[AXES.index(axis)] for axis in axes]
    pairs = [
        (int(np.ravel_multi_index(src, sizes)), int(np.ravel_multi_index(move(src), sizes)))
        for src in np.ndindex(*sizes)
    ]
    return lax.ppermute(values, axes, pairs)


def plane_turn(zl):
    return (0, 1, 0, 2)[zl]


def to_plane(values):
    def move(i):
        zh, zl, yh, yl = i
        return ((yh * 2 + yl + plane_turn(zl)) % NZH, (zl + 2) % NZL) + divmod(zh, 2)

    return shift(values, ("zh", "zl") + Y, move)


def to_home(values):
    def move(i):
        zh, core, zl, yh, yl = i
        step = 4 * ((yh * 2 + yl + 2 * core + zl) % 4) + 2
        zh_home, zl_home = divmod((zh * NZL + zl + step) % 16, NZL)
        return (zh_home, core, zl_home) + divmod((zh - plane_turn(zl_home)) % NY, 2)

    return shift(values, ("zh", "core", "zl") + Y, move)


def along_z(values, step):
    return shift(values, ("zh", "zl"), lambda i: divmod((i[0] * NZL + i[1] + step) % 16, NZL))


def along_z_two(values):
    def move(i):
        step = 2 if i[1] % 2 == 0 else -2
        return divmod((i[0] * NZL + i[1] + step) % 16, NZL)

    return shift(values, ("zh", "zl"), move)


def swap_cores(values):
    return shift(values, ("core",), lambda i: (1 - i[0],))


def spread(values, axes, count):
    return lax.all_to_all(jnp.broadcast_to(values[None], (count,) + values.shape), axes, 0, 0)


def copies_kernel(tokens, out):
    for target in range(NZH):
        out[target] = tokens[...]


def share_kernel(tokens, ln_gain, out):
    lane = lax.broadcasted_iota(jnp.int32, (128, 128), 1)
    columns = jnp.zeros((128, 128), jnp.float32)
    for quarter in range(NZH):
        x = tokens[quarter].astype(jnp.float32)
        columns = jnp.where(lane == quarter, jnp.sum(x, axis=1, keepdims=True), columns)
        columns = jnp.where(lane == quarter + NZH, jnp.sum(x * x, axis=1, keepdims=True), columns)
    sums = columns.T[: 2 * NZH]
    for target in range(NZL * NY):
        out[target, 0:8] = sums
        out[target, 8:11] = ln_gain[...].astype(jnp.float32)


def layout_kernel(where, w_mine, w_theirs, w):
    core, x_here = where[1], where[3]
    half = w_mine.shape[2]
    for step in range(NX):
        x = lax.rem(x_here + step, NX)
        for s in range(3):
            cols = slice(s * 256, s * 256 + 256)
            w[x, pl.ds(pl.multiple_of(core * half, half), half), cols] = w_mine[step, s]
            w[x, pl.ds(pl.multiple_of((1 - core) * half, half), half), cols] = w_theirs[step, s]


def partial_kernel(where, t0, t1, t2, t3, shared, w, out, acc):
    zl, turn, y_here = where[0], where[2], where[4]
    tokens = (t0, t1, t2, t3)

    sums = shared[0, 0:8]
    for group in range(1, NZL * NY):
        sums += shared[group, 0:8]
    center = sums[:NZH] / FEATURES
    scale = lax.rsqrt(sums[NZH:] / FEATURES - center * center + EPSILON)
    stats = jnp.concatenate([center, scale], axis=0).T

    for slot in range(NZL):
        part = lax.rem(zl + slot, NZL)
        rows = shared[part * NY + y_here, 8:11]
        row_gain = jnp.concatenate([rows[0:1], rows[1:2], rows[2:3]], axis=1)
        normed = []
        for quarter in range(NZH):
            x = tokens[slot][quarter].astype(jnp.float32)
            center = stats[:, quarter : quarter + 1]
            scale = stats[:, NZH + quarter : NZH + quarter + 1]
            normed.append(((x - center) * scale * row_gain).astype(jnp.bfloat16))
        term = jnp.dot(
            jnp.concatenate(normed, axis=0),
            w[part],
            preferred_element_type=jnp.float32,
        )
        if slot == 0:
            acc[...] = term
        else:
            acc[...] += term
    for core_to in range(CORES):
        for y_to in range(NY):
            quarter = lax.rem(turn + y_to + 2 * core_to, NZH)
            rows = pl.ds(pl.multiple_of(quarter * 128, 128), 128)
            head = y_to // 2
            for s in range(3):
                cols = slice(s * 256 + head * DH, s * 256 + head * DH + DH)
                out[core_to, y_to, :, s * DH : s * DH + DH] = acc[rows, cols].astype(jnp.bfloat16)


def heads_kernel(where, part, head_gain, q_out, kv_out):
    high = where[5] > 0
    q_row = jnp.where(high, head_gain[1:2], head_gain[0:1])
    k_row = jnp.where(high, head_gain[3:4], head_gain[2:3])

    def head_norm(values, row):
        mid = jnp.mean(values, axis=1, keepdims=True)
        var = jnp.mean(values * values, axis=1, keepdims=True) - mid * mid
        return ((values - mid) * lax.rsqrt(var + EPSILON) * row).astype(jnp.bfloat16)

    for source in range(2):
        rows = slice(source * 128, source * 128 + 128)
        acc = sum(part[source, y].astype(jnp.float32) for y in range(NY))
        q_out[rows] = head_norm(acc[:, :DH], q_row)
        key = head_norm(acc[:, DH : 2 * DH], k_row)
        value = acc[:, 2 * DH :].astype(jnp.bfloat16)
        for target in range(NX * 2):
            kv_out[target, 0, rows] = key
            kv_out[target, 1, rows] = value


def head_scores(q, kv):
    keys = kv[:, 0].reshape(-1, DH)
    return lax.dot_general(
        q[...], keys, (((1,), (1,)), ((), ())), preferred_element_type=jnp.float32
    )


def attend_first_kernel(q, kv, mixed, extremes):
    scores = head_scores(q, kv)
    top = jnp.max(scores, axis=1, keepdims=True)
    weights = jnp.exp2((scores - top) * SCORE_SCALE)
    total = jnp.sum(weights, axis=1, keepdims=True)
    lane = lax.broadcasted_iota(jnp.int32, extremes.shape, 1)
    extremes[...] = jnp.where(lane == 0, top, total)
    mixed[...] = jnp.dot(
        weights.astype(jnp.bfloat16), kv[:, 1].reshape(-1, DH), preferred_element_type=jnp.float32
    )


def attend_second_kernel(where, q, kv, mixed, extremes, out):
    scores = head_scores(q, kv)
    top_before = extremes[:, 0:1]
    top = jnp.maximum(top_before, jnp.max(scores, axis=1, keepdims=True))
    scale = jnp.exp2((top_before - top) * SCORE_SCALE)
    weights = jnp.exp2((scores - top) * SCORE_SCALE)
    total = extremes[:, 1:2] * scale + jnp.sum(weights, axis=1, keepdims=True)
    both = mixed[...] * scale + jnp.dot(
        weights.astype(jnp.bfloat16), kv[:, 1].reshape(-1, DH), preferred_element_type=jnp.float32
    )
    rows = (both / total).astype(jnp.bfloat16)
    for half in range(2):
        place = lax.rem(where[1] + half, 2)
        out[pl.ds(pl.multiple_of(place * 128, 128), 128)] = rows[half * 128 : half * 128 + 128]


def kernel_call(kernel, out_shape, args, scalars=0, scratch=()):
    vmem = pl.BlockSpec(memory_space=pltpu.VMEM)
    smem = pl.BlockSpec(memory_space=pltpu.SMEM)
    return pl.pallas_call(
        kernel,
        out_shape=out_shape,
        in_specs=[smem] * scalars + [vmem] * (len(args) - scalars),
        out_specs=jax.tree.map(lambda _: vmem, out_shape),
        scratch_shapes=scratch,
        compiler_params=pltpu.CompilerParams(vmem_limit_bytes=VMEM_LIMIT),
    )(*args)


def body(tokens, ln_gain, w_qkv, q_gain, k_gain):
    core = lax.axis_index("core")
    zl = lax.axis_index("zl")
    zh = lax.axis_index("zh")
    y_high = lax.axis_index("yh")
    y_here = y_high * 2 + lax.axis_index("yl")
    turn = (zh + zl + (zl >= 2)) % NZH
    where = jnp.stack(
        [zl, core, turn, lax.axis_index("x"), y_here, y_high]
    ).astype(jnp.int32)

    with jax.named_scope("weights"):
        w_moved = to_plane(jnp.transpose(w_qkv, (1, 0, 2)))
        head_gain = to_plane(jnp.concatenate([q_gain, k_gain]).reshape(4, DH))

    with jax.named_scope("tokens"):
        copies = kernel_call(
            copies_kernel,
            jax.ShapeDtypeStruct((NZH,) + tokens.shape, jnp.bfloat16),
            (tokens,),
        )
        copies, w_moved, head_gain = lax.optimization_barrier((copies, w_moved, head_gain))
        t0 = lax.all_to_all(copies, "zh", 0, 0)

    with jax.named_scope("weights"):
        along_x = [
            shift(w_moved, ("x",), lambda i, step=step: ((i[0] - step) % NX,)) for step in (1, 2, 3)
        ]
        t0, *along_x = lax.optimization_barrier((t0, *along_x))
        w_mine = jnp.stack([w_moved] + along_x)
        w_theirs = swap_cores(w_mine)

    with jax.named_scope("tokens"):
        t1 = along_z(t0, -1)
        t3 = along_z(t0, 1)
        t2 = along_z_two(t0)

    with jax.named_scope("norm"):
        shared = kernel_call(
            share_kernel,
            jax.ShapeDtypeStruct((NZL * NY, 11, 128), jnp.float32),
            (t0, ln_gain.reshape(3, 128)),
        )
        shared = lax.all_to_all(shared, ("zl",) + Y, 0, 0)

    with jax.named_scope("project"):
        w = kernel_call(
            layout_kernel,
            jax.ShapeDtypeStruct((NX, 384, 768), jnp.bfloat16),
            (where, w_mine, w_theirs),
            scalars=1,
        )
        part = kernel_call(
            partial_kernel,
            jax.ShapeDtypeStruct((CORES, NY, 128, 3 * DH), jnp.bfloat16),
            (where, t0, t1, t2, t3, shared, w),
            scalars=1,
            scratch=[
                pltpu.VMEM((512, 768), jnp.float32),
            ],
        )
        part = part.reshape(CORES * NY, 128, 3 * DH)
        part = lax.all_to_all(part, ("core",) + Y, 0, 0).reshape(CORES, NY, 128, 3 * DH)
        q, kv = kernel_call(
            heads_kernel,
            (
                jax.ShapeDtypeStruct((256, DH), jnp.bfloat16),
                jax.ShapeDtypeStruct((NX * 2, 2, 256, DH), jnp.bfloat16),
            ),
            (where, part, head_gain),
            scalars=1,
        )

    with jax.named_scope("keys"):
        kv_mine = lax.all_to_all(kv, ("x", "yl"), 0, 0)
        kv_theirs = swap_cores(kv_mine)

    with jax.named_scope("attend"):
        partial = kernel_call(
            attend_first_kernel,
            (
                jax.ShapeDtypeStruct((256, DH), jnp.float32),
                jax.ShapeDtypeStruct((256, DH), jnp.float32),
            ),
            (q, kv_mine),
        )
        out = kernel_call(
            attend_second_kernel,
            jax.ShapeDtypeStruct((256, DH), jnp.bfloat16),
            (where, q, kv_theirs, *partial),
            scalars=1,
        )

    with jax.named_scope("home"):
        arrived = to_home(out)
        same = arrived[:128]
        cross = swap_cores(arrived[128:])
        zl_from = (zl + 2) % NZL
        zh_from = y_here + jnp.where(zl == 1, 1, jnp.where(zl == 3, 2, 0))
        y_from = zh + 4 * NY - zh_from - zl_from - (zl_from >= 2) - 2 * core
        first = y_from % NY < 2
        return jnp.where(
            first,
            jnp.concatenate([same, cross], axis=1),
            jnp.concatenate([cross, same], axis=1),
        )


def solution(mesh):
    fine = Mesh(mesh.devices.reshape(SIZES), AXES)
    rows = ("x", "zh", "core")
    cols = ("zl",) + Y
    in_specs = (P(rows, cols), P(cols), P(rows, None, cols), P(cols), P(cols))
    return jax.shard_map(body, mesh=fine, in_specs=in_specs, out_specs=P(rows, cols), check_vma=False)
```
